128 devices in a mesh: dp: 8 (over x, core), seq: 16 (over z, y).
Axes of the slice: x: 4, y: 4, z: 4, core: 2. Of those that a mesh axis runs over, the one named last changes fastest.
Arguments:
- trunk: bfloat16 [8, 4096, 1536], P('dp', 'seq'), may hold values from -34 to 34
- skip: bfloat16 [8, 8192, 1536], P('dp', 'seq'), may hold values from -6 to 6
- valid_bins: int32 [8], P('dp'), may hold values from 2048 to 4096, as said below
- query_weight: bfloat16 [1536, 256], replicated, as said below
- key_weight: bfloat16 [1536, 256], replicated, as said below
- value_weight: bfloat16 [1536, 768], replicated, may hold values from -0.15625 to 0.15625
- out_weight: bfloat16 [768, 1536], replicated, may hold values from -0.21875 to 0.21875
- depth_weight: float32 [3, 1536], replicated, may hold values from -3 to 3
- point_weight: bfloat16 [1536, 1536], replicated, may hold values from -0.15625 to 0.15625
- cotangent: bfloat16 [8, 8192, 1536], P('dp', 'seq'), may hold values from -6 to 6
Outputs:
- grad_pointwise: bfloat16 [1536, 1536], replicated
- grad_depthwise: float32 [3, 1536], replicated
- grad_skip: bfloat16 [8, 8192, 1536], P('dp', 'seq')
The draws below stay inside these ranges and needn't reach their ends.
Inputs may be any that keep to these rules, and one draw needn't show every extreme that they name: Bins at or past a window's valid_bins are padding; in every draw some window is whole. `query_weight`: entries are of order C ** -0.5. `key_weight`: entries are of order C ** -0.5.
All inputs are finite; a program needn't handle non-finite values.
Results may differ from the reference program's by a relative error of at most 0.017.
Values may be sent and summed in bfloat16 or wider, within the bound.
No kernel may reach another device: no remote copies, remote signals or barrier semaphores. Data moves between devices by JAX's collectives and lax.ppermute only.
A program may use at most 128 MiB of HBM per device.

```python
import math
from functools import partial
import jax
import jax.numpy as jnp
from jax import lax

C = 1536
H = 4
DH = 64
DV = 192
BINS = 4096
WINDOWS = 8


def draw_trunk(key, part):
    base = jnp.clip(jax.random.normal(jax.random.fold_in(key, 1), (WINDOWS, BINS, C), jnp.float32), -4.0, 4.0)
    return base.astype(jnp.bfloat16)


def shared_query(key):
    return jnp.clip(jax.random.normal(jax.random.fold_in(key, 31), (C, H * DH), jnp.float32), -4.0, 4.0) / math.sqrt(C)


def draw_query_weight(key, part):
    return shared_query(key).astype(jnp.bfloat16)


def draw_key_weight(key, part):
    weights = jnp.clip(jax.random.normal(jax.random.fold_in(key, 33), (C, H * DH), jnp.float32), -4.0, 4.0) / math.sqrt(C)
    return weights.astype(jnp.bfloat16)


def draw_valid_bins(key, part):
    cut = jax.random.randint(jax.random.fold_in(key, 41), (WINDOWS,), 0, BINS // 2 + 1)
    return (BINS - (cut - jnp.min(cut))).astype(jnp.int32)


def block_scale(key, shape, split, smallest, largest):
    def one(position, parts):
        steps = jax.random.uniform(jax.random.fold_in(jax.random.fold_in(key, 6), position), (parts,), jnp.float32, smallest / len(split), largest / len(split))
        return jnp.repeat(jnp.exp(steps), shape[position] // parts).reshape((-1,) + (1,) * (len(shape) - position - 1))

    loudness = one(*split[0])
    for cut in split[1:]:
        loudness = loudness * one(*cut)
    return loudness


def gaussian(own_key, dims, scale, reach, cuts=(), held_as=jnp.bfloat16):
    level = block_scale(own_key, dims, cuts, -0.22, 0.18) if cuts else 1.0
    entries = jax.random.normal(own_key, dims, jnp.float32) * scale * level
    return jnp.minimum(jnp.maximum(entries, -reach), reach).astype(held_as)


def setup_inputs(seed: int = 0) -> dict:
    streams_of = jax.random.split(jax.random.key(seed), 11)
    trunk = draw_trunk(jax.random.fold_in(streams_of[10], 71), 0)
    skip = gaussian(streams_of[1], (WINDOWS, 2 * BINS, C), 1.0, 6.0, ((0, 8), (1, 16)))
    valid_bins = draw_valid_bins(jax.random.fold_in(streams_of[10], 71), 0)
    query_weight = draw_query_weight(jax.random.fold_in(streams_of[10], 71), 0)
    key_weight = draw_key_weight(jax.random.fold_in(streams_of[10], 71), 0)
    value_weight = gaussian(streams_of[5], (C, H * DV), C ** -0.5, 0.15625)
    out_weight = gaussian(streams_of[6], (H * DV, C), (H * DV) ** -0.5, 0.21875)
    depth_weight = gaussian(streams_of[7], (3, C), 0.6, 3.0, (), jnp.float32)
    point_weight = gaussian(streams_of[8], (C, C), C ** -0.5, 0.15625)
    cotangent = gaussian(streams_of[9], (WINDOWS, 2 * BINS, C), 1.0, 6.0, ((0, 8), (1, 16)))
    return dict(trunk=trunk, skip=skip, valid_bins=valid_bins, query_weight=query_weight, key_weight=key_weight, value_weight=value_weight, out_weight=out_weight, depth_weight=depth_weight, point_weight=point_weight, cotangent=cotangent)


def reference(trunk, skip, valid_bins, query_weight, key_weight, value_weight, out_weight, depth_weight, point_weight, cotangent):
    score_scale = 1.0 / math.sqrt(DH)

    def window_step(carry, inputs):
        sum_point, sum_depth = carry
        tokens, skipped, limit, upstream = inputs
        queries = jnp.dot(tokens, query_weight, preferred_element_type=jnp.float32).astype(jnp.bfloat16)
        keys = jnp.dot(tokens, key_weight, preferred_element_type=jnp.float32).astype(jnp.bfloat16)
        values = jnp.dot(tokens, value_weight, preferred_element_type=jnp.float32).astype(jnp.bfloat16)
        keep = jnp.arange(BINS, dtype=jnp.int32) < limit
        pieces = []
        for head in range(H):
            query_head = queries[:, head * DH:(head + 1) * DH]
            key_head = keys[:, head * DH:(head + 1) * DH]
            value_head = values[:, head * DV:(head + 1) * DV]
            scores = jnp.dot(query_head, key_head.T, preferred_element_type=jnp.float32) * score_scale
            scores = jnp.where(keep[None, :], scores, -1e+30)
            highest = lax.optimization_barrier(jnp.max(scores, axis=1, keepdims=True))
            weights_raw = jnp.exp(scores - highest)
            denom = lax.optimization_barrier(jnp.sum(weights_raw, axis=1, keepdims=True))
            pieces.append(jnp.dot(weights_raw.astype(jnp.bfloat16), value_head, preferred_element_type=jnp.float32) / denom)
        mixed = jnp.concatenate(pieces, axis=1)
        attended = (mixed * lax.rsqrt(lax.optimization_barrier(jnp.mean(mixed * mixed, axis=1, keepdims=True)) + 1e-05)).astype(jnp.bfloat16)
        hidden = (tokens.astype(jnp.float32) + jnp.dot(attended, out_weight, preferred_element_type=jnp.float32)).astype(jnp.bfloat16)
        upsampled = (jnp.repeat(hidden, 2, axis=0).astype(jnp.float32) + skipped.astype(jnp.float32)).astype(jnp.bfloat16)
        padded = jnp.pad(upsampled, ((1, 1), (0, 0)))
        pre_act = depth_weight[0] * padded[:-2] + depth_weight[1] * padded[1:-1] + depth_weight[2] * padded[2:]
        act_value, pullback = jax.vjp(partial(jax.nn.gelu, approximate=True), pre_act)
        activated = act_value.astype(jnp.bfloat16)
        grad_act = lax.dot_general(upstream, point_weight, (((1,), (1,)), ((), ())), preferred_element_type=jnp.float32)
        grad_pre = pullback(grad_act)[0].astype(jnp.bfloat16)
        point_term = lax.dot_general(activated, upstream, (((0,), (0,)), ((), ())), preferred_element_type=jnp.float32)
        row_count = grad_pre.shape[0]
        grad_wide = grad_pre.astype(jnp.float32)
        depth_term = jnp.stack([lax.optimization_barrier(jnp.sum(padded[offset:offset + row_count].astype(jnp.float32) * grad_wide, axis=0)) for offset in range(3)])
        grad_padded = jnp.pad(grad_pre, ((1, 1), (0, 0)))
        grad_skip = (depth_weight[0] * grad_padded[2:] + depth_weight[1] * grad_padded[1:-1] + depth_weight[2] * grad_padded[:-2]).astype(jnp.bfloat16)
        return ((sum_point + point_term, sum_depth + depth_term), grad_skip)
    start = (jnp.zeros((C, C), jnp.float32), jnp.zeros((3, C), jnp.float32))
    (sum_point, sum_depth), grad_skip = lax.scan(window_step, start, (trunk, skip, valid_bins, cotangent))
    norm_scale = 1.0 / math.sqrt(2 * WINDOWS * BINS)
    return ((sum_point * norm_scale).astype(jnp.bfloat16), sum_depth * norm_scale, grad_skip)
```

```python
from functools import partial
import math

import jax
import jax.numpy as jnp
from jax import lax
from jax.experimental import pallas as pl
from jax.experimental.pallas import tpu as pltpu
from jax.sharding import Mesh, PartitionSpec as P

H = 4
DH = 64
DV = 192
AXES = ("x", "c", "z", "y")
SIZES = (4, 2, 4, 4)
EXTRA = 16
BF = jnp.bfloat16
F32 = jnp.float32


def flat(x, c, z, y):
    return ((x * 2 + c) * 4 + z) * 4 + y


def turn(phase, step):
    pairs = []
    for x in range(4):
        for c in range(2):
            for z in range(4):
                for y in range(4):
                    at = {"x": x, "z": z, "y": y}
                    axis = ("x", "y", "z")[(phase + c) % 3]
                    to = dict(at)
                    to[axis] = (at[axis] + step) % 4
                    pairs.append((flat(x, c, z, y), flat(to["x"], c, to["z"], to["y"])))
    return pairs


def ring(step):
    return [(i, (i + step) % 4) for i in range(4)]


def exchange(pieces, phase):
    got = [pieces[0], None, None, None]
    for d in (2, 1, 3):
        got[d] = lax.ppermute(pieces[d], AXES, turn(phase, d))
    return got


def total_of(got):
    a, b, c, d = (g.astype(F32) for g in got)
    return (a + c) + (b + d)


def attend(bases, q, kv, state, last):
    rows = q[0].shape[0]
    width = kv.shape[0]
    part = width // 4
    first = state is None

    def kernel(bases_ref, *refs):
        q_refs, refs = refs[:4], refs[4:]
        kv_ref, refs = refs[0], refs[1:]
        if not first:
            max_in, sum_in, refs = refs[:4], refs[4:8], refs[8:]
        if last:
            out_refs = refs
        else:
            max_out, sum_out = refs[:4], refs[4:8]
        lane = lax.broadcasted_iota(jnp.int32, (width, 256), 1)
        pair = kv_ref[...]
        keys = pair[:, 128:]
        values = jnp.where(lane == DV, jnp.ones((), BF), pair)
        place = lax.broadcasted_iota(jnp.int32, (1, part), 1)
        keep = jnp.concatenate([place + bases_ref[i] < bases_ref[4] for i in range(4)], axis=1)
        for i in range(4):
            scores = lax.dot_general(
                q_refs[i][...], keys, (((1,), (1,)), ((), ())), preferred_element_type=F32
            )
            scores = jnp.where(keep, scores * (1.0 / math.sqrt(DH)), -1e30)
            high = jnp.max(scores, axis=1, keepdims=True)
            if not first:
                before = max_in[i][:, :1]
                high = jnp.maximum(high, before)
            probs = jnp.exp(scores - high).astype(BF)
            update = jnp.dot(probs, values, preferred_element_type=F32)
            if not first:
                update = update + sum_in[i][...] * jnp.exp(before - high)
            if last:
                out_refs[i][...] = (update / update[:, DV : DV + 1]).astype(BF)
            else:
                max_out[i][...] = jnp.broadcast_to(high, (rows, 128))
                sum_out[i][...] = update

    vmem = pl.BlockSpec(memory_space=pltpu.VMEM)
    ins = [*q, kv]
    if not first:
        ins += [*state[0], *state[1]]
    if last:
        outs = [jax.ShapeDtypeStruct((rows, 256), BF)] * 4
    else:
        outs = [jax.ShapeDtypeStruct((rows, 128), F32)] * 4
        outs += [jax.ShapeDtypeStruct((rows, 256), F32)] * 4
    got = pl.pallas_call(
        kernel,
        out_shape=outs,
        in_specs=[pl.BlockSpec(memory_space=pltpu.SMEM)] + [vmem] * len(ins),
        out_specs=[vmem] * len(outs),
        compiler_params=pltpu.CompilerParams(vmem_limit_bytes=40 << 20),
        cost_estimate=pl.CostEstimate(
            flops=4 * 2 * rows * width * 512, bytes_accessed=4 << 20, transcendentals=4 * rows * width
        ),
    )(bases, *ins)
    return got if last else (got[:4], got[4:])


def local(
    trunk,
    skip,
    valid_bins,
    query_weight,
    key_weight,
    value_weight,
    out_weight,
    depth_weight,
    point_weight,
    cotangent,
):
    tokens, skipped, upstream = trunk[0], skip[0], cotangent[0]
    rows = tokens.shape[0]
    fine = skipped.shape[0]
    ix, ic, iz, iy = (lax.axis_index(a) for a in AXES)
    place = iz * 4 + iy

    down = jnp.concatenate([tokens[-1:], skipped[-2:], upstream[-1:]], axis=0)
    up = jnp.concatenate([tokens[:1], skipped[:2], upstream[:1]], axis=0)
    before = lax.ppermute(down, ("z", "y"), [(i, i + 1) for i in range(15)])
    after = lax.ppermute(up, ("z", "y"), [(i + 1, i) for i in range(15)])

    keys = jnp.dot(tokens, key_weight, preferred_element_type=F32).astype(BF)
    values = jnp.dot(tokens, value_weight, preferred_element_type=F32).astype(BF)
    key_heads = keys.reshape(rows, H, DH).transpose(1, 0, 2)
    value_heads = values.reshape(rows, H, DV).transpose(1, 0, 2)
    pairs = jnp.concatenate([value_heads, key_heads], axis=2)
    own = [lax.dynamic_index_in_dim(pairs, (iy + d) % 4, 0, keepdims=False) for d in range(4)]
    kv = [own[0], None, None, None]
    for d in (2, 1, 3):
        kv[d] = lax.ppermute(own[d], "y", ring(d))
    kv_own = jnp.concatenate(kv, axis=0)
    kv_far = {d: lax.ppermute(kv_own, "z", ring(d)) for d in (1, 3, 2)}

    tail = jnp.concatenate([before[:1], after[:1], jnp.zeros((EXTRA - 2, tokens.shape[1]), BF)], axis=0)
    queries = jnp.dot(
        jnp.concatenate([tokens, tail], axis=0), query_weight, preferred_element_type=F32
    ).astype(BF)
    query_heads = queries.reshape(rows + EXTRA, H, DH).transpose(1, 0, 2)
    query_heads = jnp.pad(query_heads, ((0, 0), (0, 0), (64, 0)))
    own = [lax.dynamic_index_in_dim(query_heads, (iy + d) % 4, 0, keepdims=False) for d in range(4)]
    q = [own[0], None, None, None]
    for d in (2, 1, 3):
        q[d] = lax.ppermute(own[d], "y", ring(d))

    def bases(far):
        depth = (iz - far) % 4
        return jnp.stack([(depth * 4 + (iy - d) % 4) * rows for d in range(4)] + [valid_bins[0]]).astype(jnp.int32)

    state = attend(bases(0), q, kv_own, None, False)
    state = attend(bases(1), q, kv_far[1], state, False)
    state = attend(bases(3), q, kv_far[3], state, False)
    mixed = attend(bases(2), q, kv_far[2], state, True)
    back = [mixed[0], None, None, None]
    for d in (2, 1, 3):
        back[d] = lax.ppermute(mixed[d], "y", ring(4 - d))
    squares = sum(jnp.sum(jnp.square(b[:, :DV].astype(F32)), axis=1, keepdims=True) for b in back)
    scale = lax.rsqrt(squares * (1.0 / (H * DV)) + 1e-05)
    out_heads = out_weight.reshape(H, DV, -1)
    attended = jnp.concatenate([(b[:, :DV].astype(F32) * scale).astype(BF) for b in back], axis=1)
    weights = jnp.concatenate(
        [lax.dynamic_index_in_dim(out_heads, (iy + d) % 4, 0, keepdims=False) for d in range(4)], axis=0
    )
    hidden = (
        jnp.concatenate([tokens, tail], axis=0).astype(F32)
        + jnp.dot(attended, weights, preferred_element_type=F32)
    ).astype(BF)

    def raised(hid, skp):
        return (jnp.repeat(hid, 2, axis=0).astype(F32) + skp.astype(F32)).astype(BF)

    zero = jnp.zeros((2, tokens.shape[1]), BF)
    padded = jnp.concatenate(
        [
            jnp.where(place > 0, raised(hidden[rows : rows + 1], before[1:3]), zero),
            raised(hidden[:rows], skipped),
            jnp.where(place < 15, raised(hidden[rows + 1 : rows + 2], after[1:3]), zero),
        ],
        axis=0,
    )
    pre_act = depth_weight[0] * padded[:-2] + depth_weight[1] * padded[1:-1] + depth_weight[2] * padded[2:]
    act_value, pullback = jax.vjp(partial(jax.nn.gelu, approximate=True), pre_act)
    activated = act_value.astype(BF)[1:-1]
    point_term = lax.dot_general(
        activated, upstream, (((0,), (0,)), ((), ())), preferred_element_type=F32
    ).astype(BF)
    wide = jnp.concatenate([before[3:4], upstream, after[3:4]], axis=0)
    grad_act = lax.dot_general(wide, point_weight, (((1,), (1,)), ((), ())), preferred_element_type=F32)
    grad_pre = pullback(grad_act)[0].astype(BF)
    grad_mid = grad_pre[1:-1].astype(F32)
    depth_term = jnp.stack(
        [jnp.sum(padded[1 + t : 1 + t + fine].astype(F32) * grad_mid, axis=0) for t in range(3)]
    )
    grad_skip = (
        depth_weight[0] * grad_pre[2:] + depth_weight[1] * grad_pre[1:-1] + depth_weight[2] * grad_pre[:-2]
    ).astype(BF)

    norm_scale = 1.0 / math.sqrt(128 * fine)
    half = point_term.shape[0] // 2
    swap = [(0, 1), (1, 0)]
    theirs = lax.dynamic_slice_in_dim(point_term, (1 - ic) * half, half, axis=0)
    mine = lax.dynamic_slice_in_dim(point_term, ic * half, half, axis=0)
    pair_sum = (mine.astype(F32) + lax.ppermute(theirs, "c", swap).astype(F32)).astype(BF)
    first_at = jnp.where(ic == 0, ix, iy)
    second_at = jnp.where(ic == 0, iy, iz)
    quarter = half // 4
    got = exchange(
        [lax.dynamic_slice_in_dim(pair_sum, (first_at + d) % 4 * quarter, quarter, axis=0) for d in range(4)], 0
    )
    sum_one = total_of(got).astype(BF)

    half_c = depth_term.shape[1] // 2
    d_theirs = lax.dynamic_slice_in_dim(depth_term, (1 - ic) * half_c, half_c, axis=1)
    d_mine = lax.dynamic_slice_in_dim(depth_term, ic * half_c, half_c, axis=1)
    d_sum = d_mine + lax.ppermute(d_theirs, "c", swap)
    d_sum = total_of(exchange([d_sum] * 4, 0))
    rider = jnp.pad(d_sum.astype(BF), ((0, 5), (0, half_c)))

    slim = quarter // 4
    got = exchange(
        [
            jnp.concatenate(
                [lax.dynamic_slice_in_dim(sum_one, (second_at + d) % 4 * slim, slim, axis=0), rider], axis=0
            )
            for d in range(4)
        ],
        1,
    )
    sum_two = total_of(got).astype(BF)
    sum_three = total_of(exchange([sum_two] * 4, 2)) * norm_scale
    d_half = sum_three[slim : slim + 3, :half_c]
    final = sum_three[:slim].astype(BF)

    def gathered(piece, phase, at):
        got = exchange([piece] * 4, phase)
        whole = jnp.zeros((4, *piece.shape), piece.dtype)
        for d in range(4):
            whole = lax.dynamic_update_index_in_dim(whole, got[d], (at - d) % 4, 0)
        return whole.reshape(4 * piece.shape[0], piece.shape[1])

    final = gathered(final, 1, second_at)
    final = gathered(final, 0, first_at)
    other = lax.ppermute(final, "c", swap)
    low = jnp.where(ic == 0, final, other)
    high = jnp.where(ic == 0, other, final)
    d_other = lax.ppermute(d_half, "c", swap)
    d_all = jnp.concatenate(
        [jnp.where(ic == 0, d_half, d_other), jnp.where(ic == 0, d_other, d_half)], axis=1
    )
    return (jnp.concatenate([low, high], axis=0), d_all, grad_skip[None])


def solution(mesh):
    fine_mesh = Mesh(mesh.devices.reshape(SIZES), AXES)
    rows = P(("x", "c"), ("z", "y"), None)
    return jax.shard_map(
        local,
        mesh=fine_mesh,
        in_specs=(rows, rows, P(("x", "c")), P(), P(), P(), P(), P(), P(), rows),
        out_specs=(P(), P(), rows),
        check_vma=False,
    )
```

```python
import math

import jax
import jax.numpy as jnp
from jax import lax
from jax.experimental import pallas as pl
from jax.experimental.pallas import tpu as pltpu
from jax.sharding import Mesh, PartitionSpec as P

H = 4
DH = 64
DV = 192
AXES = ("x", "c", "z", "y")
SIZES = (4, 2, 4, 4)
BF = jnp.bfloat16
F32 = jnp.float32
TAIL = 16
VMEM = pl.BlockSpec(memory_space=pltpu.VMEM)
SMEM = pl.BlockSpec(memory_space=pltpu.SMEM)
ANY = pl.BlockSpec(memory_space=pl.ANY)
SUM_RINGS = (("x", "y"), ("y", "z"), ("z", "x"))
HEAD_RING = ("y", "z")
ROW_RING = ("z", "y")


def params(mib):
    return pltpu.CompilerParams(vmem_limit_bytes=mib << 20)


def turn(axes, step):
    pairs = []
    for x in range(4):
        for c in range(2):
            for z in range(4):
                for y in range(4):
                    at = {"x": x, "z": z, "y": y}
                    to = dict(at)
                    to[axes[c]] = (at[axes[c]] + step) % 4
                    flat = [((p["x"] * 2 + c) * 4 + p["z"]) * 4 + p["y"] for p in (at, to)]
                    pairs.append(tuple(flat))
    return pairs


def exchange(pieces, axes, sign=1):
    got = [pieces[0], None, None, None]
    for d in (2, 1, 3):
        got[d] = lax.ppermute(pieces[d], AXES, turn(axes, sign * d))
    return got


def total_of(got):
    a, b, c, d = (g.astype(F32) for g in got)
    return (a + c) + (b + d)


def project(at, tokens, query_weight, key_weight, value_weight):
    rows = tokens.shape[0]

    def kernel(at_ref, tok_ref, wq_ref, wk_ref, wv_ref, *refs):
        outs, held = refs[:4], refs[4]
        tok = tok_ref[...]
        v = jnp.dot(tok, wv_ref[...], preferred_element_type=F32)
        k = jnp.dot(tok, wk_ref[...], preferred_element_type=F32)
        q = jnp.dot(tok, wq_ref[...], preferred_element_type=F32)
        zero = jnp.zeros((rows, DH), F32)
        for h in range(H):
            held[h] = jnp.concatenate(
                [
                    v[:, h * DV : (h + 1) * DV],
                    k[:, h * DH : (h + 1) * DH],
                    zero,
                    q[:, h * DH : (h + 1) * DH],
                ],
                axis=1,
            ).astype(BF)
        for d in range(4):
            outs[d][...] = held[(at_ref[0] + d) % 4]

    return pl.pallas_call(
        kernel,
        out_shape=[jax.ShapeDtypeStruct((rows, 384), BF)] * 4,
        in_specs=[SMEM] + [VMEM] * 4,
        out_specs=[VMEM] * 4,
        scratch_shapes=[pltpu.VMEM((4, rows, 384), BF)],
        compiler_params=params(40),
        name="project",
    )(at, tokens, query_weight, key_weight, value_weight)


def stack_rows(parts):
    rows = parts[0].shape[0]

    def kernel(*refs):
        ins, out = refs[:4], refs[4]
        row = lax.broadcasted_iota(jnp.int32, (TAIL, 128), 0)
        tail = jnp.zeros((TAIL, 128), F32)
        for d in range(4):
            out[d * rows : (d + 1) * rows, :] = ins[d][:, :256]
            first = ins[d][:TAIL, 256:].astype(F32)[:1]
            final = ins[d][rows - TAIL :, 256:].astype(F32)[TAIL - 1 :]
            tail = jnp.where(row == d, first, tail)
            tail = jnp.where(row == 4 + d, final, tail)
        out[4 * rows :, :128] = jnp.zeros((TAIL, 128), BF)
        out[4 * rows :, 128:] = tail.astype(BF)

    return pl.pallas_call(
        kernel,
        out_shape=jax.ShapeDtypeStruct((4 * rows + TAIL, 256), BF),
        in_specs=[VMEM] * 4,
        out_specs=VMEM,
        compiler_params=params(16),
        name="stack_rows",
    )(*parts)


def attend(bases, q, pairs, state, flags=None):
    rows = q[0].shape[0]
    width = 4 * rows
    first = state is None
    last = flags is not None

    def kernel(bases_ref, *refs):
        if last:
            flags_ref, refs = refs[0], refs[1:]
        q_refs, refs = refs[:4], refs[4:]
        pair_refs, refs = refs[: len(pairs)], refs[len(pairs) :]
        if not first:
            max_in, sum_in, refs = refs[:4], refs[4:8], refs[8:]
        lane = lax.broadcasted_iota(jnp.int32, (width, 256), 1)
        place = lax.broadcasted_iota(jnp.int32, (1, rows), 1)

        def masks(n):
            return jnp.concatenate(
                [place + bases_ref[4 * n + i] < bases_ref[16] for i in range(4)], axis=1
            )

        def values_of(ref):
            return jnp.where(lane == DV, jnp.ones((), BF), ref[:width, :])

        def scores_of(query, ref, keep):
            scores = lax.dot_general(
                query, ref[:width, 128:], (((1,), (1,)), ((), ())), preferred_element_type=F32
            )
            return jnp.where(keep, scores * (1.0 / math.sqrt(DH)), -1e30)

        def shares(sums):
            return sums / sums[:, DV : DV + 1]

        if last:
            tails = [r[width:, 128:].astype(F32) for r in pair_refs]
            own, low, high = tails[0], tails[1], tails[2]
            row = lax.broadcasted_iota(jnp.int32, (TAIL, 128), 0)
            edge = jnp.zeros((TAIL, 128), F32)
            for d in range(4):
                n, m = (d + 1) % 4, (d + 3) % 4
                other = jnp.where(flags_ref[0] == 0, own[4 + n : 5 + n], low[4 + d : 5 + d])
                prev = jnp.where(flags_ref[1 + d] == 1, low[4 + n : 5 + n], other)
                other = jnp.where(flags_ref[0] == 0, own[m : m + 1], high[d : d + 1])
                nxt = jnp.where(flags_ref[5 + d] == 1, high[m : m + 1], other)
                edge = jnp.where(row == d, prev, edge)
                edge = jnp.where(row == 4 + d, nxt, edge)
            edge = edge.astype(BF)
            parts = [scores_of(edge, r, masks(n)) for n, r in enumerate(pair_refs)]
            peak = jnp.max(parts[0], axis=1, keepdims=True)
            for s in parts[1:]:
                peak = jnp.maximum(peak, jnp.max(s, axis=1, keepdims=True))
            edge_sums = jnp.zeros((TAIL, 256), F32)
            for s, r in zip(parts, pair_refs):
                edge_sums += jnp.dot(jnp.exp(s - peak).astype(BF), values_of(r), preferred_element_type=F32)
            edge_out = shares(edge_sums)
            row = lax.broadcasted_iota(jnp.int32, (TAIL, 256), 0)

        near = len(pairs) - 1
        keep = masks(near)
        values = values_of(pair_refs[near])
        for i in range(4):
            scores = scores_of(q_refs[i][:, 256:], pair_refs[near], keep)
            peak = jnp.max(scores, axis=1, keepdims=True)
            if not first:
                before = max_in[i][:, :1]
                peak = jnp.maximum(peak, before)
            probs = jnp.exp(scores - peak).astype(BF)
            update = jnp.dot(probs, values, preferred_element_type=F32)
            if not first:
                update = update + sum_in[i][...] * jnp.exp(before - peak)
            if last:
                refs[i][:rows, :] = shares(update).astype(BF)
                ends = jnp.where(row == 0, edge_out[i : i + 1], jnp.zeros((TAIL, 256), F32))
                ends = jnp.where(row == 1, edge_out[4 + i : 5 + i], ends)
                refs[i][rows:, :] = ends.astype(BF)
            else:
                refs[i][...] = jnp.broadcast_to(peak, (rows, 128))
                refs[4 + i][...] = update

    ins = [*q, *pairs]
    if not first:
        ins += [*state[0], *state[1]]
    if last:
        outs = [jax.ShapeDtypeStruct((rows + TAIL, 256), BF)] * 4
    else:
        outs = [jax.ShapeDtypeStruct((rows, 128), F32)] * 4
        outs += [jax.ShapeDtypeStruct((rows, 256), F32)] * 4
    scalars = [bases, flags] if last else [bases]
    got = pl.pallas_call(
        kernel,
        out_shape=outs,
        in_specs=[SMEM] * len(scalars) + [VMEM] * len(ins),
        out_specs=[VMEM] * len(outs),
        compiler_params=params(40),
        cost_estimate=pl.CostEstimate(
            flops=4 * 2 * rows * width * 512, bytes_accessed=4 << 20, transcendentals=4 * rows * width
        ),
        name="attend",
    )(*scalars, *ins)
    return got if last else (got[:4], got[4:])


def gelu_parts(pre):
    slope = math.sqrt(2.0 / math.pi)
    square = pre * pre
    bend = jnp.tanh(slope * (pre + 0.044715 * (square * pre)))
    return bend, square, slope


def forward(scalars, back, tokens, halo, skipped, out_heads, depth_weight):
    rows, columns = tokens.shape
    fine = 2 * rows
    wide = 256

    def kernel(s_ref, b0, b1, b2, b3, tok_ref, halo_ref, skip_ref, ow_ref, dw_ref, up_ref, act_ref, att, held):
        @pl.when(pl.program_id(0) == 0)
        def _():
            mixed = [b[:, :DV].astype(F32) for b in (b0, b1, b2, b3)]
            squares = sum(jnp.sum(m * m, axis=1, keepdims=True) for m in mixed)
            scale = lax.rsqrt(squares * (1.0 / (H * DV)) + 1e-05)
            for d in range(4):
                att[d] = (mixed[d] * scale).astype(BF)

        grown = jnp.zeros((rows + TAIL, wide), F32)
        for d in range(4):
            grown += jnp.dot(att[d], ow_ref[(s_ref[0] + d) % 4], preferred_element_type=F32)
        hidden = (tok_ref[...].astype(F32) + grown[:rows]).astype(BF)
        ends = (halo_ref[:TAIL, :] + grown[rows:]).astype(BF).astype(F32)
        twice = lax.broadcasted_iota(jnp.int32, (fine, rows), 0) // 2
        twice = jnp.where(twice == lax.broadcasted_iota(jnp.int32, (fine, rows), 1), 1.0, 0.0).astype(BF)
        up = jnp.dot(twice, hidden, preferred_element_type=F32) + skip_ref[...].astype(F32)
        held[8 : 8 + fine, :] = up.astype(BF).astype(F32)
        row = lax.broadcasted_iota(jnp.int32, (8, wide), 0)
        low = (ends[:1] + halo_ref[16:24, :]).astype(BF).astype(F32)
        held[:8, :] = jnp.where((row >= 6) & (s_ref[1] > 0), low, 0.0)
        high = (ends[1:2] + halo_ref[24:32, :]).astype(BF).astype(F32)
        held[8 + fine :, :] = jnp.where((row < 2) & (s_ref[2] > 0), high, 0.0)
        up_ref[...] = held[...].astype(BF)
        pre = (
            dw_ref[0:1, :] * held[7 : 7 + fine, :]
            + dw_ref[1:2, :] * held[8 : 8 + fine, :]
            + dw_ref[2:3, :] * held[9 : 9 + fine, :]
        )
        bend, _, _ = gelu_parts(pre)
        act_ref[...] = (pre * (0.5 * (1.0 + bend))).astype(BF)

    def cols(count):
        return pl.BlockSpec((count, wide), lambda j: (0, j))

    whole = pl.BlockSpec((rows + TAIL, 256), lambda j: (0, 0))
    return pl.pallas_call(
        kernel,
        grid=(columns // wide,),
        out_shape=[
            jax.ShapeDtypeStruct((fine + 16, columns), BF),
            jax.ShapeDtypeStruct((fine, columns), BF),
        ],
        in_specs=[SMEM]
        + [whole] * 4
        + [
            cols(rows),
            cols(32),
            cols(fine),
            pl.BlockSpec((H, DV, wide), lambda j: (0, 0, j)),
            cols(3),
        ],
        out_specs=[cols(fine + 16), cols(fine)],
        scratch_shapes=[pltpu.VMEM((4, rows + TAIL, DV), BF), pltpu.VMEM((fine + 16, wide), F32)],
        compiler_params=params(40),
        name="forward",
    )(scalars, *back, tokens, halo, skipped, out_heads, depth_weight)


def backward(up, grad_act, grad_act_ends, depth_weight):
    fine, columns = grad_act.shape
    wide = 256

    def kernel(up_ref, ga_ref, ge_ref, dw_ref, gs_ref, gd_ref, held, grad):
        held[:8, :] = jnp.zeros((8, wide), F32)
        held[8 : fine + 24, :] = up_ref[...].astype(F32)
        held[fine + 24 :, :] = jnp.zeros((8, wide), F32)

        def grad_of(start, count, upstream):
            pre = (
                dw_ref[0:1, :] * held[start - 1 : start - 1 + count, :]
                + dw_ref[1:2, :] * held[start : start + count, :]
                + dw_ref[2:3, :] * held[start + 1 : start + 1 + count, :]
            )
            bend, square, slope = gelu_parts(pre)
            rate = 0.5 * (1.0 + bend) + (0.5 * slope) * pre * (1.0 - bend * bend) * (
                1.0 + (3 * 0.044715) * square
            )
            return (upstream * rate).astype(BF).astype(F32)

        grad[:8, :] = grad_of(8, 8, ge_ref[:8, :])
        mid = grad_of(16, fine, ga_ref[...])
        grad[8 : 8 + fine, :] = mid
        grad[8 + fine :, :] = grad_of(16 + fine, 8, ge_ref[8:, :])
        gs_ref[...] = (
            dw_ref[0:1, :] * grad[9 : 9 + fine, :]
            + dw_ref[1:2, :] * mid
            + dw_ref[2:3, :] * grad[7 : 7 + fine, :]
        ).astype(BF)
        for t in range(3):
            gd_ref[t : t + 1, :] = jnp.sum(held[15 + t : 15 + t + fine, :] * mid, axis=0, keepdims=True)

    def cols(count):
        return pl.BlockSpec((count, wide), lambda j: (0, j))

    return pl.pallas_call(
        kernel,
        grid=(columns // wide,),
        out_shape=[jax.ShapeDtypeStruct((fine, columns), BF), jax.ShapeDtypeStruct((3, columns), F32)],
        in_specs=[cols(fine + 16), cols(fine), cols(16), cols(3)],
        out_specs=[cols(fine), cols(3)],
        scratch_shapes=[pltpu.VMEM((fine + 32, wide), F32), pltpu.VMEM((fine + 16, wide), F32)],
        compiler_params=params(40),
        cost_estimate=pl.CostEstimate(flops=60 * fine * columns, bytes_accessed=9 << 20, transcendentals=fine * columns),
        name="backward",
    )(up, grad_act, grad_act_ends, depth_weight)


def product(scalars, act, upstream, steps, arrived=None):
    half, quarter = act.shape[1] // 2, upstream.shape[1] // 4
    joint = arrived is None

    def kernel(s_ref, a_ref, g_ref, *refs):
        left = a_ref[:, pl.ds(pl.multiple_of(s_ref[0] * half, 128), half)]
        for n, d in enumerate(steps):
            at = pl.multiple_of((s_ref[1] + d) % 4 * quarter, 128)
            block = lax.dot_general(
                left, g_ref[:, pl.ds(at, quarter)], (((0,), (0,)), ((), ())), preferred_element_type=F32
            )
            if joint:
                refs[0][n] = block.astype(BF)
            else:
                refs[1 + n][...] = (block + refs[0][n].astype(F32)).astype(BF)

    if joint:
        outs = jax.ShapeDtypeStruct((len(steps), half, quarter), BF)
        out_specs = VMEM
    else:
        outs = [jax.ShapeDtypeStruct((half, quarter), BF)] * len(steps)
        out_specs = [VMEM] * len(steps)
    ins = [act, upstream] if joint else [act, upstream, arrived]
    return pl.pallas_call(
        kernel,
        out_shape=outs,
        in_specs=[SMEM] + [VMEM] * len(ins),
        out_specs=out_specs,
        compiler_params=params(40),
        cost_estimate=pl.CostEstimate(
            flops=2 * act.shape[0] * half * quarter * len(steps), bytes_accessed=6 << 20, transcendentals=0
        ),
        name="product",
    )(scalars, *ins)


def split_rows(at, got, rider):
    rows, columns = got[0].shape
    slim = rows // 4

    def kernel(at_ref, *refs):
        ins, rider_ref, outs = refs[:4], refs[4], refs[5:]
        for d in range(4):
            take = pl.ds(pl.multiple_of((at_ref[0] + d) % 4 * slim, 16), slim)
            outs[d][:slim, :] = total_of([r[take, :] for r in ins]).astype(BF)
            outs[d][slim:, :] = rider_ref[...]

    return pl.pallas_call(
        kernel,
        out_shape=[jax.ShapeDtypeStruct((slim + TAIL, columns), BF)] * 4,
        in_specs=[SMEM] + [VMEM] * 5,
        out_specs=[VMEM] * 4,
        compiler_params=params(24),
        name="split_rows",
    )(at, *got, rider)


def join_rows(at, got, rider):
    slim, columns = got[0].shape

    def kernel(at_ref, *refs):
        ins, rider_ref, out = refs[:4], refs[4], refs[5]
        for d in range(4):
            put = pl.ds(pl.multiple_of((at_ref[0] + 4 - d) % 4 * slim, 16), slim)
            out[put, :] = ins[d][...]
        out[4 * slim :, :] = rider_ref[...]

    return pl.pallas_call(
        kernel,
        out_shape=jax.ShapeDtypeStruct((4 * slim + TAIL, columns), BF),
        in_specs=[SMEM] + [VMEM] * 5,
        out_specs=VMEM,
        compiler_params=params(24),
        name="join_rows",
    )(at, *got, rider)


def lay_out(scalars, own, other):
    half, quarter = own[0].shape[0] - TAIL, own[0].shape[1]

    def kernel(s_ref, *refs):
        blocks, out, sems = refs[:8], refs[8], refs[9]
        copies = []
        for n in range(8):
            mine = n < 4
            side = s_ref[0] if mine else 1 - s_ref[0]
            at = s_ref[1] if mine else s_ref[2]
            down = pl.multiple_of(side * half, 16)
            over = pl.multiple_of((at + 4 - n % 4) % 4 * quarter, 128)
            copies.append(
                pltpu.make_async_copy(
                    blocks[n].at[pl.ds(0, half), :],
                    out.at[pl.ds(down, half), pl.ds(over, quarter)],
                    sems.at[n],
                )
            )
        for copy in copies:
            copy.start()
        for copy in copies:
            copy.wait()

    return pl.pallas_call(
        kernel,
        out_shape=jax.ShapeDtypeStruct((2 * half, 4 * quarter), BF),
        in_specs=[SMEM] + [ANY] * 8,
        out_specs=ANY,
        scratch_shapes=[pltpu.SemaphoreType.DMA((8,))],
        name="lay_out",
    )(scalars, *own, *other)


def local(
    trunk,
    skip,
    valid_bins,
    query_weight,
    key_weight,
    value_weight,
    out_weight,
    depth_weight,
    point_weight,
    cotangent,
):
    tokens, skipped, upstream = trunk[0], skip[0], cotangent[0]
    rows, columns = tokens.shape
    fine = skipped.shape[0]
    ix, ic, iz, iy = (lax.axis_index(a) for a in AXES)
    index = {"x": ix, "z": iz, "y": iy}
    place = iz * 4 + iy

    def at(axes, swap=False):
        a, b = axes[::-1] if swap else axes
        return jnp.where(ic == 0, index[a], index[b])

    def ints(*values):
        return jnp.stack([jnp.asarray(v, jnp.int32) for v in values])

    head_at, row_at = at(HEAD_RING), at(ROW_RING)

    blocks = project(ints(head_at), tokens, query_weight, key_weight, value_weight)
    q = exchange(blocks, HEAD_RING)
    own = stack_rows(q)
    far = {d: lax.ppermute(own, AXES, turn(ROW_RING, d)) for d in (1, 3, 2)}

    def bases(*steps):
        values = []
        for far_by in steps:
            for d in range(4):
                h, r = (head_at - d) % 4, (row_at - far_by) % 4
                values.append(jnp.where(ic == 0, r * 4 + h, h * 4 + r) * rows)
        values += [jnp.int32(0)] * (16 - len(values)) + [valid_bins[0]]
        return ints(*values)

    state = attend(bases(0), q, [own], None)

    (tokens_l, skipped_l, upstream_l), _ = lax.optimization_barrier(
        ((tokens, skipped, upstream), state[0][0])
    )
    down = jnp.concatenate([tokens_l[-1:], skipped_l[-2:], upstream_l[-1:]], axis=0)
    up = jnp.concatenate([tokens_l[:1], skipped_l[:2], upstream_l[:1]], axis=0)
    before = lax.ppermute(down, ("z", "y"), [(i, i + 1) for i in range(15)])
    after = lax.ppermute(up, ("z", "y"), [(i + 1, i) for i in range(15)])

    def blank(count):
        return jnp.zeros((count, columns), BF)

    halo = jnp.concatenate(
        [before[:1], after[:1], blank(20), before[1:3], after[1:3], blank(6)], axis=0
    ).astype(F32)
    ends = jnp.concatenate([blank(7), before[3:4], after[3:4], blank(7)], axis=0)
    dims = (((1,), (1,)), ((), ()))
    grad_act = lax.dot_general(upstream_l, point_weight, dims, preferred_element_type=F32)
    grad_act_ends = lax.dot_general(ends, point_weight, dims, preferred_element_type=F32)

    state = attend(bases(1), q, [far[1]], state)
    state = attend(bases(3), q, [far[3]], state)
    flags = [ic]
    for d in range(4):
        flags.append(jnp.where(ic == 0, (iy - d) % 4, iy) == 0)
    for d in range(4):
        flags.append(jnp.where(ic == 0, (iy - d) % 4, iy) == 3)
    mixed = attend(bases(0, 1, 3, 2), q, [own, far[1], far[3], far[2]], state, ints(*flags))
    back = exchange(mixed, HEAD_RING, -1)
    up_rows, act = forward(
        ints(head_at, place > 0, place < 15), back, tokens, halo, skipped, out_weight.reshape(H, DV, -1), depth_weight
    )

    swap = [(0, 1), (1, 0)]
    theirs = ints(1 - ic, at(SUM_RINGS[0], True))
    mine = ints(ic, at(SUM_RINGS[0]))
    sent = [product(theirs, act, upstream, steps) for steps in ((2, 1), (3, 0))]
    arrived = [lax.ppermute(s, "c", swap) for s in sent]
    piece_2, piece_1 = product(mine, act, upstream, (2, 1), arrived[0])
    piece_3, piece_0 = product(mine, act, upstream, (3, 0), arrived[1])
    got = exchange([piece_0, piece_1, piece_2, piece_3], SUM_RINGS[0])

    (up_rows, grad_act), _ = lax.optimization_barrier(((up_rows, grad_act), (piece_0, piece_1)))
    grad_skip, depth_term = backward(up_rows, grad_act, grad_act_ends, depth_weight)
    half = columns // 2
    d_theirs = lax.dynamic_slice_in_dim(depth_term, (1 - ic) * half, half, axis=1)
    d_mine = lax.dynamic_slice_in_dim(depth_term, ic * half, half, axis=1)
    d_sum = d_mine + lax.ppermute(d_theirs, "c", swap)
    rider = jnp.pad(d_sum.reshape(6, half // 2).astype(BF), ((0, TAIL - 6), (0, 0)))

    slim = half // 4
    second_at = at(SUM_RINGS[1])
    got = exchange(split_rows(ints(second_at), got, rider), SUM_RINGS[1])
    got = exchange([total_of(got).astype(BF)] * 4, SUM_RINGS[2])
    norm_scale = 1.0 / math.sqrt(128 * fine)
    summed = (total_of(got) * norm_scale).astype(BF)
    piece, rider = summed[:slim], summed[slim:]
    joined = join_rows(ints(second_at), exchange([piece] * 4, SUM_RINGS[1]), rider)
    got = exchange([joined] * 4, SUM_RINGS[0])
    other = [lax.ppermute(g, "c", swap) for g in got]
    grad_pointwise = lay_out(ints(ic, at(SUM_RINGS[0]), at(SUM_RINGS[0], True)), got, other)

    def depth_of(blocks):
        return total_of([b[half : half + 6] for b in blocks]).reshape(3, half)

    d_own, d_other = depth_of(got), depth_of(other)
    grad_depth = jnp.concatenate(
        [jnp.where(ic == 0, d_own, d_other), jnp.where(ic == 0, d_other, d_own)], axis=1
    )
    return (grad_pointwise, grad_depth, grad_skip[None])


def solution(mesh):
    fine_mesh = Mesh(mesh.devices.reshape(SIZES), AXES)
    rows = P(("x", "c"), ("z", "y"), None)
    return jax.shard_map(
        local,
        mesh=fine_mesh,
        in_specs=(rows, rows, P(("x", "c")), P(), P(), P(), P(), P(), P(), rows),
        out_specs=(P(), P(), rows),
        check_vma=False,
    )
```

```python
import math

import jax
import jax.numpy as jnp
from jax import lax
from jax.experimental import pallas as pl
from jax.experimental.pallas import tpu as pltpu
from jax.sharding import Mesh, PartitionSpec as P

H = 4
DH = 64
DV = 192
AXES = ("x", "c", "z", "y")
SIZES = (4, 2, 4, 4)
BF = jnp.bfloat16
F32 = jnp.float32
TAIL = 16
VMEM = pl.BlockSpec(memory_space=pltpu.VMEM)
SMEM = pl.BlockSpec(memory_space=pltpu.SMEM)
ANY = pl.BlockSpec(memory_space=pl.ANY)
SUM_RINGS = (("x", "y"), ("y", "z"), ("z", "x"))
HEAD_RING = ("y", "z")
ROW_RING = ("z", "y")


def params(mib):
    return pltpu.CompilerParams(vmem_limit_bytes=mib << 20)


def turn(axes, step):
    pairs = []
    for x in range(4):
        for c in range(2):
            for z in range(4):
                for y in range(4):
                    at = {"x": x, "z": z, "y": y}
                    to = dict(at)
                    to[axes[c]] = (at[axes[c]] + step) % 4
                    flat = [((p["x"] * 2 + c) * 4 + p["z"]) * 4 + p["y"] for p in (at, to)]
                    pairs.append(tuple(flat))
    return pairs


def exchange(pieces, axes, sign=1):
    got = [pieces[0], None, None, None]
    for d in (2, 1, 3):
        got[d] = lax.ppermute(pieces[d], AXES, turn(axes, sign * d))
    return got


def total_of(got):
    a, b, c, d = (g.astype(F32) for g in got)
    return (a + c) + (b + d)


def project(at, tokens, query_weight, key_weight, value_weight):
    rows, depth = tokens.shape
    step = 384
    count = depth // step

    def kernel(at_ref, tok_ref, wq_ref, wk_ref, wv_ref, *refs):
        outs, q_sum, k_sum, v_sum, held = refs[:4], refs[4], refs[5], refs[6], refs[7]
        j = pl.program_id(0)
        tok = tok_ref[...]
        for total, w_ref in ((v_sum, wv_ref), (k_sum, wk_ref), (q_sum, wq_ref)):
            term = jnp.dot(tok, w_ref[...], preferred_element_type=F32)

            @pl.when(j == 0)
            def _():
                total[...] = term

            @pl.when(j > 0)
            def _():
                total[...] += term

        @pl.when(j == count - 1)
        def _():
            zero = jnp.zeros((rows, DH), F32)
            for h in range(H):
                held[h] = jnp.concatenate(
                    [
                        v_sum[:, h * DV : (h + 1) * DV],
                        k_sum[:, h * DH : (h + 1) * DH],
                        zero,
                        q_sum[:, h * DH : (h + 1) * DH] * (1.0 / math.sqrt(DH)),
                    ],
                    axis=1,
                ).astype(BF)
            for d in range(4):
                outs[d][...] = held[(at_ref[0] + d) % 4]

    def deep(width):
        return pl.BlockSpec((step, width), lambda j: (j, 0))

    return pl.pallas_call(
        kernel,
        grid=(count,),
        out_shape=[jax.ShapeDtypeStruct((rows, 384), BF)] * 4,
        in_specs=[
            SMEM,
            pl.BlockSpec((rows, step), lambda j: (0, j)),
            deep(H * DH),
            deep(H * DH),
            deep(H * DV),
        ],
        out_specs=[pl.BlockSpec((rows, 384), lambda j: (0, 0))] * 4,
        scratch_shapes=[
            pltpu.VMEM((rows, H * DH), F32),
            pltpu.VMEM((rows, H * DH), F32),
            pltpu.VMEM((rows, H * DV), F32),
            pltpu.VMEM((4, rows, 384), BF),
        ],
        compiler_params=params(60),
        name="project",
    )(at, tokens, query_weight, key_weight, value_weight)


def stack_rows(parts):
    rows = parts[0].shape[0]

    def kernel(*refs):
        ins, out = refs[:4], refs[4]
        row = lax.broadcasted_iota(jnp.int32, (TAIL, 128), 0)
        tail = jnp.zeros((TAIL, 128), F32)
        for d in range(4):
            out[d * rows : (d + 1) * rows, :] = ins[d][:, :256]
            first = ins[d][:TAIL, 256:].astype(F32)[:1]
            final = ins[d][rows - TAIL :, 256:].astype(F32)[TAIL - 1 :]
            tail = jnp.where(row == d, first, tail)
            tail = jnp.where(row == 4 + d, final, tail)
        out[4 * rows :, :128] = jnp.zeros((TAIL, 128), BF)
        out[4 * rows :, 128:] = tail.astype(BF)

    return pl.pallas_call(
        kernel,
        out_shape=jax.ShapeDtypeStruct((4 * rows + TAIL, 256), BF),
        in_specs=[VMEM] * 4,
        out_specs=VMEM,
        compiler_params=params(16),
        name="stack_rows",
    )(*parts)


def attend(bases, q, pairs, state, flags=None):
    rows = q[0].shape[0]
    width = 4 * rows
    first = state is None
    last = flags is not None

    def kernel(bases_ref, *refs):
        if last:
            flags_ref, refs = refs[0], refs[1:]
        q_refs, refs = refs[:4], refs[4:]
        pair_refs, refs = refs[: len(pairs)], refs[len(pairs) :]
        if not first:
            max_in, sum_in, refs = refs[:4], refs[4:8], refs[8:]
        lane = lax.broadcasted_iota(jnp.int32, (width, 256), 1)
        place = lax.broadcasted_iota(jnp.int32, (1, rows), 1)

        def masks(n):
            return jnp.concatenate(
                [place + bases_ref[4 * n + i] < bases_ref[16] for i in range(4)], axis=1
            )

        def values_of(ref):
            return jnp.where(lane == DV, jnp.ones((), BF), ref[:width, :])

        def scores_of(query, ref, keep):
            scores = lax.dot_general(
                query, ref[:width, 128:], (((1,), (1,)), ((), ())), preferred_element_type=F32
            )
            return jnp.where(keep, scores, -1e30)

        def shares(sums):
            return sums / sums[:, DV : DV + 1]

        if last:
            tails = [r[width:, 128:].astype(F32) for r in pair_refs]
            own, low, high = tails[0], tails[1], tails[2]
            row = lax.broadcasted_iota(jnp.int32, (TAIL, 128), 0)
            edge = jnp.zeros((TAIL, 128), F32)
            for d in range(4):
                n, m = (d + 1) % 4, (d + 3) % 4
                other = jnp.where(flags_ref[0] == 0, own[4 + n : 5 + n], low[4 + d : 5 + d])
                prev = jnp.where(flags_ref[1 + d] == 1, low[4 + n : 5 + n], other)
                other = jnp.where(flags_ref[0] == 0, own[m : m + 1], high[d : d + 1])
                nxt = jnp.where(flags_ref[5 + d] == 1, high[m : m + 1], other)
                edge = jnp.where(row == d, prev, edge)
                edge = jnp.where(row == 4 + d, nxt, edge)
            edge = edge.astype(BF)
            parts = [scores_of(edge, r, masks(n)) for n, r in enumerate(pair_refs)]
            peak = jnp.max(parts[0], axis=1, keepdims=True)
            for s in parts[1:]:
                peak = jnp.maximum(peak, jnp.max(s, axis=1, keepdims=True))
            edge_sums = jnp.zeros((TAIL, 256), F32)
            for s, r in zip(parts, pair_refs):
                edge_sums += jnp.dot(jnp.exp(s - peak).astype(BF), values_of(r), preferred_element_type=F32)
            edge_out = shares(edge_sums)
            row = lax.broadcasted_iota(jnp.int32, (TAIL, 256), 0)

        near = len(pairs) - 1
        keep = masks(near)
        values = values_of(pair_refs[near])
        for i in range(4):
            scores = scores_of(q_refs[i][:, 256:], pair_refs[near], keep)
            peak = jnp.max(scores, axis=1, keepdims=True)
            if not first:
                before = max_in[i][:, :1]
                peak = jnp.maximum(peak, before)
            probs = jnp.exp(scores - peak).astype(BF)
            update = jnp.dot(probs, values, preferred_element_type=F32)
            if not first:
                update = update + sum_in[i][...] * jnp.exp(before - peak)
            if last:
                refs[i][:rows, :] = shares(update).astype(BF)
                ends = jnp.where(row == 0, edge_out[i : i + 1], jnp.zeros((TAIL, 256), F32))
                ends = jnp.where(row == 1, edge_out[4 + i : 5 + i], ends)
                refs[i][rows:, :] = ends.astype(BF)
            else:
                refs[i][...] = jnp.broadcast_to(peak, (rows, 128))
                refs[4 + i][...] = update

    ins = [*q, *pairs]
    if not first:
        ins += [*state[0], *state[1]]
    if last:
        outs = [jax.ShapeDtypeStruct((rows + TAIL, 256), BF)] * 4
    else:
        outs = [jax.ShapeDtypeStruct((rows, 128), F32)] * 4
        outs += [jax.ShapeDtypeStruct((rows, 256), F32)] * 4
    scalars = [bases, flags] if last else [bases]
    got = pl.pallas_call(
        kernel,
        out_shape=outs,
        in_specs=[SMEM] * len(scalars) + [VMEM] * len(ins),
        out_specs=[VMEM] * len(outs),
        compiler_params=params(40),
        cost_estimate=pl.CostEstimate(
            flops=4 * 2 * rows * width * 512, bytes_accessed=4 << 20, transcendentals=4 * rows * width
        ),
        name="attend",
    )(*scalars, *ins)
    return got if last else (got[:4], got[4:])


def gelu_parts(pre):
    slope = math.sqrt(2.0 / math.pi)
    square = pre * pre
    bend = jnp.tanh(slope * (pre + 0.044715 * (square * pre)))
    return bend, square, slope


def forward(scalars, back, tokens, halo, skipped, out_heads, depth_weight):
    rows, columns = tokens.shape
    fine = 2 * rows
    wide = 256

    def kernel(s_ref, b0, b1, b2, b3, tok_ref, halo_ref, skip_ref, ow_ref, dw_ref, up_ref, act_ref, att, held):
        @pl.when(pl.program_id(0) == 0)
        def _():
            mixed = [b[:, :DV].astype(F32) for b in (b0, b1, b2, b3)]
            squares = sum(jnp.sum(m * m, axis=1, keepdims=True) for m in mixed)
            scale = lax.rsqrt(squares * (1.0 / (H * DV)) + 1e-05)
            for d in range(4):
                att[d] = (mixed[d] * scale).astype(BF)

        grown = jnp.zeros((rows + TAIL, wide), F32)
        for d in range(4):
            grown += jnp.dot(att[d], ow_ref[(s_ref[0] + d) % 4], preferred_element_type=F32)
        hidden = (tok_ref[...].astype(F32) + grown[:rows]).astype(BF)
        ends = (halo_ref[:TAIL, :] + grown[rows:]).astype(BF).astype(F32)
        twice = lax.broadcasted_iota(jnp.int32, (fine, rows), 0) // 2
        twice = jnp.where(twice == lax.broadcasted_iota(jnp.int32, (fine, rows), 1), 1.0, 0.0).astype(BF)
        up = jnp.dot(twice, hidden, preferred_element_type=F32) + skip_ref[...].astype(F32)
        held[8 : 8 + fine, :] = up.astype(BF).astype(F32)
        row = lax.broadcasted_iota(jnp.int32, (8, wide), 0)
        low = (ends[:1] + halo_ref[16:24, :]).astype(BF).astype(F32)
        held[:8, :] = jnp.where((row >= 6) & (s_ref[1] > 0), low, 0.0)
        high = (ends[1:2] + halo_ref[24:32, :]).astype(BF).astype(F32)
        held[8 + fine :, :] = jnp.where((row < 2) & (s_ref[2] > 0), high, 0.0)
        up_ref[...] = held[...].astype(BF)
        pre = (
            dw_ref[0:1, :] * held[7 : 7 + fine, :]
            + dw_ref[1:2, :] * held[8 : 8 + fine, :]
            + dw_ref[2:3, :] * held[9 : 9 + fine, :]
        )
        bend, _, _ = gelu_parts(pre)
        act_ref[...] = (pre * (0.5 * (1.0 + bend))).astype(BF)

    def cols(count):
        return pl.BlockSpec((count, wide), lambda j: (0, j))

    whole = pl.BlockSpec((rows + TAIL, 256), lambda j: (0, 0))
    return pl.pallas_call(
        kernel,
        grid=(columns // wide,),
        out_shape=[
            jax.ShapeDtypeStruct((fine + 16, columns), BF),
            jax.ShapeDtypeStruct((fine, columns), BF),
        ],
        in_specs=[SMEM]
        + [whole] * 4
        + [
            cols(rows),
            cols(32),
            cols(fine),
            pl.BlockSpec((H, DV, wide), lambda j: (0, 0, j)),
            cols(3),
        ],
        out_specs=[cols(fine + 16), cols(fine)],
        scratch_shapes=[pltpu.VMEM((4, rows + TAIL, DV), BF), pltpu.VMEM((fine + 16, wide), F32)],
        compiler_params=params(60),
        name="forward",
    )(scalars, *back, tokens, halo, skipped, out_heads, depth_weight)


def backward(up, upstream, ends, point_weight, depth_weight):
    fine, columns = upstream.shape
    wide = 256

    def kernel(up_ref, g_ref, e_ref, pw_ref, dw_ref, gs_ref, gd_ref, held, grad):
        dims = (((1,), (1,)), ((), ()))
        upper = lax.dot_general(g_ref[...], pw_ref[...], dims, preferred_element_type=F32)
        edges = lax.dot_general(e_ref[...], pw_ref[...], dims, preferred_element_type=F32)
        held[:8, :] = jnp.zeros((8, wide), F32)
        held[8 : fine + 24, :] = up_ref[...].astype(F32)
        held[fine + 24 :, :] = jnp.zeros((8, wide), F32)

        def grad_of(start, count, upstream):
            pre = (
                dw_ref[0:1, :] * held[start - 1 : start - 1 + count, :]
                + dw_ref[1:2, :] * held[start : start + count, :]
                + dw_ref[2:3, :] * held[start + 1 : start + 1 + count, :]
            )
            bend, square, slope = gelu_parts(pre)
            rate = 0.5 * (1.0 + bend) + (0.5 * slope) * pre * (1.0 - bend * bend) * (
                1.0 + (3 * 0.044715) * square
            )
            return (upstream * rate).astype(BF).astype(F32)

        grad[:8, :] = grad_of(8, 8, edges[:8])
        mid = grad_of(16, fine, upper)
        grad[8 : 8 + fine, :] = mid
        grad[8 + fine :, :] = grad_of(16 + fine, 8, edges[8:])
        gs_ref[...] = (
            dw_ref[0:1, :] * grad[9 : 9 + fine, :]
            + dw_ref[1:2, :] * mid
            + dw_ref[2:3, :] * grad[7 : 7 + fine, :]
        ).astype(BF)
        for t in range(3):
            gd_ref[t : t + 1, :] = jnp.sum(held[15 + t : 15 + t + fine, :] * mid, axis=0, keepdims=True)

    def cols(count):
        return pl.BlockSpec((count, wide), lambda j: (0, j))

    return pl.pallas_call(
        kernel,
        grid=(columns // wide,),
        out_shape=[jax.ShapeDtypeStruct((fine, columns), BF), jax.ShapeDtypeStruct((3, columns), F32)],
        in_specs=[
            cols(fine + 16),
            pl.BlockSpec((fine, columns), lambda j: (0, 0)),
            pl.BlockSpec((16, columns), lambda j: (0, 0)),
            pl.BlockSpec((wide, columns), lambda j: (j, 0)),
            cols(3),
        ],
        out_specs=[cols(fine), cols(3)],
        scratch_shapes=[pltpu.VMEM((fine + 32, wide), F32), pltpu.VMEM((fine + 16, wide), F32)],
        compiler_params=params(40),
        cost_estimate=pl.CostEstimate(
            flops=2 * fine * columns * columns, bytes_accessed=11 << 20, transcendentals=fine * columns
        ),
        name="backward",
    )(up, upstream, ends, point_weight, depth_weight)


def product(scalars, act, turned, steps, arrived=None):
    half, quarter = act.shape[1] // 2, turned.shape[0] // 4
    joint = arrived is None

    def kernel(s_ref, a_ref, g_ref, *refs):
        right = a_ref[:, pl.ds(pl.multiple_of(s_ref[0] * half, 128), half)]
        for n, d in enumerate(steps):
            at = pl.multiple_of((s_ref[1] + d) % 4 * quarter, 16)
            block = jnp.dot(g_ref[pl.ds(at, quarter), :], right, preferred_element_type=F32)
            if joint:
                refs[0][n] = block.astype(BF)
            else:
                refs[1 + n][...] = (block + refs[0][n].astype(F32)).astype(BF)

    if joint:
        outs = jax.ShapeDtypeStruct((len(steps), quarter, half), BF)
        out_specs = VMEM
    else:
        outs = [jax.ShapeDtypeStruct((quarter, half), BF)] * len(steps)
        out_specs = [VMEM] * len(steps)
    ins = [act, turned] if joint else [act, turned, arrived]
    return pl.pallas_call(
        kernel,
        out_shape=outs,
        in_specs=[SMEM] + [VMEM] * len(ins),
        out_specs=out_specs,
        compiler_params=params(40),
        cost_estimate=pl.CostEstimate(
            flops=2 * act.shape[0] * half * quarter * len(steps), bytes_accessed=6 << 20, transcendentals=0
        ),
        name="product",
    )(scalars, *ins)


def split_rows(at, got, rider):
    rows, columns = got[0].shape
    slim = rows // 4

    def kernel(at_ref, *refs):
        ins, rider_ref, outs = refs[:4], refs[4], refs[5:]
        for d in range(4):
            take = pl.ds(pl.multiple_of((at_ref[0] + d) % 4 * slim, 16), slim)
            outs[d][:slim, :] = total_of([r[take, :] for r in ins]).astype(BF)
            outs[d][slim:, :] = rider_ref[...]

    return pl.pallas_call(
        kernel,
        out_shape=[jax.ShapeDtypeStruct((slim + TAIL, columns), BF)] * 4,
        in_specs=[SMEM] + [VMEM] * 5,
        out_specs=[VMEM] * 4,
        compiler_params=params(24),
        name="split_rows",
    )(at, *got, rider)


def join_rows(at, got, rider):
    slim, columns = got[0].shape

    def kernel(at_ref, *refs):
        ins, rider_ref, out, held = refs[:4], refs[4], refs[5], refs[6]
        for d in range(4):
            put = pl.ds(pl.multiple_of((at_ref[0] + 4 - d) % 4 * slim, 16), slim)
            held[put, :] = ins[d][...]
        out[:columns, :] = held[...].T
        last = rider_ref[...].astype(F32)[:8]
        out[columns:, :] = jnp.concatenate([last[:, : 4 * slim], last[:, 4 * slim :]], axis=0).astype(BF)

    return pl.pallas_call(
        kernel,
        out_shape=jax.ShapeDtypeStruct((columns + TAIL, 4 * slim), BF),
        in_specs=[SMEM] + [VMEM] * 5,
        out_specs=VMEM,
        scratch_shapes=[pltpu.VMEM((4 * slim, columns), BF)],
        compiler_params=params(24),
        name="join_rows",
    )(at, *got, rider)


def lay_out(scalars, own, other):
    half, quarter = own[0].shape[0] - TAIL, own[0].shape[1]

    def kernel(s_ref, *refs):
        blocks, out = refs[:8], refs[8]
        for n in range(8):

            @pl.when(pl.program_id(0) == n)
            def _():
                out[...] = blocks[n][:half, :]

    def place(n, s_ref):
        mine = n < 4
        side = jnp.where(mine, s_ref[0], 1 - s_ref[0])
        at = jnp.where(mine, s_ref[1], s_ref[2])
        return side, (at + 8 - n) % 4

    return pl.pallas_call(
        kernel,
        out_shape=jax.ShapeDtypeStruct((2 * half, 4 * quarter), BF),
        grid_spec=pltpu.PrefetchScalarGridSpec(
            num_scalar_prefetch=1,
            grid=(8,),
            in_specs=[pl.BlockSpec((half + TAIL, quarter), lambda n, s_ref: (0, 0))] * 8,
            out_specs=pl.BlockSpec((half, quarter), place),
        ),
        compiler_params=params(24),
        name="lay_out",
    )(scalars, *own, *other)


def local(
    trunk,
    skip,
    valid_bins,
    query_weight,
    key_weight,
    value_weight,
    out_weight,
    depth_weight,
    point_weight,
    cotangent,
):
    tokens, skipped, upstream = trunk[0], skip[0], cotangent[0]
    rows, columns = tokens.shape
    fine = skipped.shape[0]
    ix, ic, iz, iy = (lax.axis_index(a) for a in AXES)
    index = {"x": ix, "z": iz, "y": iy}
    place = iz * 4 + iy

    def at(axes, swap=False):
        a, b = axes[::-1] if swap else axes
        return jnp.where(ic == 0, index[a], index[b])

    def ints(*values):
        return jnp.stack([jnp.asarray(v, jnp.int32) for v in values])

    head_at, row_at = at(HEAD_RING), at(ROW_RING)

    blocks = project(ints(head_at), tokens, query_weight, key_weight, value_weight)
    q = exchange(blocks, HEAD_RING)
    own = stack_rows(q)
    far = {d: lax.ppermute(own, AXES, turn(ROW_RING, d)) for d in (1, 3)}

    def bases(*steps):
        values = []
        for far_by in steps:
            for d in range(4):
                h, r = (head_at - d) % 4, (row_at - far_by) % 4
                values.append(jnp.where(ic == 0, r * 4 + h, h * 4 + r) * rows)
        values += [jnp.int32(0)] * (16 - len(values)) + [valid_bins[0]]
        return ints(*values)

    state = attend(bases(0), q, [own], None)
    own_2, _ = lax.optimization_barrier((own, state[0][0]))
    far[2] = lax.ppermute(own_2, AXES, turn(ROW_RING, 2))

    (tokens_l, skipped_l, upstream_l), _ = lax.optimization_barrier(
        ((tokens, skipped, upstream), state[0][0])
    )
    down = jnp.concatenate([tokens_l[-1:], skipped_l[-2:], upstream_l[-1:]], axis=0)
    up = jnp.concatenate([tokens_l[:1], skipped_l[:2], upstream_l[:1]], axis=0)
    before = lax.ppermute(down, ("z", "y"), [(i, i + 1) for i in range(15)])
    after = lax.ppermute(up, ("z", "y"), [(i + 1, i) for i in range(15)])

    def blank(count):
        return jnp.zeros((count, columns), BF)

    halo = jnp.concatenate(
        [before[:1], after[:1], blank(20), before[1:3], after[1:3], blank(6)], axis=0
    ).astype(F32)
    ends = jnp.concatenate([blank(7), before[3:4], after[3:4], blank(7)], axis=0)
    turned = upstream_l.T

    state = attend(bases(1), q, [far[1]], state)
    state = attend(bases(3), q, [far[3]], state)
    flags = [ic]
    for d in range(4):
        flags.append(jnp.where(ic == 0, (iy - d) % 4, iy) == 0)
    for d in range(4):
        flags.append(jnp.where(ic == 0, (iy - d) % 4, iy) == 3)
    mixed = attend(bases(0, 1, 3, 2), q, [own, far[1], far[3], far[2]], state, ints(*flags))
    back = exchange(mixed, HEAD_RING, -1)
    up_rows, act = forward(
        ints(head_at, place > 0, place < 15), back, tokens, halo, skipped, out_weight.reshape(H, DV, -1), depth_weight
    )

    swap = [(0, 1), (1, 0)]
    theirs = ints(1 - ic, at(SUM_RINGS[0], True))
    mine = ints(ic, at(SUM_RINGS[0]))
    sent = [product(theirs, act, turned, steps) for steps in ((2, 1), (3, 0))]
    arrived = [lax.ppermute(s, "c", swap) for s in sent]
    piece_2, piece_1 = product(mine, act, turned, (2, 1), arrived[0])
    piece_3, piece_0 = product(mine, act, turned, (3, 0), arrived[1])
    got = exchange([piece_0, piece_1, piece_2, piece_3], SUM_RINGS[0])

    up_rows, _ = lax.optimization_barrier((up_rows, (piece_0, piece_1)))
    grad_skip, depth_term = backward(up_rows, upstream, ends, point_weight, depth_weight)
    half = columns // 2
    d_theirs = lax.dynamic_slice_in_dim(depth_term, (1 - ic) * half, half, axis=1)
    d_mine = lax.dynamic_slice_in_dim(depth_term, ic * half, half, axis=1)
    d_sum = d_mine + lax.ppermute(d_theirs, "c", swap)
    rider = jnp.pad(d_sum.astype(BF), ((0, TAIL - 3), (0, 0)))

    slim = columns // 16
    second_at = at(SUM_RINGS[1])
    got = exchange(split_rows(ints(second_at), got, rider), SUM_RINGS[1])
    got = exchange([total_of(got).astype(BF)] * 4, SUM_RINGS[2])
    norm_scale = 1.0 / math.sqrt(128 * fine)
    summed = (total_of(got) * norm_scale).astype(BF)
    piece, rider = summed[:slim], summed[slim:]
    joined = join_rows(ints(second_at), exchange([piece] * 4, SUM_RINGS[1]), rider)
    got = exchange([joined] * 4, SUM_RINGS[0])
    other = [lax.ppermute(g, "c", swap) for g in got]
    grad_pointwise = lay_out(ints(ic, at(SUM_RINGS[0]), at(SUM_RINGS[0], True)), got, other)

    def depth_of(blocks):
        rows = total_of([b[half:] for b in blocks])
        return jnp.concatenate([rows[:3], rows[8:11]], axis=1)

    d_own, d_other = depth_of(got), depth_of(other)
    grad_depth = jnp.concatenate(
        [jnp.where(ic == 0, d_own, d_other), jnp.where(ic == 0, d_other, d_own)], axis=1
    )
    return (grad_pointwise, grad_depth, grad_skip[None])


def solution(mesh):
    fine_mesh = Mesh(mesh.devices.reshape(SIZES), AXES)
    rows = P(("x", "c"), ("z", "y"), None)
    return jax.shard_map(
        local,
        mesh=fine_mesh,
        in_specs=(rows, rows, P(("x", "c")), P(), P(), P(), P(), P(), P(), rows),
        out_specs=(P(), P(), rows),
        check_vma=False,
    )
```

```python
import math

import jax
import jax.numpy as jnp
from jax import lax
from jax.experimental import pallas as pl
from jax.experimental.pallas import tpu as pltpu
from jax.sharding import Mesh, PartitionSpec as P

H = 4
DH = 64
DV = 192
AXES = ("x", "c", "z", "y")
SIZES = (4, 2, 4, 4)
BF = jnp.bfloat16
F32 = jnp.float32
TAIL = 16
VMEM = pl.BlockSpec(memory_space=pltpu.VMEM)
SMEM = pl.BlockSpec(memory_space=pltpu.SMEM)
ANY = pl.BlockSpec(memory_space=pl.ANY)
SUM_RINGS = (("x", "y"), ("y", "z"), ("z", "x"))
HEAD_RING = ("y", "z")
CORE, HEAD_AT, HAS_LOW, HAS_HIGH, FIRST_AT, THEIR_FIRST, SECOND_AT, FLAGS, BASES, VALID = 0, 1, 2, 3, 4, 5, 6, 8, 17, 33
ROW_RING = ("z", "y")


def params(mib):
    return pltpu.CompilerParams(vmem_limit_bytes=mib << 20)


def turn(axes, step):
    pairs = []
    for x in range(4):
        for c in range(2):
            for z in range(4):
                for y in range(4):
                    at = {"x": x, "z": z, "y": y}
                    to = dict(at)
                    to[axes[c]] = (at[axes[c]] + step) % 4
                    flat = [((p["x"] * 2 + c) * 4 + p["z"]) * 4 + p["y"] for p in (at, to)]
                    pairs.append(tuple(flat))
    return pairs


def exchange(pieces, axes, sign=1):
    got = [pieces[0], None, None, None]
    for d in (2, 1, 3):
        got[d] = lax.ppermute(pieces[d], AXES, turn(axes, sign * d))
    return got


def total_of(got):
    a, b, c, d = (g.astype(F32) for g in got)
    return (a + c) + (b + d)


def project(at, tokens, query_weight, key_weight, value_weight):
    rows, depth = tokens.shape
    cut = depth // 2

    def kernel(at_ref, tok_hbm, wq_hbm, wk_hbm, wv_hbm, *refs):
        outs, (tok_ref, wq_ref, wk_ref, wv_ref, held, sems) = refs[:4], refs[4:]
        low, high = pl.ds(0, cut), pl.ds(cut, depth - cut)
        copies = [
            pltpu.make_async_copy(tok_hbm, tok_ref, sems.at[0]),
            pltpu.make_async_copy(wv_hbm.at[low, :], wv_ref.at[low, :], sems.at[1]),
            pltpu.make_async_copy(wv_hbm.at[high, :], wv_ref.at[high, :], sems.at[2]),
            pltpu.make_async_copy(wk_hbm, wk_ref, sems.at[3]),
            pltpu.make_async_copy(wq_hbm, wq_ref, sems.at[4]),
        ]
        for copy in copies:
            copy.start()
        copies[0].wait()
        tok = tok_ref[...]
        copies[1].wait()
        v = jnp.dot(tok[:, :cut], wv_ref[:cut, :], preferred_element_type=F32)
        copies[2].wait()
        v += jnp.dot(tok[:, cut:], wv_ref[cut:, :], preferred_element_type=F32)
        copies[3].wait()
        k = jnp.dot(tok, wk_ref[...], preferred_element_type=F32)
        copies[4].wait()
        q = jnp.dot(tok, wq_ref[...], preferred_element_type=F32) * (1.0 / math.sqrt(DH))
        zero = jnp.zeros((rows, DH), F32)
        for h in range(H):
            held[h] = jnp.concatenate(
                [
                    v[:, h * DV : (h + 1) * DV],
                    k[:, h * DH : (h + 1) * DH],
                    zero,
                    q[:, h * DH : (h + 1) * DH],
                ],
                axis=1,
            ).astype(BF)
        for d in range(4):
            outs[d][...] = held[(at_ref[HEAD_AT] + d) % 4]

    return pl.pallas_call(
        kernel,
        out_shape=[jax.ShapeDtypeStruct((rows, 384), BF)] * 4,
        in_specs=[SMEM] + [ANY] * 4,
        out_specs=[VMEM] * 4,
        scratch_shapes=[
            pltpu.VMEM((rows, depth), BF),
            pltpu.VMEM((depth, H * DH), BF),
            pltpu.VMEM((depth, H * DH), BF),
            pltpu.VMEM((depth, H * DV), BF),
            pltpu.VMEM((4, rows, 384), BF),
            pltpu.SemaphoreType.DMA((5,)),
        ],
        compiler_params=params(53),
        name="project",
    )(at, tokens, query_weight, key_weight, value_weight)


def stack_rows(parts):
    rows = parts[0].shape[0]

    def kernel(*refs):
        ins, out = refs[:4], refs[4]
        row = lax.broadcasted_iota(jnp.int32, (TAIL, 128), 0)
        tail = jnp.zeros((TAIL, 128), F32)
        for d in range(4):
            out[d * rows : (d + 1) * rows, :] = ins[d][:, :256]
            first = ins[d][:TAIL, 256:].astype(F32)[:1]
            final = ins[d][rows - TAIL :, 256:].astype(F32)[TAIL - 1 :]
            tail = jnp.where(row == d, first, tail)
            tail = jnp.where(row == 4 + d, final, tail)
        out[4 * rows :, :128] = jnp.zeros((TAIL, 128), BF)
        out[4 * rows :, 128:] = tail.astype(BF)

    return pl.pallas_call(
        kernel,
        out_shape=jax.ShapeDtypeStruct((4 * rows + TAIL, 256), BF),
        in_specs=[VMEM] * 4,
        out_specs=VMEM,
        compiler_params=params(8),
        name="stack_rows",
    )(*parts)


def attend(scalars, near, q, pairs, state):
    rows = q[0].shape[0]
    width = 4 * rows
    first = state is None
    last = len(pairs) == 4

    def kernel(s_ref, *refs):
        q_refs, refs = refs[:4], refs[4:]
        pair_refs, refs = refs[: len(pairs)], refs[len(pairs) :]
        if not first:
            old, refs = refs[0], refs[1:]
        lane = lax.broadcasted_iota(jnp.int32, (width, 256), 1)
        place = lax.broadcasted_iota(jnp.int32, (1, rows), 1)

        def masks(n):
            return jnp.concatenate(
                [place + s_ref[BASES + 4 * n + i] < s_ref[VALID] for i in range(4)], axis=1
            )

        def values_of(ref):
            return jnp.where(lane == DV, jnp.ones((), BF), ref[:width, :])

        def scores_of(query, ref, keep):
            scores = lax.dot_general(
                query, ref[:width, 128:], (((1,), (1,)), ((), ())), preferred_element_type=F32
            )
            return jnp.where(keep, scores, -1e30)

        def shares(sums):
            return sums / sums[:, DV : DV + 1]

        if last:
            tails = [r[width:, 128:].astype(F32) for r in pair_refs]
            own, low, high = tails[0], tails[1], tails[2]
            row = lax.broadcasted_iota(jnp.int32, (TAIL, 128), 0)
            edge = jnp.zeros((TAIL, 128), F32)
            for d in range(4):
                n, m = (d + 1) % 4, (d + 3) % 4
                other = jnp.where(s_ref[FLAGS] == 0, own[4 + n : 5 + n], low[4 + d : 5 + d])
                prev = jnp.where(s_ref[FLAGS + 1 + d] == 1, low[4 + n : 5 + n], other)
                other = jnp.where(s_ref[FLAGS] == 0, own[m : m + 1], high[d : d + 1])
                nxt = jnp.where(s_ref[FLAGS + 5 + d] == 1, high[m : m + 1], other)
                edge = jnp.where(row == d, prev, edge)
                edge = jnp.where(row == 4 + d, nxt, edge)
            edge = edge.astype(BF)
            parts = [scores_of(edge, r, masks(n)) for n, r in enumerate(pair_refs)]
            peak = jnp.max(parts[0], axis=1, keepdims=True)
            for s in parts[1:]:
                peak = jnp.maximum(peak, jnp.max(s, axis=1, keepdims=True))
            edge_sums = jnp.zeros((TAIL, 256), F32)
            for s, r in zip(parts, pair_refs):
                edge_sums += jnp.dot(jnp.exp(s - peak).astype(BF), values_of(r), preferred_element_type=F32)
            edge_out = shares(edge_sums)
            row = lax.broadcasted_iota(jnp.int32, (TAIL, 256), 0)

        spot = lax.broadcasted_iota(jnp.int32, (rows, 256), 1)
        if not last:
            refs[1][...] = jnp.zeros((8, 128), F32)
        pair_ref = pair_refs[-1]
        keep = masks(near)
        values = values_of(pair_ref)
        for i in range(4):
            scores = scores_of(q_refs[i][:, 256:], pair_ref, keep)
            peak = jnp.max(scores, axis=1, keepdims=True)
            if not first:
                sums = old[i * rows : (i + 1) * rows, :]
                before = sums[:, DV + 1 : DV + 2]
                peak = jnp.maximum(peak, before)
            probs = jnp.exp(scores - peak).astype(BF)
            update = jnp.dot(probs, values, preferred_element_type=F32)
            if not first:
                update = update + sums * jnp.exp(before - peak)
            if last:
                refs[i][:rows, :] = shares(update).astype(BF)
                ends = jnp.where(row == 0, edge_out[i : i + 1], jnp.zeros((TAIL, 256), F32))
                ends = jnp.where(row == 1, edge_out[4 + i : 5 + i], ends)
                refs[i][rows:, :] = ends.astype(BF)
            else:
                refs[0][i * rows : (i + 1) * rows, :] = jnp.where(spot == DV + 1, peak, update)

    ins = [*q, *pairs]
    if not first:
        ins += [state]
    if last:
        outs = [jax.ShapeDtypeStruct((rows + TAIL, 256), BF)] * 4
    else:
        outs = [jax.ShapeDtypeStruct((4 * rows, 256), F32), jax.ShapeDtypeStruct((8, 128), F32)]
    got = pl.pallas_call(
        kernel,
        out_shape=outs,
        in_specs=[SMEM] + [VMEM] * len(ins),
        out_specs=[VMEM] * len(outs),
        compiler_params=params(16),
        cost_estimate=pl.CostEstimate(
            flops=4 * 2 * rows * width * 512, bytes_accessed=4 << 20, transcendentals=4 * rows * width
        ),
        name="attend",
    )(scalars, *ins)
    return got


def gelu_parts(pre):
    slope = math.sqrt(2.0 / math.pi)
    square = pre * pre
    bend = jnp.tanh(slope * (pre + 0.044715 * (square * pre)))
    return bend, square, slope


def edges(mark, trunk, skip, cotangent):
    columns = trunk.shape[1]

    def kernel(mark_ref, t_ref, s_ref, c_ref, down, up, buffer, sems):
        copies = []
        for n, ref in enumerate((t_ref, s_ref, c_ref)):
            for end in range(2):
                start = end * (ref.shape[0] - TAIL)
                copies.append(
                    pltpu.make_async_copy(
                        ref.at[pl.ds(start, TAIL), :], buffer.at[2 * n + end], sems.at[2 * n + end]
                    )
                )
        for copy in copies:
            copy.start()
        for copy in copies:
            copy.wait()
        t_first, t_last, s_first, s_last, c_first, c_last = (buffer[n].astype(F32) for n in range(6))
        row = lax.broadcasted_iota(jnp.int32, (TAIL, columns), 0)

        def four(a, b, c, d):
            rest = jnp.where(row == 2, c, jnp.where(row == 3, d, 0.0))
            return jnp.where(row == 0, a, jnp.where(row == 1, b, rest)).astype(BF)

        up[...] = four(t_first[:1], s_first[:1], s_first[1:2], c_first[:1])
        e = TAIL - 1
        down[...] = four(t_last[e:], s_last[e - 1 : e], s_last[e:], c_last[e:])

    return pl.pallas_call(
        kernel,
        out_shape=[jax.ShapeDtypeStruct((TAIL, columns), BF)] * 2,
        in_specs=[VMEM, ANY, ANY, ANY],
        out_specs=[VMEM] * 2,
        scratch_shapes=[pltpu.VMEM((6, TAIL, columns), BF), pltpu.SemaphoreType.DMA((6,))],
        compiler_params=params(8),
        name="edges",
    )(mark, trunk, skip, cotangent)


def gelu_parts(pre):
    slope = math.sqrt(2.0 / math.pi)
    square = pre * pre
    bend = jnp.tanh(slope * (pre + 0.044715 * (square * pre)))
    return bend, square, slope


WIDE = 256


def forward(scalars, ours, back, tokens, skipped, out_heads, before, after, depth_weight, turned):
    rows, columns = tokens.shape
    fine = 2 * rows
    half = columns // 2
    steps = half // WIDE
    quarter = columns // 4

    def side(s_ref):
        return s_ref[CORE] if ours else 1 - s_ref[CORE]

    def kernel(s_ref, b0, b1, b2, b3, low_ref, high_ref, dw_ref, tok_hbm, skip_hbm, ow_hbm, g_hbm, *refs):
        if ours:
            up_ref, act_ref = refs[:2]
            refs = refs[2:]
        else:
            up_ref, prod_ref, act_ref, g_ref = refs[:4]
            refs = refs[4:]
        att, held, tok, skp, ow, sems = refs
        j = pl.program_id(0)

        def copies(n):
            put = pl.ds(n * WIDE, WIDE)
            take = pl.ds(pl.multiple_of(side(s_ref) * half + n * WIDE, 128), WIDE)
            return [
                pltpu.make_async_copy(ow_hbm.at[:, :, take], ow.at[n], sems.at[3 * n]),
                pltpu.make_async_copy(tok_hbm.at[:, take], tok.at[n], sems.at[3 * n + 1]),
                pltpu.make_async_copy(skip_hbm.at[:, take], skp.at[n], sems.at[3 * n + 2]),
            ]

        turned_copy = None if ours else pltpu.make_async_copy(g_hbm, g_ref, sems.at[3 * steps])

        @pl.when(j == 0)
        def _():
            for n in range(steps):
                for copy in copies(n):
                    copy.start()
            if not ours:
                turned_copy.start()
            mixed = [b[:, :DV].astype(F32) for b in (b0, b1, b2, b3)]
            squares = sum(jnp.sum(m * m, axis=1, keepdims=True) for m in mixed)
            scale = lax.rsqrt(squares * (1.0 / (H * DV)) + 1e-05)
            for d in range(4):
                att[d] = (mixed[d] * scale).astype(BF)

        def chunk(n):
            for copy in copies(n):
                copy.wait()
            cut = pl.ds(n * WIDE, WIDE)
            low, high = low_ref[...].astype(F32), high_ref[...].astype(F32)
            grown = jnp.zeros((rows + TAIL, WIDE), F32)
            for d in range(4):
                grown += jnp.dot(att[d], ow[n, (s_ref[HEAD_AT] + d) % 4], preferred_element_type=F32)
            hidden = (tok[n].astype(F32) + grown[:rows]).astype(BF)
            low_hid = (low[:1] + grown[rows : rows + 1]).astype(BF).astype(F32)
            high_hid = (high[:1] + grown[rows + 1 : rows + 2]).astype(BF).astype(F32)
            twice = lax.broadcasted_iota(jnp.int32, (fine, rows), 0) // 2
            twice = jnp.where(twice == lax.broadcasted_iota(jnp.int32, (fine, rows), 1), 1.0, 0.0).astype(BF)
            up = jnp.dot(twice, hidden, preferred_element_type=F32) + skp[n].astype(F32)
            held[8 : 8 + fine, :] = up.astype(BF).astype(F32)
            row = lax.broadcasted_iota(jnp.int32, (8, WIDE), 0)
            edge = (low_hid + jnp.where(row == 6, low[1:2], low[2:3])).astype(BF).astype(F32)
            held[:8, :] = jnp.where((row >= 6) & (s_ref[HAS_LOW] > 0), edge, 0.0)
            edge = (high_hid + jnp.where(row == 0, high[1:2], high[2:3])).astype(BF).astype(F32)
            held[8 + fine :, :] = jnp.where((row < 2) & (s_ref[HAS_HIGH] > 0), edge, 0.0)
            up_ref[...] = held[...].astype(BF)
            pre = (
                dw_ref[0:1, :] * held[7 : 7 + fine, :]
                + dw_ref[1:2, :] * held[8 : 8 + fine, :]
                + dw_ref[2:3, :] * held[9 : 9 + fine, :]
            )
            bend, _, _ = gelu_parts(pre)
            value = (pre * (0.5 * (1.0 + bend))).astype(BF)
            if ours:
                act_ref[...] = value
            else:
                act_ref[:, n * WIDE : (n + 1) * WIDE] = value

        for n in range(steps):
            pl.when(j == n)(lambda n=n: chunk(n))

        if not ours:

            @pl.when(j == steps)
            def _():
                turned_copy.wait()

            @pl.when(j >= steps)
            def _():
                at = pl.multiple_of((s_ref[THEIR_FIRST] + j - steps) % 4 * quarter, 16)
                prod_ref[0] = jnp.dot(
                    g_ref[pl.ds(at, quarter), :], act_ref[...], preferred_element_type=F32
                ).astype(BF)

    def cols(count, full):
        def place(j, s_ref):
            n = jnp.minimum(j, steps - 1)
            return 0, (side(s_ref) * steps + n if full else n)

        return pl.BlockSpec((count, WIDE), place)

    def flat(count, width):
        return pl.BlockSpec((count, width), lambda j, s_ref: (0, 0))

    outs = [jax.ShapeDtypeStruct((fine + 16, half), BF)]
    out_specs = [cols(fine + 16, False)]
    scratch = []
    if ours:
        outs += [jax.ShapeDtypeStruct((fine, half), BF)]
        out_specs += [cols(fine, False)]
    else:
        outs += [jax.ShapeDtypeStruct((4, quarter, half), BF)]
        out_specs += [
            pl.BlockSpec((1, quarter, half), lambda j, s_ref: (jnp.maximum(j - steps, 0), 0, 0))
        ]
        scratch += [pltpu.VMEM((fine, half), BF), pltpu.VMEM((columns, fine), BF)]
    scratch += [
        pltpu.VMEM((4, rows + TAIL, DV), BF),
        pltpu.VMEM((fine + 16, WIDE), F32),
        pltpu.VMEM((steps, rows, WIDE), BF),
        pltpu.VMEM((steps, fine, WIDE), BF),
        pltpu.VMEM((steps, H, DV, WIDE), BF),
        pltpu.SemaphoreType.DMA((3 * steps + 1,)),
    ]
    return pl.pallas_call(
        kernel,
        out_shape=outs,
        grid_spec=pltpu.PrefetchScalarGridSpec(
            num_scalar_prefetch=1,
            grid=(steps if ours else steps + 4,),
            in_specs=[flat(rows + TAIL, 256)] * 4
            + [cols(TAIL, True), cols(TAIL, True), cols(3, True)]
            + [ANY] * 4,
            out_specs=out_specs,
            scratch_shapes=scratch,
        ),
        compiler_params=params(48),
        cost_estimate=pl.CostEstimate(
            flops=2 * fine * columns * columns, bytes_accessed=9 << 20, transcendentals=fine * half
        ),
        name="forward",
    )(scalars, *back, before, after, depth_weight, tokens, skipped, out_heads, turned)


def backward(scalars, ours, up, upstream, before, after, point_weight, depth_weight, behind, whole=None):
    fine, columns = upstream.shape
    half = columns // 2
    steps = half // WIDE

    def side(s_ref):
        return s_ref[CORE] if ours else 1 - s_ref[CORE]

    def kernel(s_ref, up_ref, g_ref, low_ref, high_ref, pw_ref, dw_ref, *refs):
        gs_ref, gd_ref, held, grad, ends = refs[-5:]
        dims = (((1,), (1,)), ((), ()))

        @pl.when(pl.program_id(0) == 0)
        def _():
            row = lax.broadcasted_iota(jnp.int32, (TAIL, columns), 0)
            low, high = low_ref[...].astype(F32), high_ref[...].astype(F32)
            ends[...] = jnp.where(row == 7, low[3:4], jnp.where(row == 8, high[3:4], 0.0)).astype(BF)

        upper = lax.dot_general(g_ref[...], pw_ref[...], dims, preferred_element_type=F32)
        outer = lax.dot_general(ends[...], pw_ref[...], dims, preferred_element_type=F32)
        held[:8, :] = jnp.zeros((8, WIDE), F32)
        held[8 : fine + 24, :] = up_ref[...].astype(F32)
        held[fine + 24 :, :] = jnp.zeros((8, WIDE), F32)

        def grad_of(start, count, coming):
            pre = (
                dw_ref[0:1, :] * held[start - 1 : start - 1 + count, :]
                + dw_ref[1:2, :] * held[start : start + count, :]
                + dw_ref[2:3, :] * held[start + 1 : start + 1 + count, :]
            )
            bend, square, slope = gelu_parts(pre)
            rate = 0.5 * (1.0 + bend) + (0.5 * slope) * pre * (1.0 - bend * bend) * (
                1.0 + (3 * 0.044715) * square
            )
            return (coming * rate).astype(BF).astype(F32)

        grad[:8, :] = grad_of(8, 8, outer[:8])
        mid = grad_of(16, fine, upper)
        grad[8 : 8 + fine, :] = mid
        grad[8 + fine :, :] = grad_of(16 + fine, 8, outer[8:])
        gs_ref[...] = (
            dw_ref[0:1, :] * grad[9 : 9 + fine, :]
            + dw_ref[1:2, :] * mid
            + dw_ref[2:3, :] * grad[7 : 7 + fine, :]
        ).astype(BF)
        for t in range(3):
            gd_ref[t : t + 1, :] = jnp.sum(held[15 + t : 15 + t + fine, :] * mid, axis=0, keepdims=True)

    def cols(count, full):
        return pl.BlockSpec((count, WIDE), lambda j, s_ref: (0, (side(s_ref) * steps if full else 0) + j))

    def flat(count):
        return pl.BlockSpec((count, columns), lambda j, s_ref: (0, 0))

    ins = [up, upstream, before, after, point_weight, depth_weight, behind]
    if whole is not None:
        ins.append(whole)
    return pl.pallas_call(
        kernel,
        out_shape=[jax.ShapeDtypeStruct((fine, columns), BF), jax.ShapeDtypeStruct((3, half), F32)],
        grid_spec=pltpu.PrefetchScalarGridSpec(
            num_scalar_prefetch=1,
            grid=(steps,),
            in_specs=[
                cols(fine + 16, False),
                flat(fine),
                flat(TAIL),
                flat(TAIL),
                pl.BlockSpec((WIDE, columns), lambda j, s_ref: (side(s_ref) * steps + j, 0)),
                cols(3, True),
            ]
            + [ANY] * (len(ins) - 6),
            out_specs=[cols(fine, True), cols(3, False)],
            scratch_shapes=[
                pltpu.VMEM((fine + 32, WIDE), F32),
                pltpu.VMEM((fine + 16, WIDE), F32),
                pltpu.VMEM((TAIL, columns), BF),
            ],
        ),
        input_output_aliases={} if whole is None else {8: 0},
        compiler_params=params(48),
        cost_estimate=pl.CostEstimate(
            flops=fine * columns * columns, bytes_accessed=6 << 20, transcendentals=fine * half
        ),
        name="backward",
    )(scalars, *ins)


def product(scalars, act, turned, steps, arrived):
    half, quarter = act.shape[1], turned.shape[0] // 4

    def kernel(s_ref, a_ref, g_ref, arrived_ref, *outs):
        for out, d in zip(outs, steps):
            at = pl.multiple_of((s_ref[FIRST_AT] + d) % 4 * quarter, 16)
            block = jnp.dot(g_ref[pl.ds(at, quarter), :], a_ref[...], preferred_element_type=F32)
            out[...] = (block + arrived_ref[d].astype(F32)).astype(BF)

    return pl.pallas_call(
        kernel,
        out_shape=[jax.ShapeDtypeStruct((quarter, half), BF)] * len(steps),
        in_specs=[SMEM] + [VMEM] * 3,
        out_specs=[VMEM] * len(steps),
        compiler_params=params(14),
        cost_estimate=pl.CostEstimate(
            flops=2 * act.shape[0] * half * quarter * len(steps), bytes_accessed=6 << 20, transcendentals=0
        ),
        name="product",
    )(scalars, act, turned, arrived)


def split_rows(at, got, rider):
    rows, columns = got[0].shape
    slim = rows // 4

    def kernel(at_ref, *refs):
        ins, rider_ref, outs = refs[:4], refs[4], refs[5:]
        for d in range(4):
            take = pl.ds(pl.multiple_of((at_ref[SECOND_AT] + d) % 4 * slim, 16), slim)
            outs[d][:slim, :] = total_of([r[take, :] for r in ins]).astype(BF)
            outs[d][slim:, :] = rider_ref[...]

    return pl.pallas_call(
        kernel,
        out_shape=[jax.ShapeDtypeStruct((slim + TAIL, columns), BF)] * 4,
        in_specs=[SMEM] + [VMEM] * 5,
        out_specs=[VMEM] * 4,
        compiler_params=params(10),
        name="split_rows",
    )(at, *got, rider)


def join_rows(at, got, rider):
    slim, columns = got[0].shape

    def kernel(at_ref, *refs):
        ins, rider_ref, out, held = refs[:4], refs[4], refs[5], refs[6]
        for d in range(4):
            put = pl.ds(pl.multiple_of((at_ref[SECOND_AT] + 4 - d) % 4 * slim, 16), slim)
            held[put, :] = ins[d][...]
        out[:columns, :] = held[...].T
        last = rider_ref[...].astype(F32)[:8]
        out[columns:, :] = jnp.concatenate([last[:, : 4 * slim], last[:, 4 * slim :]], axis=0).astype(BF)

    return pl.pallas_call(
        kernel,
        out_shape=jax.ShapeDtypeStruct((columns + TAIL, 4 * slim), BF),
        in_specs=[SMEM] + [VMEM] * 5,
        out_specs=VMEM,
        scratch_shapes=[pltpu.VMEM((4 * slim, columns), BF)],
        compiler_params=params(10),
        name="join_rows",
    )(at, *got, rider)


def lay_out(scalars, step, own, other, whole=None):
    half, quarter = own.shape[0] - TAIL, own.shape[1]

    def kernel(s_ref, own_ref, other_ref, *refs):
        out = refs[-1]
        for n, ref in enumerate((own_ref, other_ref)):

            @pl.when(pl.program_id(0) == n)
            def _():
                out[...] = ref[:half, :]

    def place(n, s_ref):
        side = jnp.where(n == 0, s_ref[CORE], 1 - s_ref[CORE])
        at = jnp.where(n == 0, s_ref[FIRST_AT], s_ref[THEIR_FIRST])
        return side, (at + 4 - step) % 4

    block = pl.BlockSpec((half + TAIL, quarter), lambda n, s_ref: (0, 0))
    extra = [] if whole is None else [whole]
    return pl.pallas_call(
        kernel,
        out_shape=jax.ShapeDtypeStruct((2 * half, 4 * quarter), BF),
        grid_spec=pltpu.PrefetchScalarGridSpec(
            num_scalar_prefetch=1,
            grid=(2,),
            in_specs=[block] * 2 + [ANY] * len(extra),
            out_specs=pl.BlockSpec((half, quarter), place),
        ),
        input_output_aliases={} if whole is None else {3: 0},
        compiler_params=params(12),
        name="lay_out",
    )(scalars, own, other, *extra)


def local(
    trunk,
    skip,
    valid_bins,
    query_weight,
    key_weight,
    value_weight,
    out_weight,
    depth_weight,
    point_weight,
    cotangent,
):
    tokens, skipped, upstream = trunk[0], skip[0], cotangent[0]
    rows, columns = tokens.shape
    fine = skipped.shape[0]
    ix, ic, iz, iy = (lax.axis_index(a) for a in AXES)
    index = {"x": ix, "z": iz, "y": iy}
    place = iz * 4 + iy

    def at(axes, swap=False):
        a, b = axes[::-1] if swap else axes
        return jnp.where(ic == 0, index[a], index[b])

    def ints(*values):
        return jnp.stack([jnp.asarray(v, jnp.int32) for v in values])

    head_at, row_at = at(HEAD_RING), at(ROW_RING)
    values = [ic, head_at, place > 0, place < 15, at(SUM_RINGS[0]), at(SUM_RINGS[0], True), at(SUM_RINGS[1]), 0, ic]
    start_at = [jnp.where(ic == 0, (iy - d) % 4, iy) for d in range(4)]
    values += [v == 0 for v in start_at] + [v == 3 for v in start_at]
    for far_by in (0, 1, 3, 2):
        for d in range(4):
            h, r = (head_at - d) % 4, (row_at - far_by) % 4
            values.append(jnp.where(ic == 0, r * 4 + h, h * 4 + r) * rows)
    scalars = ints(*values, valid_bins[0])

    blocks = project(scalars, tokens, query_weight, key_weight, value_weight)
    q = exchange(blocks, HEAD_RING)
    own = stack_rows(q)
    far = {d: lax.ppermute(own, AXES, turn(ROW_RING, d)) for d in (1, 3, 2)}
    state, mark = attend(scalars, 0, q, [own], None)

    down, up = edges(mark, tokens, skipped, upstream)
    before = lax.ppermute(down, ("z", "y"), [(i, i + 1) for i in range(15)])
    after = lax.ppermute(up, ("z", "y"), [(i + 1, i) for i in range(15)])
    turned = upstream.T

    state, _ = attend(scalars, 1, q, [far[1]], state)
    state, _ = attend(scalars, 2, q, [far[3]], state)
    mixed = attend(scalars, 3, q, [own, far[1], far[3], far[2]], state)
    back = exchange(mixed, HEAD_RING, -1)
    swap = [(0, 1), (1, 0)]
    given = (back, tokens, skipped, out_weight.reshape(H, DV, -1), before, after, depth_weight, turned)
    up_theirs, sent = forward(scalars, False, *given)
    arrived = lax.ppermute(sent, "c", swap)
    up_ours, act = forward(scalars, True, *given)
    piece_2, piece_1 = product(scalars, act, turned, (2, 1), arrived)
    piece_3, piece_0 = product(scalars, act, turned, (3, 0), arrived)
    got = exchange([piece_0, piece_1, piece_2, piece_3], SUM_RINGS[0])

    given = (upstream, before, after, point_weight, depth_weight, piece_0)
    grad_skip, d_theirs = backward(scalars, False, up_theirs, *given)
    d_arrived = lax.ppermute(d_theirs, "c", swap)
    grad_skip, d_mine = backward(scalars, True, up_ours, *given, grad_skip)
    d_sum = d_mine + d_arrived
    half = columns // 2
    rider = jnp.pad(d_sum.astype(BF), ((0, TAIL - 3), (0, 0)))

    slim = columns // 16
    got = exchange(split_rows(scalars, got, rider), SUM_RINGS[1])
    got = exchange([total_of(got).astype(BF)] * 4, SUM_RINGS[2])
    norm_scale = 1.0 / math.sqrt(128 * fine)
    summed = (total_of(got) * norm_scale).astype(BF)
    piece, rider = summed[:slim], summed[slim:]
    joined = join_rows(scalars, exchange([piece] * 4, SUM_RINGS[1]), rider)
    got = exchange([joined] * 4, SUM_RINGS[0])
    other = [lax.ppermute(g, "c", swap) for g in got]
    grad_pointwise = None
    for d in (0, 1, 3, 2):
        grad_pointwise = lay_out(scalars, d, got[d], other[d], grad_pointwise)

    def depth_of(blocks):
        rows = total_of([b[half:] for b in blocks])
        return jnp.concatenate([rows[:3], rows[8:11]], axis=1)

    d_own, d_other = depth_of(got), depth_of(other)
    grad_depth = jnp.concatenate(
        [jnp.where(ic == 0, d_own, d_other), jnp.where(ic == 0, d_other, d_own)], axis=1
    )
    return (grad_pointwise, grad_depth, grad_skip[None])


def solution(mesh):
    fine_mesh = Mesh(mesh.devices.reshape(SIZES), AXES)
    rows = P(("x", "c"), ("z", "y"), None)
    return jax.shard_map(
        local,
        mesh=fine_mesh,
        in_specs=(rows, rows, P(("x", "c")), P(), P(), P(), P(), P(), P(), rows),
        out_specs=(P(), P(), rows),
        check_vma=False,
    )
```

```python
import math

import jax
import jax.numpy as jnp
from jax import lax
from jax.experimental import pallas as pl
from jax.experimental.pallas import tpu as pltpu
from jax.sharding import Mesh, PartitionSpec as P

H = 4
DH = 64
DV = 192
AXES = ("x", "c", "z", "y")
SIZES = (4, 2, 4, 4)
BF = jnp.bfloat16
F32 = jnp.float32
TAIL = 16
VMEM = pl.BlockSpec(memory_space=pltpu.VMEM)
SMEM = pl.BlockSpec(memory_space=pltpu.SMEM)
ANY = pl.BlockSpec(memory_space=pl.ANY)
SUM_RINGS = (("x", "y"), ("y", "z"), ("z", "x"))
HEAD_RING = ("y", "z")
ROW_RING = ("z", "y")


class Spot:
    def __init__(self, s_ref):
        x, core, z, y = (s_ref[n] for n in range(4))
        first = core == 0
        self.core, self.y, self.valid = core, y, s_ref[4]
        self.head_at = jnp.where(first, y, z)
        self.row_at = jnp.where(first, z, y)
        self.first_at = jnp.where(first, x, y)
        self.their_first = jnp.where(first, y, x)
        self.second_at = jnp.where(first, y, z)
        self.place = z * 4 + y

    def base(self, far_by, d):
        h, r = (self.head_at + 4 - d) % 4, (self.row_at + 4 - far_by) % 4
        return jnp.where(self.core == 0, r * 4 + h, h * 4 + r)

    def ring_place(self, d):
        return jnp.where(self.core == 0, (self.y + 4 - d) % 4, self.y)


def params(mib):
    return pltpu.CompilerParams(vmem_limit_bytes=mib << 20)


def turn(axes, step):
    pairs = []
    for x in range(4):
        for c in range(2):
            for z in range(4):
                for y in range(4):
                    at = {"x": x, "z": z, "y": y}
                    to = dict(at)
                    to[axes[c]] = (at[axes[c]] + step) % 4
                    flat = [((p["x"] * 2 + c) * 4 + p["z"]) * 4 + p["y"] for p in (at, to)]
                    pairs.append(tuple(flat))
    return pairs


def exchange(pieces, axes, sign=1):
    got = [pieces[0], None, None, None]
    for d in (2, 1, 3):
        got[d] = lax.ppermute(pieces[d], AXES, turn(axes, sign * d))
    return got


def total_of(got):
    a, b, c, d = (g.astype(F32) for g in got)
    return (a + c) + (b + d)


def project(at, tokens, query_weight, key_weight, value_weight):
    rows, depth = tokens.shape
    cut = depth // 2

    def kernel(at_ref, tok_hbm, wq_hbm, wk_hbm, wv_hbm, *refs):
        outs, (tok_ref, wq_ref, wk_ref, wv_ref, held, sems) = refs[:4], refs[4:]
        low, high = pl.ds(0, cut), pl.ds(cut, depth - cut)
        copies = [
            pltpu.make_async_copy(tok_hbm, tok_ref, sems.at[0]),
            pltpu.make_async_copy(wv_hbm.at[low, :], wv_ref.at[low, :], sems.at[1]),
            pltpu.make_async_copy(wv_hbm.at[high, :], wv_ref.at[high, :], sems.at[2]),
            pltpu.make_async_copy(wk_hbm, wk_ref, sems.at[3]),
            pltpu.make_async_copy(wq_hbm, wq_ref, sems.at[4]),
        ]
        for copy in copies:
            copy.start()
        copies[0].wait()
        tok = tok_ref[...]
        copies[1].wait()
        v = jnp.dot(tok[:, :cut], wv_ref[:cut, :], preferred_element_type=F32)
        copies[2].wait()
        v += jnp.dot(tok[:, cut:], wv_ref[cut:, :], preferred_element_type=F32)
        copies[3].wait()
        k = jnp.dot(tok, wk_ref[...], preferred_element_type=F32)
        copies[4].wait()
        q = jnp.dot(tok, wq_ref[...], preferred_element_type=F32) * (1.0 / math.sqrt(DH))
        zero = jnp.zeros((rows, DH), F32)
        for h in range(H):
            held[h] = jnp.concatenate(
                [
                    v[:, h * DV : (h + 1) * DV],
                    k[:, h * DH : (h + 1) * DH],
                    zero,
                    q[:, h * DH : (h + 1) * DH],
                ],
                axis=1,
            ).astype(BF)
        for d in range(4):
            outs[d][...] = held[(Spot(at_ref).head_at + d) % 4]

    return pl.pallas_call(
        kernel,
        out_shape=[jax.ShapeDtypeStruct((rows, 384), BF)] * 4,
        in_specs=[SMEM] + [ANY] * 4,
        out_specs=[VMEM] * 4,
        scratch_shapes=[
            pltpu.VMEM((rows, depth), BF),
            pltpu.VMEM((depth, H * DH), BF),
            pltpu.VMEM((depth, H * DH), BF),
            pltpu.VMEM((depth, H * DV), BF),
            pltpu.VMEM((4, rows, 384), BF),
            pltpu.SemaphoreType.DMA((5,)),
        ],
        compiler_params=params(53),
        name="project",
    )(at, tokens, query_weight, key_weight, value_weight)


def stack_rows(parts):
    rows = parts[0].shape[0]

    def kernel(*refs):
        ins, out = refs[:4], refs[4]
        row = lax.broadcasted_iota(jnp.int32, (TAIL, 128), 0)
        tail = jnp.zeros((TAIL, 128), F32)
        for d in range(4):
            out[d * rows : (d + 1) * rows, :] = ins[d][:, :256]
            first = ins[d][:TAIL, 256:].astype(F32)[:1]
            final = ins[d][rows - TAIL :, 256:].astype(F32)[TAIL - 1 :]
            tail = jnp.where(row == d, first, tail)
            tail = jnp.where(row == 4 + d, final, tail)
        out[4 * rows :, :128] = jnp.zeros((TAIL, 128), BF)
        out[4 * rows :, 128:] = tail.astype(BF)

    return pl.pallas_call(
        kernel,
        out_shape=jax.ShapeDtypeStruct((4 * rows + TAIL, 256), BF),
        in_specs=[VMEM] * 4,
        out_specs=VMEM,
        compiler_params=params(8),
        name="stack_rows",
    )(*parts)


def attend(scalars, near, q, pairs, state, behind=()):
    rows = q[0].shape[0]
    width = 4 * rows
    first = state is None
    last = len(pairs) == 4
    strip = 32

    def kernel(s_ref, *refs):
        spot = Spot(s_ref)
        score_ref, prob_ref, peak_ref = refs[-3:]
        q_refs, refs = refs[:4], refs[4:]
        pair_refs, refs = refs[: len(pairs)], refs[len(pairs) :]
        if not first:
            old, refs = refs[0], refs[1:]
        refs = refs[len(behind) :]
        lane = lax.broadcasted_iota(jnp.int32, (width, 256), 1)
        place = lax.broadcasted_iota(jnp.int32, (1, rows), 1)

        def masks(n):
            far_by = (0, 1, 3, 2)[n]
            return jnp.concatenate(
                [place + spot.base(far_by, i) * rows < spot.valid for i in range(4)], axis=1
            )

        def values_of(ref):
            return jnp.where(lane == DV, jnp.ones((), BF), ref[:width, :])

        def raw_scores(query, ref):
            return lax.dot_general(
                query, ref[:width, 128:], (((1,), (1,)), ((), ())), preferred_element_type=F32
            )

        def shares(sums):
            return sums / sums[:, DV : DV + 1]

        if last:
            tails = [r[width:, 128:].astype(F32) for r in pair_refs]
            own, low, high = tails[0], tails[1], tails[2]
            row = lax.broadcasted_iota(jnp.int32, (TAIL, 128), 0)
            edge = jnp.zeros((TAIL, 128), F32)
            for d in range(4):
                n, m = (d + 1) % 4, (d + 3) % 4
                at = spot.ring_place(d)
                other = jnp.where(spot.core == 0, own[4 + n : 5 + n], low[4 + d : 5 + d])
                prev = jnp.where(at == 0, low[4 + n : 5 + n], other)
                other = jnp.where(spot.core == 0, own[m : m + 1], high[d : d + 1])
                nxt = jnp.where(at == 3, high[m : m + 1], other)
                edge = jnp.where(row == d, prev, edge)
                edge = jnp.where(row == 4 + d, nxt, edge)
            edge = edge.astype(BF)
            parts = [jnp.where(masks(n), raw_scores(edge, r), -1e30) for n, r in enumerate(pair_refs)]
            peak = jnp.max(parts[0], axis=1, keepdims=True)
            for s in parts[1:]:
                peak = jnp.maximum(peak, jnp.max(s, axis=1, keepdims=True))
            edge_sums = jnp.zeros((TAIL, 256), F32)
            for s, r in zip(parts, pair_refs):
                edge_sums += jnp.dot(jnp.exp(s - peak).astype(BF), values_of(r), preferred_element_type=F32)
            edge_out = shares(edge_sums)
            row = lax.broadcasted_iota(jnp.int32, (TAIL, 256), 0)

        column = lax.broadcasted_iota(jnp.int32, (rows, 256), 1)
        if not last:
            refs[1][...] = jnp.zeros((8, 128), F32)
        pair_ref = pair_refs[-1]
        keep = masks(near)
        values = values_of(pair_ref)
        for i in range(4):
            score_ref[i] = raw_scores(q_refs[i][:, 256:], pair_ref)
        for i in range(4):
            for k in range(0, rows, strip):
                cut = slice(k, k + strip)
                scores = jnp.where(keep, score_ref[i, cut, :], -1e30)
                peak = jnp.max(scores, axis=1, keepdims=True)
                if not first:
                    peak = jnp.maximum(peak, old[i * rows + k : i * rows + k + strip, DV + 1 : DV + 2])
                prob_ref[i, cut, :] = jnp.exp(scores - peak).astype(BF)
                peak_ref[i, cut, :] = jnp.broadcast_to(peak, (strip, 128))
            update = jnp.dot(prob_ref[i], values, preferred_element_type=F32)
            peak = peak_ref[i, :, :1]
            if not first:
                sums = old[i * rows : (i + 1) * rows, :]
                update = update + sums * jnp.exp(sums[:, DV + 1 : DV + 2] - peak)
            if last:
                refs[i][:rows, :] = shares(update).astype(BF)
                ends = jnp.where(row == 0, edge_out[i : i + 1], jnp.zeros((TAIL, 256), F32))
                ends = jnp.where(row == 1, edge_out[4 + i : 5 + i], ends)
                refs[i][rows:, :] = ends.astype(BF)
            else:
                refs[0][i * rows : (i + 1) * rows, :] = jnp.where(column == DV + 1, peak, update)

    ins = [*q, *pairs]
    if not first:
        ins += [state]
    if last:
        outs = [jax.ShapeDtypeStruct((rows + TAIL, 256), BF)] * 4
    else:
        outs = [jax.ShapeDtypeStruct((4 * rows, 256), F32), jax.ShapeDtypeStruct((8, 128), F32)]
    return pl.pallas_call(
        kernel,
        out_shape=outs,
        in_specs=[SMEM] + [VMEM] * len(ins) + [ANY] * len(behind),
        out_specs=[VMEM] * len(outs),
        scratch_shapes=[
            pltpu.VMEM((4, rows, width), F32),
            pltpu.VMEM((4, rows, width), BF),
            pltpu.VMEM((4, rows, 128), F32),
        ],
        compiler_params=params(24),
        cost_estimate=pl.CostEstimate(
            flops=4 * 2 * rows * width * 512, bytes_accessed=4 << 20, transcendentals=4 * rows * width
        ),
        name="attend",
    )(scalars, *ins, *behind)


def edges(mark, trunk, skip, cotangent):
    columns = trunk.shape[1]

    def kernel(mark_ref, t_ref, s_ref, c_ref, down, up, buffer, sems):
        copies = []
        for n, ref in enumerate((t_ref, s_ref, c_ref)):
            for end in range(2):
                start = end * (ref.shape[0] - TAIL)
                copies.append(
                    pltpu.make_async_copy(
                        ref.at[pl.ds(start, TAIL), :], buffer.at[2 * n + end], sems.at[2 * n + end]
                    )
                )
        for copy in copies:
            copy.start()
        for copy in copies:
            copy.wait()
        t_first, t_last, s_first, s_last, c_first, c_last = (buffer[n].astype(F32) for n in range(6))
        row = lax.broadcasted_iota(jnp.int32, (TAIL, columns), 0)

        def four(a, b, c, d):
            rest = jnp.where(row == 2, c, jnp.where(row == 3, d, 0.0))
            return jnp.where(row == 0, a, jnp.where(row == 1, b, rest)).astype(BF)

        up[...] = four(t_first[:1], s_first[:1], s_first[1:2], c_first[:1])
        e = TAIL - 1
        down[...] = four(t_last[e:], s_last[e - 1 : e], s_last[e:], c_last[e:])

    return pl.pallas_call(
        kernel,
        out_shape=[jax.ShapeDtypeStruct((TAIL, columns), BF)] * 2,
        in_specs=[VMEM, ANY, ANY, ANY],
        out_specs=[VMEM] * 2,
        scratch_shapes=[pltpu.VMEM((6, TAIL, columns), BF), pltpu.SemaphoreType.DMA((6,))],
        compiler_params=params(53),
        name="edges",
    )(mark, trunk, skip, cotangent)


def gelu_parts(pre):
    slope = math.sqrt(2.0 / math.pi)
    square = pre * pre
    bend = jnp.tanh(slope * (pre + 0.044715 * (square * pre)))
    return bend, square, slope


WIDE = 256
STRIP = 32


def forward(scalars, ours, back, tokens, skipped, out_heads, before, after, depth_weight, turned):
    rows, columns = tokens.shape
    fine = 2 * rows
    half = columns // 2
    steps = half // WIDE
    quarter = columns // 4

    def side(s_ref):
        return s_ref[1] if ours else 1 - s_ref[1]

    def kernel(s_ref, b0, b1, b2, b3, low_ref, high_ref, dw_ref, tok_hbm, skip_hbm, ow_hbm, g_hbm, *refs):
        if ours:
            up_ref, act_ref = refs[:2]
            refs = refs[2:]
        else:
            up_ref, prod_ref, act_ref, g_ref = refs[:4]
            refs = refs[4:]
        att, held, tok, skp, ow, sems = refs
        j = pl.program_id(0)

        def copies(n):
            take = pl.ds(pl.multiple_of(side(s_ref) * half + n * WIDE, 128), WIDE)
            return [
                pltpu.make_async_copy(ow_hbm.at[:, :, take], ow.at[n], sems.at[3 * n]),
                pltpu.make_async_copy(tok_hbm.at[:, take], tok.at[n], sems.at[3 * n + 1]),
                pltpu.make_async_copy(skip_hbm.at[:, take], skp.at[n], sems.at[3 * n + 2]),
            ]

        turned_copy = None if ours else pltpu.make_async_copy(g_hbm, g_ref, sems.at[3 * steps])

        @pl.when(j == 0)
        def _():
            for n in range(steps):
                for copy in copies(n):
                    copy.start()
            if not ours:
                turned_copy.start()
            mixed = [b[:, :DV].astype(F32) for b in (b0, b1, b2, b3)]
            squares = sum(jnp.sum(m * m, axis=1, keepdims=True) for m in mixed)
            scale = lax.rsqrt(squares * (1.0 / (H * DV)) + 1e-05)
            for d in range(4):
                att[d] = (mixed[d] * scale).astype(BF)

        @pl.when(j < steps)
        def _():
            spot = Spot(s_ref)
            n = jnp.minimum(j, steps - 1)
            for copy in copies(n):
                copy.wait()
            low, high = low_ref[...].astype(F32), high_ref[...].astype(F32)
            grown = jnp.zeros((rows + TAIL, WIDE), F32)
            for d in range(4):
                grown += jnp.dot(att[d], ow[n, (spot.head_at + d) % 4], preferred_element_type=F32)
            hidden = (tok[n].astype(F32) + grown[:rows]).astype(BF)
            low_hid = (low[:1] + grown[rows : rows + 1]).astype(BF).astype(F32)
            high_hid = (high[:1] + grown[rows + 1 : rows + 2]).astype(BF).astype(F32)
            twice = lax.broadcasted_iota(jnp.int32, (fine, rows), 0) // 2
            twice = jnp.where(twice == lax.broadcasted_iota(jnp.int32, (fine, rows), 1), 1.0, 0.0).astype(BF)
            doubled = jnp.dot(twice, hidden, preferred_element_type=F32)
            row = lax.broadcasted_iota(jnp.int32, (TAIL, WIDE), 0)
            edge = (low_hid + jnp.where(row == 14, low[1:2], low[2:3])).astype(BF).astype(F32)
            edge = jnp.where((row >= 14) & (spot.place > 0), edge, 0.0)
            held[:TAIL, :] = edge
            up_ref[:TAIL, :] = edge.astype(BF)
            edge = (high_hid + jnp.where(row == 0, high[1:2], high[2:3])).astype(BF).astype(F32)
            edge = jnp.where((row < 2) & (spot.place < 15), edge, 0.0)
            held[TAIL + fine :, :] = edge
            up_ref[TAIL + fine :, :] = edge.astype(BF)
            for k in range(0, fine, STRIP):
                up = (doubled[k : k + STRIP] + skp[n, k : k + STRIP, :].astype(F32)).astype(BF)
                up_ref[TAIL + k : TAIL + k + STRIP, :] = up
                held[TAIL + k : TAIL + k + STRIP, :] = up.astype(F32)
            w = [dw_ref[t : t + 1, :] for t in range(3)]
            cut = pl.ds(0 if ours else pl.multiple_of(n * WIDE, 128), WIDE)
            for k in range(0, fine, STRIP):
                near = held[8 + k : 24 + k + STRIP, :]
                pre = w[0] * near[7 : 7 + STRIP] + w[1] * near[8 : 8 + STRIP] + w[2] * near[9 : 9 + STRIP]
                bend, _, _ = gelu_parts(pre)
                act_ref[k : k + STRIP, cut] = (pre * (0.5 + 0.5 * bend)).astype(BF)

        if not ours:

            @pl.when(j == steps)
            def _():
                turned_copy.wait()

            @pl.when(j >= steps)
            def _():
                at = pl.multiple_of((Spot(s_ref).their_first + j - steps) % 4 * quarter, 16)
                prod_ref[0] = jnp.dot(
                    g_ref[pl.ds(at, quarter), :], act_ref[...], preferred_element_type=F32
                ).astype(BF)

    def cols(count, full):
        def place(j, s_ref):
            n = jnp.minimum(j, steps - 1)
            return 0, (side(s_ref) * steps + n if full else n)

        return pl.BlockSpec((count, WIDE), place)

    def flat(count, width):
        return pl.BlockSpec((count, width), lambda j, s_ref: (0, 0))

    outs = [jax.ShapeDtypeStruct((fine + 2 * TAIL, half), BF)]
    out_specs = [cols(fine + 2 * TAIL, False)]
    scratch = []
    if ours:
        outs += [jax.ShapeDtypeStruct((fine, half), BF)]
        out_specs += [cols(fine, False)]
    else:
        outs += [jax.ShapeDtypeStruct((4, quarter, half), BF)]
        out_specs += [
            pl.BlockSpec((1, quarter, half), lambda j, s_ref: (jnp.maximum(j - steps, 0), 0, 0))
        ]
        scratch += [pltpu.VMEM((fine, half), BF), pltpu.VMEM((columns, fine), BF)]
    scratch += [
        pltpu.VMEM((4, rows + TAIL, DV), BF),
        pltpu.VMEM((fine + 2 * TAIL, WIDE), F32),
        pltpu.VMEM((steps, rows, WIDE), BF),
        pltpu.VMEM((steps, fine, WIDE), BF),
        pltpu.VMEM((steps, H, DV, WIDE), BF),
        pltpu.SemaphoreType.DMA((3 * steps + 1,)),
    ]
    return pl.pallas_call(
        kernel,
        out_shape=outs,
        grid_spec=pltpu.PrefetchScalarGridSpec(
            num_scalar_prefetch=1,
            grid=(steps if ours else steps + 4,),
            in_specs=[flat(rows + TAIL, 256)] * 4
            + [cols(TAIL, True), cols(TAIL, True), cols(3, True)]
            + [ANY] * 4,
            out_specs=out_specs,
            scratch_shapes=scratch,
        ),
        compiler_params=params(53),
        cost_estimate=pl.CostEstimate(
            flops=2 * fine * columns * columns, bytes_accessed=9 << 20, transcendentals=fine * half
        ),
        name="forward",
    )(scalars, *back, before, after, depth_weight, tokens, skipped, out_heads, turned)


def backward(scalars, ours, up, upstream, before, after, point_weight, depth_weight, behind, whole=None):
    fine, columns = upstream.shape
    half = columns // 2
    steps = half // WIDE

    def side(s_ref):
        return s_ref[1] if ours else 1 - s_ref[1]

    def kernel(s_ref, up_ref, g_ref, low_ref, high_ref, pw_ref, dw_ref, *refs):
        gs_ref, gd_ref, grad, upper, ends = refs[-5:]
        dims = (((1,), (1,)), ((), ()))

        @pl.when(pl.program_id(0) == 0)
        def _():
            row = lax.broadcasted_iota(jnp.int32, (TAIL, columns), 0)
            low, high = low_ref[...].astype(F32), high_ref[...].astype(F32)
            ends[...] = jnp.where(row == 7, low[3:4], jnp.where(row == 8, high[3:4], 0.0)).astype(BF)

        upper[...] = lax.dot_general(g_ref[...], pw_ref[...], dims, preferred_element_type=F32)
        outer = lax.dot_general(ends[...], pw_ref[...], dims, preferred_element_type=F32)
        w = [dw_ref[t : t + 1, :] for t in range(3)]

        def grad_of(near, start, count, coming):
            taps = [near[start - 1 + t : start - 1 + t + count] for t in range(3)]
            pre = w[0] * taps[0] + w[1] * taps[1] + w[2] * taps[2]
            bend, square, slope = gelu_parts(pre)
            rate = 0.5 + 0.5 * bend + (pre * (1.0 - bend * bend)) * (
                0.5 * slope + (1.5 * slope * 0.044715) * square
            )
            return taps, (coming * rate).astype(BF).astype(F32)

        _, grad[8:16, :] = grad_of(up_ref[:32, :].astype(F32), 8, 8, outer[:8])
        _, grad[16 + fine : 24 + fine, :] = grad_of(up_ref[fine:, :].astype(F32), 16, 8, outer[8:])
        sums = [jnp.zeros((8, WIDE), F32)] * 3
        for k in range(0, fine, STRIP):
            near = up_ref[k : k + STRIP + 2 * TAIL, :].astype(F32)
            taps, mid = grad_of(near, TAIL, STRIP, upper[k : k + STRIP, :])
            grad[16 + k : 16 + k + STRIP, :] = mid
            for t in range(3):
                term = taps[t] * mid
                for r in range(0, STRIP, 8):
                    sums[t] = sums[t] + term[r : r + 8]
        for t in range(3):
            gd_ref[t : t + 1, :] = jnp.sum(sums[t], axis=0, keepdims=True)
        for k in range(0, fine, STRIP):
            near = grad[8 + k : 24 + k + STRIP, :]
            gs_ref[k : k + STRIP, :] = (
                w[0] * near[9 : 9 + STRIP] + w[1] * near[8 : 8 + STRIP] + w[2] * near[7 : 7 + STRIP]
            ).astype(BF)

    def cols(count, full):
        return pl.BlockSpec((count, WIDE), lambda j, s_ref: (0, (side(s_ref) * steps if full else 0) + j))

    def flat(count):
        return pl.BlockSpec((count, columns), lambda j, s_ref: (0, 0))

    ins = [up, upstream, before, after, point_weight, depth_weight, behind]
    if whole is not None:
        ins.append(whole)
    return pl.pallas_call(
        kernel,
        out_shape=[jax.ShapeDtypeStruct((fine, columns), BF), jax.ShapeDtypeStruct((3, half), F32)],
        grid_spec=pltpu.PrefetchScalarGridSpec(
            num_scalar_prefetch=1,
            grid=(steps,),
            in_specs=[
                cols(fine + 2 * TAIL, False),
                flat(fine),
                flat(TAIL),
                flat(TAIL),
                pl.BlockSpec((WIDE, columns), lambda j, s_ref: (side(s_ref) * steps + j, 0)),
                cols(3, True),
            ]
            + [ANY] * (len(ins) - 6),
            out_specs=[cols(fine, True), cols(3, False)],
            scratch_shapes=[
                pltpu.VMEM((fine + 2 * TAIL, WIDE), F32),
                pltpu.VMEM((fine, WIDE), F32),
                pltpu.VMEM((TAIL, columns), BF),
            ],
        ),
        input_output_aliases={} if whole is None else {8: 0},
        compiler_params=params(48),
        cost_estimate=pl.CostEstimate(
            flops=fine * columns * columns, bytes_accessed=6 << 20, transcendentals=fine * half
        ),
        name="backward",
    )(scalars, *ins)


def product(scalars, act, turned, steps, arrived):
    half, quarter = act.shape[1], turned.shape[0] // 4

    def kernel(s_ref, a_ref, g_ref, arrived_ref, *outs):
        for out, d in zip(outs, steps):
            at = pl.multiple_of((Spot(s_ref).first_at + d) % 4 * quarter, 16)
            block = jnp.dot(g_ref[pl.ds(at, quarter), :], a_ref[...], preferred_element_type=F32)
            out[...] = (block + arrived_ref[d].astype(F32)).astype(BF)

    return pl.pallas_call(
        kernel,
        out_shape=[jax.ShapeDtypeStruct((quarter, half), BF)] * len(steps),
        in_specs=[SMEM] + [VMEM] * 3,
        out_specs=[VMEM] * len(steps),
        compiler_params=params(14),
        cost_estimate=pl.CostEstimate(
            flops=2 * act.shape[0] * half * quarter * len(steps), bytes_accessed=6 << 20, transcendentals=0
        ),
        name="product",
    )(scalars, act, turned, arrived)


def split_rows(at, got, rider):
    rows, columns = got[0].shape
    slim = rows // 4

    def kernel(at_ref, *refs):
        ins, rider_ref, outs = refs[:4], refs[4], refs[5:]
        for d in range(4):
            take = pl.ds(pl.multiple_of((Spot(at_ref).second_at + d) % 4 * slim, 16), slim)
            outs[d][:slim, :] = total_of([r[take, :] for r in ins]).astype(BF)
            outs[d][slim:, :] = rider_ref[...]

    return pl.pallas_call(
        kernel,
        out_shape=[jax.ShapeDtypeStruct((slim + TAIL, columns), BF)] * 4,
        in_specs=[SMEM] + [VMEM] * 5,
        out_specs=[VMEM] * 4,
        compiler_params=params(10),
        name="split_rows",
    )(at, *got, rider)


def join_rows(at, got, rider):
    slim, columns = got[0].shape

    def kernel(at_ref, *refs):
        ins, rider_ref, out, held = refs[:4], refs[4], refs[5], refs[6]
        for d in range(4):
            put = pl.ds(pl.multiple_of((Spot(at_ref).second_at + 4 - d) % 4 * slim, 16), slim)
            held[put, :] = ins[d][...]
        out[:columns, :] = held[...].T
        last = rider_ref[...].astype(F32)[:8]
        out[columns:, :] = jnp.concatenate([last[:, : 4 * slim], last[:, 4 * slim :]], axis=0).astype(BF)

    return pl.pallas_call(
        kernel,
        out_shape=jax.ShapeDtypeStruct((columns + TAIL, 4 * slim), BF),
        in_specs=[SMEM] + [VMEM] * 5,
        out_specs=VMEM,
        scratch_shapes=[pltpu.VMEM((4 * slim, columns), BF)],
        compiler_params=params(10),
        name="join_rows",
    )(at, *got, rider)


def lay_out(scalars, steps, own, other, whole=None):
    half, quarter = own[0].shape[0] - TAIL, own[0].shape[1]
    count = len(steps)

    def kernel(s_ref, *refs):
        out, sems = refs[-2:]
        spot = Spot(s_ref)
        copies = []
        for n in range(2 * count):
            mine = n < count
            down = (spot.core if mine else 1 - spot.core) * half
            over = ((spot.first_at if mine else spot.their_first) + 4 - steps[n % count]) % 4 * quarter
            copies.append(
                pltpu.make_async_copy(
                    refs[n].at[pl.ds(0, half), :],
                    out.at[pl.ds(pl.multiple_of(down, 16), half), pl.ds(pl.multiple_of(over, 128), quarter)],
                    sems.at[n],
                )
            )
        for copy in copies:
            copy.start()
        for copy in copies:
            copy.wait()

    extra = [] if whole is None else [whole]
    return pl.pallas_call(
        kernel,
        out_shape=jax.ShapeDtypeStruct((2 * half, 4 * quarter), BF),
        in_specs=[SMEM] + [VMEM] * (2 * count) + [ANY] * len(extra),
        out_specs=ANY,
        scratch_shapes=[pltpu.SemaphoreType.DMA((2 * count,))],
        input_output_aliases={} if whole is None else {1 + 2 * count: 0},
        compiler_params=params(8),
        name="lay_out",
    )(scalars, *own, *other, *extra)


def local(
    trunk,
    skip,
    valid_bins,
    query_weight,
    key_weight,
    value_weight,
    out_weight,
    depth_weight,
    point_weight,
    cotangent,
):
    tokens, skipped, upstream = trunk[0], skip[0], cotangent[0]
    rows, columns = tokens.shape
    fine = skipped.shape[0]
    ix, ic, iz, iy = (lax.axis_index(a) for a in AXES)
    scalars = jnp.stack([v.astype(jnp.int32) for v in (ix, ic, iz, iy, valid_bins[0])])
    blocks = project(scalars, tokens, query_weight, key_weight, value_weight)
    q = exchange(blocks, HEAD_RING)
    own = stack_rows(q)
    far = {d: lax.ppermute(own, AXES, turn(ROW_RING, d)) for d in (1, 3, 2)}
    state, mark = attend(scalars, 0, q, [own], None)

    down, up = edges(mark, tokens, skipped, upstream)
    before = lax.ppermute(down, ("z", "y"), [(i, i + 1) for i in range(15)])
    after = lax.ppermute(up, ("z", "y"), [(i + 1, i) for i in range(15)])
    turned = upstream.T

    state, _ = attend(scalars, 1, q, [far[1]], state)
    state, _ = attend(scalars, 2, q, [far[3]], state, (before, after))
    mixed = attend(scalars, 3, q, [own, far[1], far[3], far[2]], state)
    back = exchange(mixed, HEAD_RING, -1)
    swap = [(0, 1), (1, 0)]
    given = (back, tokens, skipped, out_weight.reshape(H, DV, -1), before, after, depth_weight, turned)
    up_theirs, sent = forward(scalars, False, *given)
    arrived = lax.ppermute(sent, "c", swap)
    up_ours, act = forward(scalars, True, *given)
    piece_2, piece_1 = product(scalars, act, turned, (2, 1), arrived)
    piece_3, piece_0 = product(scalars, act, turned, (3, 0), arrived)
    got = exchange([piece_0, piece_1, piece_2, piece_3], SUM_RINGS[0])

    given = (upstream, before, after, point_weight, depth_weight, piece_0)
    grad_skip, d_theirs = backward(scalars, False, up_theirs, *given)
    d_arrived = lax.ppermute(d_theirs, "c", swap)
    grad_skip, d_mine = backward(scalars, True, up_ours, *given, grad_skip)
    d_sum = d_mine + d_arrived
    half = columns // 2
    rider = jnp.pad(d_sum.astype(BF), ((0, TAIL - 3), (0, 0)))

    slim = columns // 16
    got = exchange(split_rows(scalars, got, rider), SUM_RINGS[1])
    got = exchange([total_of(got).astype(BF)] * 4, SUM_RINGS[2])
    norm_scale = 1.0 / math.sqrt(128 * fine)
    summed = (total_of(got) * norm_scale).astype(BF)
    piece, rider = summed[:slim], summed[slim:]
    joined = join_rows(scalars, exchange([piece] * 4, SUM_RINGS[1]), rider)
    got = exchange([joined] * 4, SUM_RINGS[0])
    other = [lax.ppermute(g, "c", swap) for g in got]
    grad_pointwise = lay_out(scalars, (0,), got[:1], other[:1])
    grad_pointwise = lay_out(scalars, (1, 2, 3), got[1:], other[1:], grad_pointwise)

    def depth_of(blocks):
        rows = total_of([b[half:] for b in blocks])
        return jnp.concatenate([rows[:3], rows[8:11]], axis=1)

    d_own, d_other = depth_of(got), depth_of(other)
    grad_depth = jnp.concatenate(
        [jnp.where(ic == 0, d_own, d_other), jnp.where(ic == 0, d_other, d_own)], axis=1
    )
    return (grad_pointwise, grad_depth, grad_skip[None])


def solution(mesh):
    fine_mesh = Mesh(mesh.devices.reshape(SIZES), AXES)
    rows = P(("x", "c"), ("z", "y"), None)
    return jax.shard_map(
        local,
        mesh=fine_mesh,
        in_specs=(rows, rows, P(("x", "c")), P(), P(), P(), P(), P(), P(), rows),
        out_specs=(P(), P(), rows),
        check_vma=False,
    )
```

```python
import math

import jax
import jax.numpy as jnp
from jax import lax
from jax.experimental import pallas as pl
from jax.experimental.pallas import tpu as pltpu
from jax.sharding import Mesh, PartitionSpec as P

H = 4
DH = 64
DV = 192
AXES = ("x", "c", "z", "y")
SIZES = (4, 2, 4, 4)
BF = jnp.bfloat16
F32 = jnp.float32
TAIL = 16
VMEM = pl.BlockSpec(memory_space=pltpu.VMEM)
SMEM = pl.BlockSpec(memory_space=pltpu.SMEM)
ANY = pl.BlockSpec(memory_space=pl.ANY)
SUM_RINGS = (("x", "y"), ("y", "z"), ("z", "x"))
HEAD_RING = ("y", "z")
ROW_RING = ("z", "y")


class Spot:
    def __init__(self, s_ref):
        x, core, z, y = (s_ref[n] for n in range(4))
        first = core == 0
        self.core, self.y, self.valid = core, y, s_ref[4]
        self.head_at = jnp.where(first, y, z)
        self.row_at = jnp.where(first, z, y)
        self.first_at = jnp.where(first, x, y)
        self.their_first = jnp.where(first, y, x)
        self.second_at = jnp.where(first, y, z)
        self.place = z * 4 + y

    def base(self, far_by, d):
        h, r = (self.head_at + 4 - d) % 4, (self.row_at + 4 - far_by) % 4
        return jnp.where(self.core == 0, r * 4 + h, h * 4 + r)

    def ring_place(self, d):
        return jnp.where(self.core == 0, (self.y + 4 - d) % 4, self.y)


def params(mib):
    return pltpu.CompilerParams(vmem_limit_bytes=mib << 20)


def turn(axes, step):
    pairs = []
    for x in range(4):
        for c in range(2):
            for z in range(4):
                for y in range(4):
                    at = {"x": x, "z": z, "y": y}
                    to = dict(at)
                    to[axes[c]] = (at[axes[c]] + step) % 4
                    flat = [((p["x"] * 2 + c) * 4 + p["z"]) * 4 + p["y"] for p in (at, to)]
                    pairs.append(tuple(flat))
    return pairs


def exchange(pieces, axes, sign=1):
    got = [pieces[0], None, None, None]
    for d in (2, 1, 3):
        got[d] = lax.ppermute(pieces[d], AXES, turn(axes, sign * d))
    return got


def total_of(got):
    a, b, c, d = (g.astype(F32) for g in got)
    return (a + c) + (b + d)


def project(at, tokens, query_weight, key_weight, value_weight):
    rows, depth = tokens.shape
    cut = depth // 2

    def kernel(at_ref, tok_hbm, wq_hbm, wk_hbm, wv_hbm, *refs):
        outs, (tok_ref, wq_ref, wk_ref, wv_ref, held, sems) = refs[:4], refs[4:]
        low, high = pl.ds(0, cut), pl.ds(cut, depth - cut)
        copies = [
            pltpu.make_async_copy(tok_hbm, tok_ref, sems.at[0]),
            pltpu.make_async_copy(wv_hbm.at[low, :], wv_ref.at[low, :], sems.at[1]),
            pltpu.make_async_copy(wv_hbm.at[high, :], wv_ref.at[high, :], sems.at[2]),
            pltpu.make_async_copy(wk_hbm, wk_ref, sems.at[3]),
            pltpu.make_async_copy(wq_hbm, wq_ref, sems.at[4]),
        ]
        for copy in copies:
            copy.start()
        copies[0].wait()
        tok = tok_ref[...]
        copies[1].wait()
        v = jnp.dot(tok[:, :cut], wv_ref[:cut, :], preferred_element_type=F32)
        copies[2].wait()
        v += jnp.dot(tok[:, cut:], wv_ref[cut:, :], preferred_element_type=F32)
        copies[3].wait()
        k = jnp.dot(tok, wk_ref[...], preferred_element_type=F32)
        copies[4].wait()
        q = jnp.dot(tok, wq_ref[...], preferred_element_type=F32) * (1.0 / math.sqrt(DH))
        zero = jnp.zeros((rows, DH), F32)
        for h in range(H):
            held[h] = jnp.concatenate(
                [
                    v[:, h * DV : (h + 1) * DV],
                    k[:, h * DH : (h + 1) * DH],
                    zero,
                    q[:, h * DH : (h + 1) * DH],
                ],
                axis=1,
            ).astype(BF)
        for d in range(4):
            outs[d][...] = held[(Spot(at_ref).head_at + d) % 4]

    return pl.pallas_call(
        kernel,
        out_shape=[jax.ShapeDtypeStruct((rows, 384), BF)] * 4,
        in_specs=[SMEM] + [ANY] * 4,
        out_specs=[VMEM] * 4,
        scratch_shapes=[
            pltpu.VMEM((rows, depth), BF),
            pltpu.VMEM((depth, H * DH), BF),
            pltpu.VMEM((depth, H * DH), BF),
            pltpu.VMEM((depth, H * DV), BF),
            pltpu.VMEM((4, rows, 384), BF),
            pltpu.SemaphoreType.DMA((5,)),
        ],
        compiler_params=params(53),
        name="project",
    )(at, tokens, query_weight, key_weight, value_weight)


def stack_rows(parts, behind):
    rows = parts[0].shape[0]

    def kernel(*refs):
        ins, out = refs[:4], refs[5]
        row = lax.broadcasted_iota(jnp.int32, (TAIL, 128), 0)
        tail = jnp.zeros((TAIL, 128), F32)
        for d in range(4):
            out[d * rows : (d + 1) * rows, :] = ins[d][:, :256]
            first = ins[d][:TAIL, 256:].astype(F32)[:1]
            final = ins[d][rows - TAIL :, 256:].astype(F32)[TAIL - 1 :]
            tail = jnp.where(row == d, first, tail)
            tail = jnp.where(row == 4 + d, final, tail)
        out[4 * rows :, :128] = jnp.zeros((TAIL, 128), BF)
        out[4 * rows :, 128:] = tail.astype(BF)

    return pl.pallas_call(
        kernel,
        out_shape=jax.ShapeDtypeStruct((4 * rows + TAIL, 256), BF),
        in_specs=[VMEM] * 4 + [ANY],
        out_specs=VMEM,
        compiler_params=params(8),
        name="stack_rows",
    )(*parts, behind)


def attend(scalars, near, q, pairs, state, behind=()):
    rows = q[0].shape[0]
    width = 4 * rows
    first = state is None
    last = len(pairs) == 4
    strip = 32

    def kernel(s_ref, *refs):
        spot = Spot(s_ref)
        score_ref, prob_ref, peak_ref = refs[-3:]
        q_refs, refs = refs[:4], refs[4:]
        pair_refs, refs = refs[: len(pairs)], refs[len(pairs) :]
        if not first:
            old, old_peak, refs = refs[0], refs[1], refs[2:]
        refs = refs[len(behind) :]
        lane = lax.broadcasted_iota(jnp.int32, (width, 256), 1)
        place = lax.broadcasted_iota(jnp.int32, (1, rows), 1)

        def masks(n):
            far_by = (0, 1, 3, 2)[n]
            return jnp.concatenate(
                [place + spot.base(far_by, i) * rows < spot.valid for i in range(4)], axis=1
            )

        def values_of(ref):
            return jnp.where(lane == DV, jnp.ones((), BF), ref[:width, :])

        def raw_scores(query, ref):
            return lax.dot_general(
                query, ref[:width, 128:], (((1,), (1,)), ((), ())), preferred_element_type=F32
            )

        def shares(sums):
            return sums / sums[:, DV : DV + 1]

        if last:
            tails = [r[width:, 128:].astype(F32) for r in pair_refs]
            own, low, high = tails[0], tails[1], tails[2]
            row = lax.broadcasted_iota(jnp.int32, (TAIL, 128), 0)
            edge = jnp.zeros((TAIL, 128), F32)
            for d in range(4):
                n, m = (d + 1) % 4, (d + 3) % 4
                at = spot.ring_place(d)
                other = jnp.where(spot.core == 0, own[4 + n : 5 + n], low[4 + d : 5 + d])
                prev = jnp.where(at == 0, low[4 + n : 5 + n], other)
                other = jnp.where(spot.core == 0, own[m : m + 1], high[d : d + 1])
                nxt = jnp.where(at == 3, high[m : m + 1], other)
                edge = jnp.where(row == d, prev, edge)
                edge = jnp.where(row == 4 + d, nxt, edge)
            edge = edge.astype(BF)
            parts = [jnp.where(masks(n), raw_scores(edge, r), -1e30) for n, r in enumerate(pair_refs)]
            peak = jnp.max(parts[0], axis=1, keepdims=True)
            for s in parts[1:]:
                peak = jnp.maximum(peak, jnp.max(s, axis=1, keepdims=True))
            edge_sums = jnp.zeros((TAIL, 256), F32)
            for s, r in zip(parts, pair_refs):
                edge_sums += jnp.dot(jnp.exp(s - peak).astype(BF), values_of(r), preferred_element_type=F32)
            edge_out = shares(edge_sums)
            row = lax.broadcasted_iota(jnp.int32, (TAIL, 256), 0)

        pair_ref = pair_refs[-1]
        keep = masks(near)
        values = values_of(pair_ref)
        for i in range(4):
            score_ref[i] = raw_scores(q_refs[i][:, 256:], pair_ref)
        for i in range(4):
            for k in range(0, rows, strip):
                cut = slice(k, k + strip)
                scores = jnp.where(keep, score_ref[i, cut, :], -1e30)
                peak = jnp.broadcast_to(jnp.max(scores, axis=1, keepdims=True), (strip, 128))
                if not first:
                    peak = jnp.maximum(peak, old_peak[i * rows + k : i * rows + k + strip, :])
                across = jnp.concatenate([peak] * (width // 128), axis=1)
                prob_ref[i, cut, :] = jnp.exp(scores - across).astype(BF)
                peak_ref[i, cut, :] = peak
            update = jnp.dot(prob_ref[i], values, preferred_element_type=F32)
            if not first:
                shrink = jnp.exp(old_peak[i * rows : (i + 1) * rows, :] - peak_ref[i])
                update = update + old[i * rows : (i + 1) * rows, :] * jnp.concatenate([shrink] * 2, axis=1)
            if last:
                refs[i][:rows, :] = shares(update).astype(BF)
                ends = jnp.where(row == 0, edge_out[i : i + 1], jnp.zeros((TAIL, 256), F32))
                ends = jnp.where(row == 1, edge_out[4 + i : 5 + i], ends)
                refs[i][rows:, :] = ends.astype(BF)
            else:
                refs[0][i * rows : (i + 1) * rows, :] = update
                refs[1][i * rows : (i + 1) * rows, :] = peak_ref[i]

    ins = [*q, *pairs]
    if not first:
        ins += [*state]
    if last:
        outs = [jax.ShapeDtypeStruct((rows + TAIL, 256), BF)] * 4
    else:
        outs = [jax.ShapeDtypeStruct((4 * rows, n), F32) for n in (256, 128)]
    return pl.pallas_call(
        kernel,
        out_shape=outs,
        in_specs=[SMEM] + [VMEM] * len(ins) + [ANY] * len(behind),
        out_specs=[VMEM] * len(outs),
        scratch_shapes=[
            pltpu.VMEM((4, rows, width), F32),
            pltpu.VMEM((4, rows, width), BF),
            pltpu.VMEM((4, rows, 128), F32),
        ],
        compiler_params=params(24),
        cost_estimate=pl.CostEstimate(
            flops=4 * 2 * rows * width * 512, bytes_accessed=4 << 20, transcendentals=4 * rows * width
        ),
        name="attend",
    )(scalars, *ins, *behind)


def edges(mark, trunk, skip, cotangent):
    columns = trunk.shape[1]

    def kernel(mark_ref, t_ref, s_ref, c_ref, down, up, buffer, sems):
        copies = []
        for n, ref in enumerate((t_ref, s_ref, c_ref)):
            for end in range(2):
                start = end * (ref.shape[0] - TAIL)
                copies.append(
                    pltpu.make_async_copy(
                        ref.at[pl.ds(start, TAIL), :], buffer.at[2 * n + end], sems.at[2 * n + end]
                    )
                )
        for copy in copies:
            copy.start()
        for copy in copies:
            copy.wait()
        t_first, t_last, s_first, s_last, c_first, c_last = (buffer[n].astype(F32) for n in range(6))
        row = lax.broadcasted_iota(jnp.int32, (TAIL, columns), 0)

        def four(a, b, c, d):
            rest = jnp.where(row == 2, c, jnp.where(row == 3, d, 0.0))
            return jnp.where(row == 0, a, jnp.where(row == 1, b, rest)).astype(BF)

        up[...] = four(t_first[:1], s_first[:1], s_first[1:2], c_first[:1])
        e = TAIL - 1
        down[...] = four(t_last[e:], s_last[e - 1 : e], s_last[e:], c_last[e:])

    return pl.pallas_call(
        kernel,
        out_shape=[jax.ShapeDtypeStruct((TAIL, columns), BF)] * 2,
        in_specs=[ANY] * 4,
        out_specs=[VMEM] * 2,
        scratch_shapes=[pltpu.VMEM((6, TAIL, columns), BF), pltpu.SemaphoreType.DMA((6,))],
        compiler_params=params(53),
        name="edges",
    )(mark, trunk, skip, cotangent)


def gelu_parts(pre):
    slope = math.sqrt(2.0 / math.pi)
    square = pre * pre
    bend = jnp.tanh(slope * (pre + 0.044715 * (square * pre)))
    return bend, square, slope


WIDE = 256
STRIP = 32


def forward(scalars, ours, back, tokens, skipped, out_heads, before, after, depth_weight, turned):
    rows, columns = tokens.shape
    fine = 2 * rows
    half = columns // 2
    steps = half // WIDE
    quarter = columns // 4

    def side(s_ref):
        return s_ref[1] if ours else 1 - s_ref[1]

    def kernel(s_ref, b0, b1, b2, b3, low_ref, high_ref, dw_ref, tok_hbm, skip_hbm, ow_hbm, g_hbm, *refs):
        if ours:
            up_ref, act_ref = refs[:2]
            refs = refs[2:]
        else:
            up_ref, prod_ref, act_ref, g_ref = refs[:4]
            refs = refs[4:]
        att, held, tok, skp, ow, sems = refs
        j = pl.program_id(0)

        def copies(n):
            take = pl.ds(pl.multiple_of(side(s_ref) * half + n * WIDE, 128), WIDE)
            return [
                pltpu.make_async_copy(ow_hbm.at[:, :, take], ow.at[n], sems.at[3 * n]),
                pltpu.make_async_copy(tok_hbm.at[:, take], tok.at[n], sems.at[3 * n + 1]),
                pltpu.make_async_copy(skip_hbm.at[:, take], skp.at[n], sems.at[3 * n + 2]),
            ]

        turned_copy = None if ours else pltpu.make_async_copy(g_hbm, g_ref, sems.at[3 * steps])

        @pl.when(j == 0)
        def _():
            for n in range(steps):
                for copy in copies(n):
                    copy.start()
            if not ours:
                turned_copy.start()
            mixed = [b[:, :DV].astype(F32) for b in (b0, b1, b2, b3)]
            squares = sum(jnp.sum(m * m, axis=1, keepdims=True) for m in mixed)
            scale = lax.rsqrt(squares * (1.0 / (H * DV)) + 1e-05)
            for d in range(4):
                att[d] = (mixed[d] * scale).astype(BF)

        @pl.when(j < steps)
        def _():
            spot = Spot(s_ref)
            n = jnp.minimum(j, steps - 1)
            for copy in copies(n):
                copy.wait()
            low, high = low_ref[...].astype(F32), high_ref[...].astype(F32)
            grown = jnp.zeros((rows + TAIL, WIDE), F32)
            for d in range(4):
                grown += jnp.dot(att[d], ow[n, (spot.head_at + d) % 4], preferred_element_type=F32)
            hidden = (tok[n].astype(F32) + grown[:rows]).astype(BF)
            low_hid = (low[:1] + grown[rows : rows + 1]).astype(BF).astype(F32)
            high_hid = (high[:1] + grown[rows + 1 : rows + 2]).astype(BF).astype(F32)
            twice = lax.broadcasted_iota(jnp.int32, (fine, rows), 0) // 2
            twice = jnp.where(twice == lax.broadcasted_iota(jnp.int32, (fine, rows), 1), 1.0, 0.0).astype(BF)
            doubled = jnp.dot(twice, hidden, preferred_element_type=F32)
            row = lax.broadcasted_iota(jnp.int32, (TAIL, WIDE), 0)
            edge = (low_hid + jnp.where(row == 14, low[1:2], low[2:3])).astype(BF).astype(F32)
            edge = jnp.where((row >= 14) & (spot.place > 0), edge, 0.0)
            held[:TAIL, :] = edge
            up_ref[:TAIL, :] = edge.astype(BF)
            edge = (high_hid + jnp.where(row == 0, high[1:2], high[2:3])).astype(BF).astype(F32)
            edge = jnp.where((row < 2) & (spot.place < 15), edge, 0.0)
            held[TAIL + fine :, :] = edge
            up_ref[TAIL + fine :, :] = edge.astype(BF)
            for k in range(0, fine, STRIP):
                up = (doubled[k : k + STRIP] + skp[n, k : k + STRIP, :].astype(F32)).astype(BF)
                up_ref[TAIL + k : TAIL + k + STRIP, :] = up
                held[TAIL + k : TAIL + k + STRIP, :] = up.astype(F32)
            w = [dw_ref[t : t + 1, :] for t in range(3)]
            cut = pl.ds(0 if ours else pl.multiple_of(n * WIDE, 128), WIDE)
            for k in range(0, fine, STRIP):
                near = held[8 + k : 24 + k + STRIP, :]
                pre = w[0] * near[7 : 7 + STRIP] + w[1] * near[8 : 8 + STRIP] + w[2] * near[9 : 9 + STRIP]
                bend, _, _ = gelu_parts(pre)
                act_ref[k : k + STRIP, cut] = (pre * (0.5 + 0.5 * bend)).astype(BF)

        if not ours:

            @pl.when(j == steps)
            def _():
                turned_copy.wait()

            @pl.when(j >= steps)
            def _():
                at = pl.multiple_of((Spot(s_ref).their_first + j - steps) % 4 * quarter, 16)
                prod_ref[0] = jnp.dot(
                    g_ref[pl.ds(at, quarter), :], act_ref[...], preferred_element_type=F32
                ).astype(BF)

    def cols(count, full):
        def place(j, s_ref):
            n = jnp.minimum(j, steps - 1)
            return 0, (side(s_ref) * steps + n if full else n)

        return pl.BlockSpec((count, WIDE), place)

    def flat(count, width):
        return pl.BlockSpec((count, width), lambda j, s_ref: (0, 0))

    outs = [jax.ShapeDtypeStruct((fine + 2 * TAIL, half), BF)]
    out_specs = [cols(fine + 2 * TAIL, False)]
    scratch = []
    if ours:
        outs += [jax.ShapeDtypeStruct((fine, half), BF)]
        out_specs += [cols(fine, False)]
    else:
        outs += [jax.ShapeDtypeStruct((4, quarter, half), BF)]
        out_specs += [
            pl.BlockSpec((1, quarter, half), lambda j, s_ref: (jnp.maximum(j - steps, 0), 0, 0))
        ]
        scratch += [pltpu.VMEM((fine, half), BF), pltpu.VMEM((columns, fine), BF)]
    scratch += [
        pltpu.VMEM((4, rows + TAIL, DV), BF),
        pltpu.VMEM((fine + 2 * TAIL, WIDE), F32),
        pltpu.VMEM((steps, rows, WIDE), BF),
        pltpu.VMEM((steps, fine, WIDE), BF),
        pltpu.VMEM((steps, H, DV, WIDE), BF),
        pltpu.SemaphoreType.DMA((3 * steps + 1,)),
    ]
    return pl.pallas_call(
        kernel,
        out_shape=outs,
        grid_spec=pltpu.PrefetchScalarGridSpec(
            num_scalar_prefetch=1,
            grid=(steps if ours else steps + 4,),
            in_specs=[flat(rows + TAIL, 256)] * 4
            + [cols(TAIL, True), cols(TAIL, True), cols(3, True)]
            + [ANY] * 4,
            out_specs=out_specs,
            scratch_shapes=scratch,
        ),
        compiler_params=params(53),
        cost_estimate=pl.CostEstimate(
            flops=2 * fine * columns * columns, bytes_accessed=9 << 20, transcendentals=fine * half
        ),
        name="forward",
    )(scalars, *back, before, after, depth_weight, tokens, skipped, out_heads, turned)


def backward(scalars, theirs, ours, upstream, before, after, point_weight, depth_weight, behind):
    fine, columns = upstream.shape
    half = columns // 2
    steps = half // WIDE

    def kernel(s_ref, theirs_ref, ours_ref, g_ref, low_ref, high_ref, pw_ref, dw_ref, behind_ref, *refs):
        gs_ref, gd_theirs, gd_ours, grad, upper, ends, up_ref = refs
        j = pl.program_id(0)

        @pl.when(j < steps)
        def _():
            up_ref[...] = theirs_ref[...]

        @pl.when(j >= steps)
        def _():
            up_ref[...] = ours_ref[...]

        dims = (((1,), (1,)), ((), ()))

        @pl.when(pl.program_id(0) == 0)
        def _():
            row = lax.broadcasted_iota(jnp.int32, (TAIL, columns), 0)
            low, high = low_ref[...].astype(F32), high_ref[...].astype(F32)
            ends[...] = jnp.where(row == 7, low[3:4], jnp.where(row == 8, high[3:4], 0.0)).astype(BF)

        upper[...] = lax.dot_general(g_ref[...], pw_ref[...], dims, preferred_element_type=F32)
        outer = lax.dot_general(ends[...], pw_ref[...], dims, preferred_element_type=F32)
        w = [dw_ref[t : t + 1, :] for t in range(3)]

        def grad_of(near, start, count, coming):
            taps = [near[start - 1 + t : start - 1 + t + count] for t in range(3)]
            pre = w[0] * taps[0] + w[1] * taps[1] + w[2] * taps[2]
            bend, square, slope = gelu_parts(pre)
            rate = 0.5 + 0.5 * bend + (pre * (1.0 - bend * bend)) * (
                0.5 * slope + (1.5 * slope * 0.044715) * square
            )
            return taps, (coming * rate).astype(BF).astype(F32)

        _, grad[8:16, :] = grad_of(up_ref[:32, :].astype(F32), 8, 8, outer[:8])
        _, grad[16 + fine : 24 + fine, :] = grad_of(up_ref[fine:, :].astype(F32), 16, 8, outer[8:])
        sums = [jnp.zeros((8, WIDE), F32)] * 3
        for k in range(0, fine, STRIP):
            near = up_ref[k : k + STRIP + 2 * TAIL, :].astype(F32)
            taps, mid = grad_of(near, TAIL, STRIP, upper[k : k + STRIP, :])
            grad[16 + k : 16 + k + STRIP, :] = mid
            for t in range(3):
                term = taps[t] * mid
                for r in range(0, STRIP, 8):
                    sums[t] = sums[t] + term[r : r + 8]
        depth = [jnp.sum(total, axis=0, keepdims=True) for total in sums]
        for ref, mine in ((gd_theirs, j < steps), (gd_ours, j >= steps)):

            @pl.when(mine)
            def _():
                for t in range(3):
                    ref[t : t + 1, :] = depth[t]

        for k in range(0, fine, STRIP):
            near = grad[8 + k : 24 + k + STRIP, :]
            gs_ref[k : k + STRIP, :] = (
                w[0] * near[9 : 9 + STRIP] + w[1] * near[8 : 8 + STRIP] + w[2] * near[7 : 7 + STRIP]
            ).astype(BF)

    def block(j, s_ref):
        return jnp.where(j < steps, (1 - s_ref[1]) * steps + j, s_ref[1] * steps + j - steps)

    def cols(count):
        return pl.BlockSpec((count, WIDE), lambda j, s_ref: (0, block(j, s_ref)))

    def early(count):
        return pl.BlockSpec((count, WIDE), lambda j, s_ref: (0, jnp.minimum(j, steps - 1)))

    def late(count):
        return pl.BlockSpec((count, WIDE), lambda j, s_ref: (0, jnp.maximum(j - steps, 0)))

    def flat(count):
        return pl.BlockSpec((count, columns), lambda j, s_ref: (0, 0))

    return pl.pallas_call(
        kernel,
        out_shape=[
            jax.ShapeDtypeStruct((fine, columns), BF),
            jax.ShapeDtypeStruct((3, half), F32),
            jax.ShapeDtypeStruct((3, half), F32),
        ],
        grid_spec=pltpu.PrefetchScalarGridSpec(
            num_scalar_prefetch=1,
            grid=(2 * steps,),
            in_specs=[
                early(fine + 2 * TAIL),
                late(fine + 2 * TAIL),
                flat(fine),
                flat(TAIL),
                flat(TAIL),
                pl.BlockSpec((WIDE, columns), lambda j, s_ref: (block(j, s_ref), 0)),
                cols(3),
                ANY,
            ],
            out_specs=[cols(fine), early(3), late(3)],
            scratch_shapes=[
                pltpu.VMEM((fine + 2 * TAIL, WIDE), F32),
                pltpu.VMEM((fine, WIDE), F32),
                pltpu.VMEM((TAIL, columns), BF),
                pltpu.VMEM((fine + 2 * TAIL, WIDE), BF),
            ],
        ),
        compiler_params=params(48),
        cost_estimate=pl.CostEstimate(
            flops=2 * fine * columns * columns, bytes_accessed=11 << 20, transcendentals=fine * columns
        ),
        name="backward",
    )(scalars, theirs, ours, upstream, before, after, point_weight, depth_weight, behind)


def product(scalars, act, turned, steps, arrived):
    half, quarter = act.shape[1], turned.shape[0] // 4

    def kernel(s_ref, a_ref, g_ref, arrived_ref, *outs):
        for out, d in zip(outs, steps):
            at = pl.multiple_of((Spot(s_ref).first_at + d) % 4 * quarter, 16)
            block = jnp.dot(g_ref[pl.ds(at, quarter), :], a_ref[...], preferred_element_type=F32)
            out[...] = (block + arrived_ref[d].astype(F32)).astype(BF)

    return pl.pallas_call(
        kernel,
        out_shape=[jax.ShapeDtypeStruct((quarter, half), BF)] * len(steps),
        in_specs=[SMEM] + [VMEM] * 3,
        out_specs=[VMEM] * len(steps),
        compiler_params=params(14),
        cost_estimate=pl.CostEstimate(
            flops=2 * act.shape[0] * half * quarter * len(steps), bytes_accessed=6 << 20, transcendentals=0
        ),
        name="product",
    )(scalars, act, turned, arrived)


def split_rows(at, got):
    rows, columns = got[0].shape
    slim = rows // 4

    def kernel(at_ref, *refs):
        ins, outs = refs[:4], refs[4:]
        for d in range(4):
            take = pl.ds(pl.multiple_of((Spot(at_ref).second_at + d) % 4 * slim, 16), slim)
            outs[d][...] = total_of([r[take, :] for r in ins]).astype(BF)

    return pl.pallas_call(
        kernel,
        out_shape=[jax.ShapeDtypeStruct((slim, columns), BF)] * 4,
        in_specs=[SMEM] + [VMEM] * 4,
        out_specs=[VMEM] * 4,
        compiler_params=params(10),
        name="split_rows",
    )(at, *got)


def join_rows(at, got):
    slim, columns = got[0].shape[0] - TAIL, got[0].shape[1]
    quarter = 4 * slim

    def kernel(at_ref, *refs):
        ins, upper, lower, held = refs[:4], refs[4], refs[5], refs[6]
        for d in range(4):
            put = pl.ds(pl.multiple_of((Spot(at_ref).second_at + 4 - d) % 4 * slim, 16), slim)
            held[put, :] = ins[d][:slim, :]
        turned = held[...].T
        upper[...] = turned[: columns // 2]
        lower[: columns // 2, :] = turned[columns // 2 :]
        last = total_of([r[slim:, :] for r in ins])[:8]
        lower[columns // 2 :, :] = jnp.concatenate([last[:, :quarter], last[:, quarter:]], axis=0).astype(BF)

    return pl.pallas_call(
        kernel,
        out_shape=[jax.ShapeDtypeStruct((columns // 2 + n, quarter), BF) for n in (0, TAIL)],
        in_specs=[SMEM] + [VMEM] * 4,
        out_specs=[VMEM] * 2,
        scratch_shapes=[pltpu.VMEM((quarter, columns), BF)],
        compiler_params=params(10),
        name="join_rows",
    )(at, *got)


def lay_out(scalars, own, other):
    part, quarter = own[0][0].shape
    half = 2 * part

    def kernel(s_ref, *refs):
        out, sems = refs[-2:]
        spot = Spot(s_ref)
        copies = []
        for n in range(16):
            mine, d, low = n < 8, n // 2 % 4, n % 2
            down = (spot.core if mine else 1 - spot.core) * half + low * part
            over = ((spot.first_at if mine else spot.their_first) + 4 - d) % 4 * quarter
            copies.append(
                pltpu.make_async_copy(
                    refs[n].at[pl.ds(0, part), :],
                    out.at[pl.ds(pl.multiple_of(down, 16), part), pl.ds(pl.multiple_of(over, 128), quarter)],
                    sems.at[n],
                )
            )
        for copy in copies:
            copy.start()
        for copy in copies:
            copy.wait()

    return pl.pallas_call(
        kernel,
        out_shape=jax.ShapeDtypeStruct((2 * half, 4 * quarter), BF),
        in_specs=[SMEM] + [VMEM] * 16,
        out_specs=ANY,
        scratch_shapes=[pltpu.SemaphoreType.DMA((16,))],
        compiler_params=params(8),
        name="lay_out",
    )(scalars, *[p for pieces in (own, other) for pair in pieces for p in pair])


def local(
    trunk,
    skip,
    valid_bins,
    query_weight,
    key_weight,
    value_weight,
    out_weight,
    depth_weight,
    point_weight,
    cotangent,
):
    tokens, skipped, upstream = trunk[0], skip[0], cotangent[0]
    rows, columns = tokens.shape
    fine = skipped.shape[0]
    ix, ic, iz, iy = (lax.axis_index(a) for a in AXES)
    scalars = jnp.stack([v.astype(jnp.int32) for v in (ix, ic, iz, iy, valid_bins[0])])
    blocks = project(scalars, tokens, query_weight, key_weight, value_weight)
    down, up = edges(blocks[0], tokens, skipped, upstream)
    before = lax.ppermute(down, ("z", "y"), [(i, i + 1) for i in range(15)])
    after = lax.ppermute(up, ("z", "y"), [(i + 1, i) for i in range(15)])
    q = exchange(blocks, HEAD_RING)
    own = stack_rows(q, down)
    far = {d: lax.ppermute(own, AXES, turn(ROW_RING, d)) for d in (1, 3, 2)}
    state = attend(scalars, 0, q, [own], None, (before, after))

    turned = upstream.T

    state = attend(scalars, 1, q, [far[1]], state)
    state = attend(scalars, 2, q, [far[3]], state)
    mixed = attend(scalars, 3, q, [own, far[1], far[3], far[2]], state)
    back = exchange(mixed, HEAD_RING, -1)
    swap = [(0, 1), (1, 0)]
    given = (back, tokens, skipped, out_weight.reshape(H, DV, -1), before, after, depth_weight, turned)
    up_theirs, sent = forward(scalars, False, *given)
    arrived = lax.ppermute(sent, "c", swap)
    up_ours, act = forward(scalars, True, *given)
    piece_2, piece_1 = product(scalars, act, turned, (2, 1), arrived)
    piece_3, piece_0 = product(scalars, act, turned, (3, 0), arrived)
    got = exchange([piece_0, piece_1, piece_2, piece_3], SUM_RINGS[0])

    grad_skip, d_theirs, d_mine = backward(
        scalars, up_theirs, up_ours, upstream, before, after, point_weight, depth_weight, piece_0
    )
    d_sum = d_mine + lax.ppermute(d_theirs, "c", swap)
    rider = jnp.pad(d_sum.astype(BF), ((0, TAIL - 3), (0, 0)))

    got = exchange(split_rows(scalars, got), SUM_RINGS[1])
    mixed = jnp.concatenate([total_of(got).astype(BF), rider], axis=0)
    got = exchange([mixed] * 4, SUM_RINGS[2])
    norm_scale = 1.0 / math.sqrt(128 * fine)
    summed = (total_of(got) * norm_scale).astype(BF)
    upper, lower = join_rows(scalars, exchange([summed] * 4, SUM_RINGS[1]))

    def go(block, step):
        return lax.ppermute(block, AXES, turn(SUM_RINGS[0], step))

    upper_1, lower_3 = go(upper, 1), go(lower, 3)
    lower_1, upper_3 = go(lower, 1), go(upper, 3)
    upper_2, lower_2 = go(upper_1, 1), go(lower_3, 3)
    own = [(upper, lower), (upper_1, lower_1), (upper_2, lower_2), (upper_3, lower_3)]
    other = [tuple(lax.ppermute(p, "c", swap) for p in pair) for pair in own]
    grad_pointwise = lay_out(scalars, own, other)

    half = columns // 2

    def depth_of(pairs):
        rows = total_of([low[half // 2 :] for _, low in pairs])
        return jnp.concatenate([rows[:3], rows[8:11]], axis=1)

    d_own, d_other = depth_of(own), depth_of(other)
    grad_depth = jnp.concatenate(
        [jnp.where(ic == 0, d_own, d_other), jnp.where(ic == 0, d_other, d_own)], axis=1
    )
    return (grad_pointwise, grad_depth, grad_skip[None])


def solution(mesh):
    fine_mesh = Mesh(mesh.devices.reshape(SIZES), AXES)
    rows = P(("x", "c"), ("z", "y"), None)
    return jax.shard_map(
        local,
        mesh=fine_mesh,
        in_specs=(rows, rows, P(("x", "c")), P(), P(), P(), P(), P(), P(), rows),
        out_specs=(P(), P(), rows),
        check_vma=False,
    )
```

```python
import math

import jax
import jax.numpy as jnp
from jax import lax
from jax.experimental import pallas as pl
from jax.experimental.pallas import tpu as pltpu
from jax.sharding import Mesh, PartitionSpec as P

H = 4
DH = 64
DV = 192
AXES = ("x", "c", "z", "y")
SIZES = (4, 2, 4, 4)
BF = jnp.bfloat16
F32 = jnp.float32
TAIL = 16
VMEM = pl.BlockSpec(memory_space=pltpu.VMEM)
SMEM = pl.BlockSpec(memory_space=pltpu.SMEM)
ANY = pl.BlockSpec(memory_space=pl.ANY)
SUM_RINGS = (("x", "y"), ("y", "z"), ("z", "x"))
HEAD_RING = ("y", "z")
ROW_RING = ("z", "y")


class Spot:
    def __init__(self, s_ref):
        x, core, z, y = (s_ref[n] for n in range(4))
        first = core == 0
        self.core, self.y, self.valid = core, y, s_ref[4]
        self.head_at = jnp.where(first, y, z)
        self.row_at = jnp.where(first, z, y)
        self.first_at = jnp.where(first, x, y)
        self.their_first = jnp.where(first, y, x)
        self.second_at = jnp.where(first, y, z)
        self.place = z * 4 + y

    def base(self, far_by, d):
        h, r = (self.head_at + 4 - d) % 4, (self.row_at + 4 - far_by) % 4
        return jnp.where(self.core == 0, r * 4 + h, h * 4 + r)

    def ring_place(self, d):
        return jnp.where(self.core == 0, (self.y + 4 - d) % 4, self.y)


def params(mib):
    return pltpu.CompilerParams(vmem_limit_bytes=mib << 20)


def turn(axes, step):
    pairs = []
    for x in range(4):
        for c in range(2):
            for z in range(4):
                for y in range(4):
                    at = {"x": x, "z": z, "y": y}
                    to = dict(at)
                    to[axes[c]] = (at[axes[c]] + step) % 4
                    flat = [((p["x"] * 2 + c) * 4 + p["z"]) * 4 + p["y"] for p in (at, to)]
                    pairs.append(tuple(flat))
    return pairs


def exchange(pieces, axes, sign=1):
    got = [pieces[0], None, None, None]
    for d in (2, 1, 3):
        got[d] = lax.ppermute(pieces[d], AXES, turn(axes, sign * d))
    return got


def total_of(got):
    a, b, c, d = (g.astype(F32) for g in got)
    return (a + c) + (b + d)


def project(at, tokens, query_weight, key_weight, value_weight):
    rows, depth = tokens.shape
    cut = depth // 2

    def kernel(at_ref, tok_hbm, wq_hbm, wk_hbm, wv_hbm, *refs):
        outs, (tok_ref, wq_ref, wk_ref, wv_ref, held, sems) = refs[:4], refs[4:]
        low, high = pl.ds(0, cut), pl.ds(cut, depth - cut)
        copies = [
            pltpu.make_async_copy(tok_hbm, tok_ref, sems.at[0]),
            pltpu.make_async_copy(wv_hbm.at[low, :], wv_ref.at[low, :], sems.at[1]),
            pltpu.make_async_copy(wv_hbm.at[high, :], wv_ref.at[high, :], sems.at[2]),
            pltpu.make_async_copy(wk_hbm, wk_ref, sems.at[3]),
            pltpu.make_async_copy(wq_hbm, wq_ref, sems.at[4]),
        ]
        for copy in copies:
            copy.start()
        copies[0].wait()
        tok = tok_ref[...]
        copies[1].wait()
        v = jnp.dot(tok[:, :cut], wv_ref[:cut, :], preferred_element_type=F32)
        copies[2].wait()
        v += jnp.dot(tok[:, cut:], wv_ref[cut:, :], preferred_element_type=F32)
        copies[3].wait()
        k = jnp.dot(tok, wk_ref[...], preferred_element_type=F32)
        copies[4].wait()
        q = jnp.dot(tok, wq_ref[...], preferred_element_type=F32) * (1.0 / math.sqrt(DH))
        zero = jnp.zeros((rows, DH), F32)
        for h in range(H):
            held[h] = jnp.concatenate(
                [
                    v[:, h * DV : (h + 1) * DV],
                    k[:, h * DH : (h + 1) * DH],
                    zero,
                    q[:, h * DH : (h + 1) * DH],
                ],
                axis=1,
            ).astype(BF)
        for d in range(4):
            outs[d][...] = held[(Spot(at_ref).head_at + d) % 4]

    return pl.pallas_call(
        kernel,
        out_shape=[jax.ShapeDtypeStruct((rows, 384), BF)] * 4,
        in_specs=[SMEM] + [ANY] * 4,
        out_specs=[VMEM] * 4,
        scratch_shapes=[
            pltpu.VMEM((rows, depth), BF),
            pltpu.VMEM((depth, H * DH), BF),
            pltpu.VMEM((depth, H * DH), BF),
            pltpu.VMEM((depth, H * DV), BF),
            pltpu.VMEM((4, rows, 384), BF),
            pltpu.SemaphoreType.DMA((5,)),
        ],
        compiler_params=params(53),
        name="project",
    )(at, tokens, query_weight, key_weight, value_weight)


def stack_rows(parts, behind):
    rows = parts[0].shape[0]

    def kernel(*refs):
        ins, out = refs[:4], refs[5]
        row = lax.broadcasted_iota(jnp.int32, (TAIL, 128), 0)
        tail = jnp.zeros((TAIL, 128), F32)
        for d in range(4):
            out[d * rows : (d + 1) * rows, :] = ins[d][:, :256]
            first = ins[d][:TAIL, 256:].astype(F32)[:1]
            final = ins[d][rows - TAIL :, 256:].astype(F32)[TAIL - 1 :]
            tail = jnp.where(row == d, first, tail)
            tail = jnp.where(row == 4 + d, final, tail)
        out[4 * rows :, :128] = jnp.zeros((TAIL, 128), BF)
        out[4 * rows :, 128:] = tail.astype(BF)

    return pl.pallas_call(
        kernel,
        out_shape=jax.ShapeDtypeStruct((4 * rows + TAIL, 256), BF),
        in_specs=[VMEM] * 4 + [ANY],
        out_specs=VMEM,
        compiler_params=params(8),
        name="stack_rows",
    )(*parts, behind)


def attend(scalars, near, q, pairs, state, behind=()):
    rows = q[0].shape[0]
    width = 4 * rows
    first = state is None
    last = len(pairs) == 4
    strip = 32

    def kernel(s_ref, *refs):
        spot = Spot(s_ref)
        score_ref, prob_ref, peak_ref = refs[-3:]
        q_refs, refs = refs[:4], refs[4:]
        pair_refs, refs = refs[: len(pairs)], refs[len(pairs) :]
        if not first:
            old, old_peak, refs = refs[0], refs[1], refs[2:]
        refs = refs[len(behind) :]
        lane = lax.broadcasted_iota(jnp.int32, (width, 256), 1)
        place = lax.broadcasted_iota(jnp.int32, (1, rows), 1)

        def masks(n):
            far_by = (0, 1, 3, 2)[n]
            return jnp.concatenate(
                [place + spot.base(far_by, i) * rows < spot.valid for i in range(4)], axis=1
            )

        def values_of(ref):
            return jnp.where(lane == DV, jnp.ones((), BF), ref[:width, :])

        def raw_scores(query, ref):
            return lax.dot_general(
                query, ref[:width, 128:], (((1,), (1,)), ((), ())), preferred_element_type=F32
            )

        def shares(sums):
            return sums / sums[:, DV : DV + 1]

        if last:
            tails = [r[width:, 128:].astype(F32) for r in pair_refs]
            own, low, high = tails[0], tails[1], tails[2]
            row = lax.broadcasted_iota(jnp.int32, (TAIL, 128), 0)
            edge = jnp.zeros((TAIL, 128), F32)
            for d in range(4):
                n, m = (d + 1) % 4, (d + 3) % 4
                at = spot.ring_place(d)
                other = jnp.where(spot.core == 0, own[4 + n : 5 + n], low[4 + d : 5 + d])
                prev = jnp.where(at == 0, low[4 + n : 5 + n], other)
                other = jnp.where(spot.core == 0, own[m : m + 1], high[d : d + 1])
                nxt = jnp.where(at == 3, high[m : m + 1], other)
                edge = jnp.where(row == d, prev, edge)
                edge = jnp.where(row == 4 + d, nxt, edge)
            edge = edge.astype(BF)
            parts = [jnp.where(masks(n), raw_scores(edge, r), -1e30) for n, r in enumerate(pair_refs)]
            peak = jnp.max(parts[0], axis=1, keepdims=True)
            for s in parts[1:]:
                peak = jnp.maximum(peak, jnp.max(s, axis=1, keepdims=True))
            edge_sums = jnp.zeros((TAIL, 256), F32)
            for s, r in zip(parts, pair_refs):
                edge_sums += jnp.dot(jnp.exp(s - peak).astype(BF), values_of(r), preferred_element_type=F32)
            edge_out = shares(edge_sums)
            row = lax.broadcasted_iota(jnp.int32, (TAIL, 256), 0)

        pair_ref = pair_refs[-1]
        keep = masks(near)
        values = values_of(pair_ref)
        for i in range(4):
            score_ref[i] = raw_scores(q_refs[i][:, 256:], pair_ref)
        for i in range(4):
            for k in range(0, rows, strip):
                cut = slice(k, k + strip)
                scores = jnp.where(keep, score_ref[i, cut, :], -1e30)
                peak = jnp.broadcast_to(jnp.max(scores, axis=1, keepdims=True), (strip, 128))
                if not first:
                    peak = jnp.maximum(peak, old_peak[i * rows + k : i * rows + k + strip, :])
                across = jnp.concatenate([peak] * (width // 128), axis=1)
                prob_ref[i, cut, :] = jnp.exp(scores - across).astype(BF)
                peak_ref[i, cut, :] = peak
            update = jnp.dot(prob_ref[i], values, preferred_element_type=F32)
            if not first:
                shrink = jnp.exp(old_peak[i * rows : (i + 1) * rows, :] - peak_ref[i])
                update = update + old[i * rows : (i + 1) * rows, :] * jnp.concatenate([shrink] * 2, axis=1)
            if last:
                refs[i][:rows, :] = shares(update).astype(BF)
                ends = jnp.where(row == 0, edge_out[i : i + 1], jnp.zeros((TAIL, 256), F32))
                ends = jnp.where(row == 1, edge_out[4 + i : 5 + i], ends)
                refs[i][rows:, :] = ends.astype(BF)
            else:
                refs[0][i * rows : (i + 1) * rows, :] = update
                refs[1][i * rows : (i + 1) * rows, :] = peak_ref[i]

    ins = [*q, *pairs]
    if not first:
        ins += [*state]
    if last:
        outs = [jax.ShapeDtypeStruct((rows + TAIL, 256), BF)] * 4
    else:
        outs = [jax.ShapeDtypeStruct((4 * rows, n), F32) for n in (256, 128)]
    return pl.pallas_call(
        kernel,
        out_shape=outs,
        in_specs=[SMEM] + [VMEM] * len(ins) + [ANY] * len(behind),
        out_specs=[VMEM] * len(outs),
        scratch_shapes=[
            pltpu.VMEM((4, rows, width), F32),
            pltpu.VMEM((4, rows, width), BF),
            pltpu.VMEM((4, rows, 128), F32),
        ],
        compiler_params=params(24),
        cost_estimate=pl.CostEstimate(
            flops=4 * 2 * rows * width * 512, bytes_accessed=4 << 20, transcendentals=4 * rows * width
        ),
        name="attend",
    )(scalars, *ins, *behind)


def edges(mark, trunk, skip, cotangent):
    columns = trunk.shape[1]

    def kernel(mark_ref, t_ref, s_ref, c_ref, down, up, buffer, sems):
        copies = []
        for n, ref in enumerate((t_ref, s_ref, c_ref)):
            for end in range(2):
                start = end * (ref.shape[0] - TAIL)
                copies.append(
                    pltpu.make_async_copy(
                        ref.at[pl.ds(start, TAIL), :], buffer.at[2 * n + end], sems.at[2 * n + end]
                    )
                )
        for copy in copies:
            copy.start()
        for copy in copies:
            copy.wait()
        t_first, t_last, s_first, s_last, c_first, c_last = (buffer[n].astype(F32) for n in range(6))
        row = lax.broadcasted_iota(jnp.int32, (TAIL, columns), 0)

        def four(a, b, c, d):
            rest = jnp.where(row == 2, c, jnp.where(row == 3, d, 0.0))
            return jnp.where(row == 0, a, jnp.where(row == 1, b, rest)).astype(BF)

        up[...] = four(t_first[:1], s_first[:1], s_first[1:2], c_first[:1])
        e = TAIL - 1
        down[...] = four(t_last[e:], s_last[e - 1 : e], s_last[e:], c_last[e:])

    return pl.pallas_call(
        kernel,
        out_shape=[jax.ShapeDtypeStruct((TAIL, columns), BF)] * 2,
        in_specs=[ANY] * 4,
        out_specs=[VMEM] * 2,
        scratch_shapes=[pltpu.VMEM((6, TAIL, columns), BF), pltpu.SemaphoreType.DMA((6,))],
        compiler_params=params(53),
        name="edges",
    )(mark, trunk, skip, cotangent)


def gelu_parts(pre):
    slope = math.sqrt(2.0 / math.pi)
    square = pre * pre
    bend = jnp.tanh(slope * (pre + 0.044715 * (square * pre)))
    return bend, square, slope


WIDE = 384
STRIP = 32


def forward(scalars, ours, back, tokens, skipped, out_heads, before, after, depth_weight, turned):
    rows, columns = tokens.shape
    fine = 2 * rows
    half = columns // 2
    steps = half // WIDE
    quarter = columns // 4

    def side(s_ref):
        return s_ref[1] if ours else 1 - s_ref[1]

    def kernel(s_ref, b0, b1, b2, b3, low_ref, high_ref, dw_ref, tok_hbm, skip_hbm, ow_hbm, g_hbm, *refs):
        if ours:
            up_ref, act_ref = refs[:2]
            refs = refs[2:]
        else:
            up_ref, prod_ref, act_ref, g_ref = refs[:4]
            refs = refs[4:]
        att, held, tok, skp, ow, sems = refs
        j = pl.program_id(0)

        def copies(n):
            take = pl.ds(pl.multiple_of(side(s_ref) * half + n * WIDE, 128), WIDE)
            return [
                pltpu.make_async_copy(ow_hbm.at[:, :, take], ow.at[n], sems.at[3 * n]),
                pltpu.make_async_copy(tok_hbm.at[:, take], tok.at[n], sems.at[3 * n + 1]),
                pltpu.make_async_copy(skip_hbm.at[:, take], skp.at[n], sems.at[3 * n + 2]),
            ]

        turned_copy = None if ours else pltpu.make_async_copy(g_hbm, g_ref, sems.at[3 * steps])

        @pl.when(j == 0)
        def _():
            for n in range(steps):
                for copy in copies(n):
                    copy.start()
            if not ours:
                turned_copy.start()
            mixed = [b[:, :DV].astype(F32) for b in (b0, b1, b2, b3)]
            squares = sum(jnp.sum(m * m, axis=1, keepdims=True) for m in mixed)
            scale = lax.rsqrt(squares * (1.0 / (H * DV)) + 1e-05)
            for d in range(4):
                att[d] = (mixed[d] * scale).astype(BF)

        @pl.when(j < steps)
        def _():
            spot = Spot(s_ref)
            n = jnp.minimum(j, steps - 1)
            for copy in copies(n):
                copy.wait()
            low, high = low_ref[...].astype(F32), high_ref[...].astype(F32)
            grown = jnp.zeros((rows + TAIL, WIDE), F32)
            for d in range(4):
                grown += jnp.dot(att[d], ow[n, (spot.head_at + d) % 4], preferred_element_type=F32)
            hidden = (tok[n].astype(F32) + grown[:rows]).astype(BF)
            low_hid = (low[:1] + grown[rows : rows + 1]).astype(BF).astype(F32)
            high_hid = (high[:1] + grown[rows + 1 : rows + 2]).astype(BF).astype(F32)
            twice = lax.broadcasted_iota(jnp.int32, (fine, rows), 0) // 2
            twice = jnp.where(twice == lax.broadcasted_iota(jnp.int32, (fine, rows), 1), 1.0, 0.0).astype(BF)
            doubled = jnp.dot(twice, hidden, preferred_element_type=F32)
            row = lax.broadcasted_iota(jnp.int32, (TAIL, WIDE), 0)
            edge = (low_hid + jnp.where(row == 14, low[1:2], low[2:3])).astype(BF).astype(F32)
            edge = jnp.where((row >= 14) & (spot.place > 0), edge, 0.0)
            held[:TAIL, :] = edge
            up_ref[:TAIL, :] = edge.astype(BF)
            edge = (high_hid + jnp.where(row == 0, high[1:2], high[2:3])).astype(BF).astype(F32)
            edge = jnp.where((row < 2) & (spot.place < 15), edge, 0.0)
            held[TAIL + fine :, :] = edge
            up_ref[TAIL + fine :, :] = edge.astype(BF)
            for k in range(0, fine, STRIP):
                up = (doubled[k : k + STRIP] + skp[n, k : k + STRIP, :].astype(F32)).astype(BF)
                up_ref[TAIL + k : TAIL + k + STRIP, :] = up
                held[TAIL + k : TAIL + k + STRIP, :] = up.astype(F32)
            w = [dw_ref[t : t + 1, :] for t in range(3)]
            cut = pl.ds(0 if ours else pl.multiple_of(n * WIDE, 128), WIDE)
            for k in range(0, fine, STRIP):
                near = held[8 + k : 24 + k + STRIP, :]
                pre = w[0] * near[7 : 7 + STRIP] + w[1] * near[8 : 8 + STRIP] + w[2] * near[9 : 9 + STRIP]
                bend, _, _ = gelu_parts(pre)
                act_ref[k : k + STRIP, cut] = (pre * (0.5 + 0.5 * bend)).astype(BF)

        if not ours:

            @pl.when(j == steps)
            def _():
                turned_copy.wait()

            @pl.when(j >= steps)
            def _():
                for n in range(2):
                    at = pl.multiple_of((Spot(s_ref).their_first + 2 * (j - steps) + n) % 4 * quarter, 16)
                    prod_ref[n] = jnp.dot(
                        g_ref[pl.ds(at, quarter), :], act_ref[...], preferred_element_type=F32
                    ).astype(BF)

    def cols(count, full):
        def place(j, s_ref):
            n = jnp.minimum(j, steps - 1)
            return 0, (side(s_ref) * steps + n if full else n)

        return pl.BlockSpec((count, WIDE), place)

    def flat(count, width):
        return pl.BlockSpec((count, width), lambda j, s_ref: (0, 0))

    outs = [jax.ShapeDtypeStruct((fine + 2 * TAIL, half), BF)]
    out_specs = [cols(fine + 2 * TAIL, False)]
    scratch = []
    if ours:
        outs += [jax.ShapeDtypeStruct((fine, half), BF)]
        out_specs += [cols(fine, False)]
    else:
        outs += [jax.ShapeDtypeStruct((4, quarter, half), BF)]
        out_specs += [
            pl.BlockSpec((2, quarter, half), lambda j, s_ref: (jnp.maximum(j - steps, 0), 0, 0))
        ]
        scratch += [pltpu.VMEM((fine, half), BF), pltpu.VMEM((columns, fine), BF)]
    scratch += [
        pltpu.VMEM((4, rows + TAIL, DV), BF),
        pltpu.VMEM((fine + 2 * TAIL, WIDE), F32),
        pltpu.VMEM((steps, rows, WIDE), BF),
        pltpu.VMEM((steps, fine, WIDE), BF),
        pltpu.VMEM((steps, H, DV, WIDE), BF),
        pltpu.SemaphoreType.DMA((3 * steps + 1,)),
    ]
    return pl.pallas_call(
        kernel,
        out_shape=outs,
        grid_spec=pltpu.PrefetchScalarGridSpec(
            num_scalar_prefetch=1,
            grid=(steps if ours else steps + 2,),
            in_specs=[flat(rows + TAIL, 256)] * 4
            + [cols(TAIL, True), cols(TAIL, True), cols(3, True)]
            + [ANY] * 4,
            out_specs=out_specs,
            scratch_shapes=scratch,
        ),
        compiler_params=params(53),
        cost_estimate=pl.CostEstimate(
            flops=2 * fine * columns * columns, bytes_accessed=9 << 20, transcendentals=fine * half
        ),
        name="forward",
    )(scalars, *back, before, after, depth_weight, tokens, skipped, out_heads, turned)


def backward(scalars, theirs, ours, upstream, before, after, point_weight, depth_weight, behind):
    fine, columns = upstream.shape
    half = columns // 2
    steps = half // WIDE

    def kernel(s_ref, theirs_ref, ours_ref, g_ref, low_ref, high_ref, pw_ref, dw_ref, behind_ref, *refs):
        gs_ref, gd_theirs, gd_ours, grad, upper, ends, up_ref = refs
        j = pl.program_id(0)

        @pl.when(j < steps)
        def _():
            up_ref[...] = theirs_ref[...]

        @pl.when(j >= steps)
        def _():
            up_ref[...] = ours_ref[...]

        dims = (((1,), (1,)), ((), ()))

        @pl.when(pl.program_id(0) == 0)
        def _():
            row = lax.broadcasted_iota(jnp.int32, (TAIL, columns), 0)
            low, high = low_ref[...].astype(F32), high_ref[...].astype(F32)
            ends[...] = jnp.where(row == 7, low[3:4], jnp.where(row == 8, high[3:4], 0.0)).astype(BF)

        upper[...] = lax.dot_general(g_ref[...], pw_ref[...], dims, preferred_element_type=F32)
        outer = lax.dot_general(ends[...], pw_ref[...], dims, preferred_element_type=F32)
        w = [dw_ref[t : t + 1, :] for t in range(3)]

        def grad_of(near, start, count, coming):
            taps = [near[start - 1 + t : start - 1 + t + count] for t in range(3)]
            pre = w[0] * taps[0] + w[1] * taps[1] + w[2] * taps[2]
            bend, square, slope = gelu_parts(pre)
            rate = 0.5 + 0.5 * bend + (pre * (1.0 - bend * bend)) * (
                0.5 * slope + (1.5 * slope * 0.044715) * square
            )
            return taps, (coming * rate).astype(BF).astype(F32)

        _, grad[8:16, :] = grad_of(up_ref[:32, :].astype(F32), 8, 8, outer[:8])
        _, grad[16 + fine : 24 + fine, :] = grad_of(up_ref[fine:, :].astype(F32), 16, 8, outer[8:])
        sums = [jnp.zeros((8, WIDE), F32)] * 3
        for k in range(0, fine, STRIP):
            near = up_ref[k : k + STRIP + 2 * TAIL, :].astype(F32)
            taps, mid = grad_of(near, TAIL, STRIP, upper[k : k + STRIP, :])
            grad[16 + k : 16 + k + STRIP, :] = mid
            for t in range(3):
                term = taps[t] * mid
                for r in range(0, STRIP, 8):
                    sums[t] = sums[t] + term[r : r + 8]
        depth = [jnp.sum(total, axis=0, keepdims=True) for total in sums]
        for ref, mine in ((gd_theirs, j < steps), (gd_ours, j >= steps)):

            @pl.when(mine)
            def _():
                for t in range(3):
                    ref[t : t + 1, :] = depth[t]

        for k in range(0, fine, STRIP):
            near = grad[8 + k : 24 + k + STRIP, :]
            gs_ref[k : k + STRIP, :] = (
                w[0] * near[9 : 9 + STRIP] + w[1] * near[8 : 8 + STRIP] + w[2] * near[7 : 7 + STRIP]
            ).astype(BF)

    def block(j, s_ref):
        return jnp.where(j < steps, (1 - s_ref[1]) * steps + j, s_ref[1] * steps + j - steps)

    def cols(count):
        return pl.BlockSpec((count, WIDE), lambda j, s_ref: (0, block(j, s_ref)))

    def early(count):
        return pl.BlockSpec((count, WIDE), lambda j, s_ref: (0, jnp.minimum(j, steps - 1)))

    def late(count):
        return pl.BlockSpec((count, WIDE), lambda j, s_ref: (0, jnp.maximum(j - steps, 0)))

    def flat(count):
        return pl.BlockSpec((count, columns), lambda j, s_ref: (0, 0))

    return pl.pallas_call(
        kernel,
        out_shape=[
            jax.ShapeDtypeStruct((fine, columns), BF),
            jax.ShapeDtypeStruct((3, half), F32),
            jax.ShapeDtypeStruct((3, half), F32),
        ],
        grid_spec=pltpu.PrefetchScalarGridSpec(
            num_scalar_prefetch=1,
            grid=(2 * steps,),
            in_specs=[
                early(fine + 2 * TAIL),
                late(fine + 2 * TAIL),
                flat(fine),
                flat(TAIL),
                flat(TAIL),
                pl.BlockSpec((WIDE, columns), lambda j, s_ref: (block(j, s_ref), 0)),
                cols(3),
                ANY,
            ],
            out_specs=[cols(fine), early(3), late(3)],
            scratch_shapes=[
                pltpu.VMEM((fine + 2 * TAIL, WIDE), F32),
                pltpu.VMEM((fine, WIDE), F32),
                pltpu.VMEM((TAIL, columns), BF),
                pltpu.VMEM((fine + 2 * TAIL, WIDE), BF),
            ],
        ),
        compiler_params=params(48),
        cost_estimate=pl.CostEstimate(
            flops=2 * fine * columns * columns, bytes_accessed=11 << 20, transcendentals=fine * columns
        ),
        name="backward",
    )(scalars, theirs, ours, upstream, before, after, point_weight, depth_weight, behind)


def product(scalars, act, turned, steps, arrived):
    half, quarter = act.shape[1], turned.shape[0] // 4

    def kernel(s_ref, a_ref, g_ref, arrived_ref, *outs):
        for out, d in zip(outs, steps):
            at = pl.multiple_of((Spot(s_ref).first_at + d) % 4 * quarter, 16)
            block = jnp.dot(g_ref[pl.ds(at, quarter), :], a_ref[...], preferred_element_type=F32)
            out[...] = (block + arrived_ref[d].astype(F32)).astype(BF)

    return pl.pallas_call(
        kernel,
        out_shape=[jax.ShapeDtypeStruct((quarter, half), BF)] * len(steps),
        in_specs=[SMEM] + [VMEM] * 3,
        out_specs=[VMEM] * len(steps),
        compiler_params=params(14),
        cost_estimate=pl.CostEstimate(
            flops=2 * act.shape[0] * half * quarter * len(steps), bytes_accessed=6 << 20, transcendentals=0
        ),
        name="product",
    )(scalars, act, turned, arrived)


def split_rows(at, got):
    rows, columns = got[0].shape
    slim = rows // 4

    def kernel(at_ref, *refs):
        ins, outs = refs[:4], refs[4:]
        for d in range(4):
            take = pl.ds(pl.multiple_of((Spot(at_ref).second_at + d) % 4 * slim, 16), slim)
            outs[d][...] = total_of([r[take, :] for r in ins]).astype(BF)

    return pl.pallas_call(
        kernel,
        out_shape=[jax.ShapeDtypeStruct((slim, columns), BF)] * 4,
        in_specs=[SMEM] + [VMEM] * 4,
        out_specs=[VMEM] * 4,
        compiler_params=params(10),
        name="split_rows",
    )(at, *got)


def join_rows(at, got):
    slim, columns = got[0].shape[0] - TAIL, got[0].shape[1]
    quarter = 4 * slim

    def kernel(at_ref, *refs):
        ins, out, held = refs[:4], refs[4], refs[5]
        for d in range(4):
            put = pl.ds(pl.multiple_of((Spot(at_ref).second_at + 4 - d) % 4 * slim, 16), slim)
            held[put, :] = ins[d][:slim, :]
        out[:columns, :] = held[...].T
        last = total_of([r[slim:, :] for r in ins])[:8]
        out[columns:, :] = jnp.concatenate([last[:, :quarter], last[:, quarter:]], axis=0).astype(BF)

    return pl.pallas_call(
        kernel,
        out_shape=jax.ShapeDtypeStruct((columns + TAIL, quarter), BF),
        in_specs=[SMEM] + [VMEM] * 4,
        out_specs=VMEM,
        scratch_shapes=[pltpu.VMEM((quarter, columns), BF)],
        compiler_params=params(10),
        name="join_rows",
    )(at, *got)


def lay_out(scalars, own, other):
    part, quarter = own[3].shape
    half = 2 * part

    def kernel(s_ref, *refs):
        out, sems = refs[-2:]
        spot = Spot(s_ref)
        copies = []
        for n in range(10):
            mine = n < 5
            d, start, count = ((0, 0, half), (1, 0, half), (3, 0, half), (2, 0, part), (2, part, part))[n % 5]
            down = (spot.core if mine else 1 - spot.core) * half + start
            over = ((spot.first_at if mine else spot.their_first) + 4 - d) % 4 * quarter
            copies.append(
                pltpu.make_async_copy(
                    refs[n].at[pl.ds(0, count), :],
                    out.at[pl.ds(pl.multiple_of(down, 16), count), pl.ds(pl.multiple_of(over, 128), quarter)],
                    sems.at[n],
                )
            )
        for copy in copies:
            copy.start()
        for copy in copies:
            copy.wait()

    return pl.pallas_call(
        kernel,
        out_shape=jax.ShapeDtypeStruct((2 * half, 4 * quarter), BF),
        in_specs=[SMEM] + [VMEM] * 10,
        out_specs=ANY,
        scratch_shapes=[pltpu.SemaphoreType.DMA((10,))],
        compiler_params=params(8),
        name="lay_out",
    )(scalars, *own, *other)


def local(
    trunk,
    skip,
    valid_bins,
    query_weight,
    key_weight,
    value_weight,
    out_weight,
    depth_weight,
    point_weight,
    cotangent,
):
    tokens, skipped, upstream = trunk[0], skip[0], cotangent[0]
    rows, columns = tokens.shape
    fine = skipped.shape[0]
    ix, ic, iz, iy = (lax.axis_index(a) for a in AXES)
    scalars = jnp.stack([v.astype(jnp.int32) for v in (ix, ic, iz, iy, valid_bins[0])])
    blocks = project(scalars, tokens, query_weight, key_weight, value_weight)
    down, up = edges(blocks[0], tokens, skipped, upstream)
    before = lax.ppermute(down, ("z", "y"), [(i, i + 1) for i in range(15)])
    after = lax.ppermute(up, ("z", "y"), [(i + 1, i) for i in range(15)])
    q = exchange(blocks, HEAD_RING)
    own = stack_rows(q, down)
    far = {d: lax.ppermute(own, AXES, turn(ROW_RING, d)) for d in (1, 3, 2)}
    state = attend(scalars, 0, q, [own], None)

    turned = upstream.T

    state = attend(scalars, 1, q, [far[1]], state)
    state = attend(scalars, 2, q, [far[3]], state)
    mixed = attend(scalars, 3, q, [own, far[1], far[3], far[2]], state, (before, after))
    back = exchange(mixed, HEAD_RING, -1)
    swap = [(0, 1), (1, 0)]
    given = (back, tokens, skipped, out_weight.reshape(H, DV, -1), before, after, depth_weight, turned)
    up_theirs, sent = forward(scalars, False, *given)
    arrived = lax.ppermute(sent, "c", swap)
    up_ours, act = forward(scalars, True, *given)
    piece_2, piece_1 = product(scalars, act, turned, (2, 1), arrived)
    piece_3, piece_0 = product(scalars, act, turned, (3, 0), arrived)
    got = exchange([piece_0, piece_1, piece_2, piece_3], SUM_RINGS[0])

    grad_skip, d_theirs, d_mine = backward(
        scalars, up_theirs, up_ours, upstream, before, after, point_weight, depth_weight, piece_0
    )
    d_sum = d_mine + lax.ppermute(d_theirs, "c", swap)
    rider = jnp.pad(d_sum.astype(BF), ((0, TAIL - 3), (0, 0)))

    got = exchange(split_rows(scalars, got), SUM_RINGS[1])
    mixed = jnp.concatenate([total_of(got).astype(BF), rider], axis=0)
    got = exchange([mixed] * 4, SUM_RINGS[2])
    norm_scale = 1.0 / math.sqrt(128 * fine)
    summed = (total_of(got) * norm_scale).astype(BF)
    joined = join_rows(scalars, exchange([summed] * 4, SUM_RINGS[1]))

    def go(block, step):
        return lax.ppermute(block, AXES, turn(SUM_RINGS[0], step))

    half, part = columns // 2, columns // 4
    one, three = go(joined, 1), go(joined, 3)
    own = [joined, one, three, go(one[:part], 1), go(three[part:], 3)]
    other = [lax.ppermute(p, "c", swap) for p in own]
    grad_pointwise = lay_out(scalars, own, other)

    def depth_of(blocks):
        rows = total_of([blocks[0][half:], blocks[1][half:], blocks[4][part:], blocks[2][half:]])
        return jnp.concatenate([rows[:3], rows[8:11]], axis=1)

    d_own, d_other = depth_of(own), depth_of(other)
    grad_depth = jnp.concatenate(
        [jnp.where(ic == 0, d_own, d_other), jnp.where(ic == 0, d_other, d_own)], axis=1
    )
    return (grad_pointwise, grad_depth, grad_skip[None])


def solution(mesh):
    fine_mesh = Mesh(mesh.devices.reshape(SIZES), AXES)
    rows = P(("x", "c"), ("z", "y"), None)
    return jax.shard_map(
        local,
        mesh=fine_mesh,
        in_specs=(rows, rows, P(("x", "c")), P(), P(), P(), P(), P(), P(), rows),
        out_specs=(P(), P(), rows),
        check_vma=False,
    )
```

```python
import math

import jax
import jax.numpy as jnp
from jax import lax
from jax.experimental import pallas as pl
from jax.experimental.pallas import tpu as pltpu
from jax.sharding import Mesh, PartitionSpec as P

H = 4
DH = 64
DV = 192
AXES = ("x", "c", "z", "y")
SIZES = (4, 2, 4, 4)
BF = jnp.bfloat16
F32 = jnp.float32
TAIL = 16
VMEM = pl.BlockSpec(memory_space=pltpu.VMEM)
SMEM = pl.BlockSpec(memory_space=pltpu.SMEM)
ANY = pl.BlockSpec(memory_space=pl.ANY)
SUM_RINGS = (("x", "y"), ("y", "z"), ("z", "x"))
HEAD_RING = ("y", "z")
ROW_RING = ("z", "y")


class Spot:
    def __init__(self, s_ref):
        x, core, z, y = (s_ref[n] for n in range(4))
        first = core == 0
        self.core, self.y = core, y
        self.head_at = jnp.where(first, y, z)
        self.row_at = jnp.where(first, z, y)
        self.first_at = jnp.where(first, x, y)
        self.their_first = jnp.where(first, y, x)
        self.second_at = jnp.where(first, y, z)
        self.place = z * 4 + y

    def base(self, far_by, d):
        h, r = (self.head_at + 4 - d) % 4, (self.row_at + 4 - far_by) % 4
        return jnp.where(self.core == 0, r * 4 + h, h * 4 + r)

    def ring_place(self, d):
        return jnp.where(self.core == 0, (self.y + 4 - d) % 4, self.y)


def params(mib):
    return pltpu.CompilerParams(vmem_limit_bytes=mib << 20)


def turn(axes, step):
    pairs = []
    for x in range(4):
        for c in range(2):
            for z in range(4):
                for y in range(4):
                    at = {"x": x, "z": z, "y": y}
                    to = dict(at)
                    to[axes[c]] = (at[axes[c]] + step) % 4
                    flat = [((p["x"] * 2 + c) * 4 + p["z"]) * 4 + p["y"] for p in (at, to)]
                    pairs.append(tuple(flat))
    return pairs


def exchange(pieces, axes, sign=1):
    got = [pieces[0], None, None, None]
    for d in (2, 1, 3):
        got[d] = lax.ppermute(pieces[d], AXES, turn(axes, sign * d))
    return got


def total_of(got):
    a, b, c, d = (g.astype(F32) for g in got)
    return (a + c) + (b + d)


def project(at, tokens, query_weight, key_weight, value_weight):
    rows, depth = tokens.shape
    cut = depth // 2

    def kernel(at_ref, tok_hbm, wq_hbm, wk_hbm, wv_hbm, *refs):
        outs, (tok_ref, wq_ref, wk_ref, wv_ref, held, sems) = refs[:4], refs[4:]
        low, high = pl.ds(0, cut), pl.ds(cut, depth - cut)
        copies = [
            pltpu.make_async_copy(tok_hbm, tok_ref, sems.at[0]),
            pltpu.make_async_copy(wv_hbm.at[low, :], wv_ref.at[low, :], sems.at[1]),
            pltpu.make_async_copy(wv_hbm.at[high, :], wv_ref.at[high, :], sems.at[2]),
            pltpu.make_async_copy(wk_hbm, wk_ref, sems.at[3]),
            pltpu.make_async_copy(wq_hbm, wq_ref, sems.at[4]),
        ]
        for copy in copies:
            copy.start()
        copies[0].wait()
        tok = tok_ref[...]
        copies[1].wait()
        v = jnp.dot(tok[:, :cut], wv_ref[:cut, :], preferred_element_type=F32)
        copies[2].wait()
        v += jnp.dot(tok[:, cut:], wv_ref[cut:, :], preferred_element_type=F32)
        copies[3].wait()
        k = jnp.dot(tok, wk_ref[...], preferred_element_type=F32)
        copies[4].wait()
        q = jnp.dot(tok, wq_ref[...], preferred_element_type=F32) * (1.0 / math.sqrt(DH))
        zero = jnp.zeros((rows, DH), F32)
        for h in range(H):
            held[h] = jnp.concatenate(
                [
                    v[:, h * DV : (h + 1) * DV],
                    k[:, h * DH : (h + 1) * DH],
                    zero,
                    q[:, h * DH : (h + 1) * DH],
                ],
                axis=1,
            ).astype(BF)
        for d in range(4):
            outs[d][...] = held[(Spot(at_ref).head_at + d) % 4]

    return pl.pallas_call(
        kernel,
        out_shape=[jax.ShapeDtypeStruct((rows, 384), BF)] * 4,
        in_specs=[SMEM] + [ANY] * 4,
        out_specs=[VMEM] * 4,
        scratch_shapes=[
            pltpu.VMEM((rows, depth), BF),
            pltpu.VMEM((depth, H * DH), BF),
            pltpu.VMEM((depth, H * DH), BF),
            pltpu.VMEM((depth, H * DV), BF),
            pltpu.VMEM((4, rows, 384), BF),
            pltpu.SemaphoreType.DMA((5,)),
        ],
        compiler_params=params(53),
        name="project",
    )(at, tokens, query_weight, key_weight, value_weight)


def stack_rows(parts, behind):
    rows = parts[0].shape[0]

    def kernel(*refs):
        ins, out = refs[:4], refs[5]
        row = lax.broadcasted_iota(jnp.int32, (TAIL, 128), 0)
        tail = jnp.zeros((TAIL, 128), F32)
        for d in range(4):
            out[d * rows : (d + 1) * rows, :] = ins[d][:, :256]
            first = ins[d][:TAIL, 256:].astype(F32)[:1]
            final = ins[d][rows - TAIL :, 256:].astype(F32)[TAIL - 1 :]
            tail = jnp.where(row == d, first, tail)
            tail = jnp.where(row == 4 + d, final, tail)
        out[4 * rows :, :128] = jnp.zeros((TAIL, 128), BF)
        out[4 * rows :, 128:] = tail.astype(BF)

    return pl.pallas_call(
        kernel,
        out_shape=jax.ShapeDtypeStruct((4 * rows + TAIL, 256), BF),
        in_specs=[VMEM] * 4 + [ANY],
        out_specs=VMEM,
        compiler_params=params(8),
        name="stack_rows",
    )(*parts, behind)


def attend(scalars, near, q, pairs, state, behind=()):
    rows = q[0].shape[0]
    width = 4 * rows
    first = state is None
    last = len(pairs) == 4
    strip = 32

    def kernel(s_ref, *refs):
        spot = Spot(s_ref)
        score_ref, prob_ref, peak_ref = refs[-3:]
        q_refs, refs = refs[:4], refs[4:]
        pair_refs, refs = refs[: len(pairs)], refs[len(pairs) :]
        if not first:
            old, old_peak, refs = refs[0], refs[1], refs[2:]
        refs = refs[len(behind) :]
        lane = lax.broadcasted_iota(jnp.int32, (width, 256), 1)
        place = lax.broadcasted_iota(jnp.int32, (1, rows), 1)

        def masks(n):
            far_by = (0, 1, 3, 2)[n]
            return jnp.concatenate(
                [place + spot.base(far_by, i) * rows < s_ref[4] for i in range(4)], axis=1
            )

        def values_of(ref):
            return jnp.where(lane == DV, jnp.ones((), BF), ref[:width, :])

        def raw_scores(query, ref):
            return lax.dot_general(
                query, ref[:width, 128:], (((1,), (1,)), ((), ())), preferred_element_type=F32
            )

        def shares(sums):
            return sums / sums[:, DV : DV + 1]

        if last:
            tails = [r[width:, 128:].astype(F32) for r in pair_refs]
            own, low, high = tails[0], tails[1], tails[2]
            row = lax.broadcasted_iota(jnp.int32, (TAIL, 128), 0)
            edge = jnp.zeros((TAIL, 128), F32)
            for d in range(4):
                n, m = (d + 1) % 4, (d + 3) % 4
                at = spot.ring_place(d)
                other = jnp.where(spot.core == 0, own[4 + n : 5 + n], low[4 + d : 5 + d])
                prev = jnp.where(at == 0, low[4 + n : 5 + n], other)
                other = jnp.where(spot.core == 0, own[m : m + 1], high[d : d + 1])
                nxt = jnp.where(at == 3, high[m : m + 1], other)
                edge = jnp.where(row == d, prev, edge)
                edge = jnp.where(row == 4 + d, nxt, edge)
            edge = edge.astype(BF)
            parts = [jnp.where(masks(n), raw_scores(edge, r), -1e30) for n, r in enumerate(pair_refs)]
            peak = jnp.max(parts[0], axis=1, keepdims=True)
            for s in parts[1:]:
                peak = jnp.maximum(peak, jnp.max(s, axis=1, keepdims=True))
            edge_sums = jnp.zeros((TAIL, 256), F32)
            for s, r in zip(parts, pair_refs):
                edge_sums += jnp.dot(jnp.exp(s - peak).astype(BF), values_of(r), preferred_element_type=F32)
            edge_out = shares(edge_sums)
            row = lax.broadcasted_iota(jnp.int32, (TAIL, 256), 0)

        pair_ref = pair_refs[-1]
        keep = masks(near)
        values = values_of(pair_ref)
        for i in range(4):
            score_ref[i] = raw_scores(q_refs[i][:, 256:], pair_ref)
        for i in range(4):
            for k in range(0, rows, strip):
                cut = slice(k, k + strip)
                scores = jnp.where(keep, score_ref[i, cut, :], -1e30)
                peak = jnp.broadcast_to(jnp.max(scores, axis=1, keepdims=True), (strip, 128))
                if not first:
                    peak = jnp.maximum(peak, old_peak[i * rows + k : i * rows + k + strip, :])
                across = jnp.concatenate([peak] * (width // 128), axis=1)
                prob_ref[i, cut, :] = jnp.exp(scores - across).astype(BF)
                peak_ref[i, cut, :] = peak
            update = jnp.dot(prob_ref[i], values, preferred_element_type=F32)
            if not first:
                shrink = jnp.exp(old_peak[i * rows : (i + 1) * rows, :] - peak_ref[i])
                update = update + old[i * rows : (i + 1) * rows, :] * jnp.concatenate([shrink] * 2, axis=1)
            if last:
                refs[i][:rows, :] = shares(update).astype(BF)
                ends = jnp.where(row == 0, edge_out[i : i + 1], jnp.zeros((TAIL, 256), F32))
                ends = jnp.where(row == 1, edge_out[4 + i : 5 + i], ends)
                refs[i][rows:, :] = ends.astype(BF)
            else:
                refs[0][i * rows : (i + 1) * rows, :] = update
                refs[1][i * rows : (i + 1) * rows, :] = peak_ref[i]

    ins = [*q, *pairs]
    if not first:
        ins += [*state]
    if last:
        outs = [jax.ShapeDtypeStruct((rows + TAIL, 256), BF)] * 4
    else:
        outs = [jax.ShapeDtypeStruct((4 * rows, n), F32) for n in (256, 128)]
    return pl.pallas_call(
        kernel,
        out_shape=outs,
        in_specs=[SMEM] + [VMEM] * len(ins) + [ANY] * len(behind),
        out_specs=[VMEM] * len(outs),
        scratch_shapes=[
            pltpu.VMEM((4, rows, width), F32),
            pltpu.VMEM((4, rows, width), BF),
            pltpu.VMEM((4, rows, 128), F32),
        ],
        compiler_params=params(24),
        cost_estimate=pl.CostEstimate(
            flops=4 * 2 * rows * width * 512, bytes_accessed=4 << 20, transcendentals=4 * rows * width
        ),
        name="attend",
    )(scalars, *ins, *behind)


def edges(mark, trunk, skip, cotangent):
    columns = trunk.shape[1]

    def kernel(mark_ref, t_ref, s_ref, c_ref, down, up, buffer, sems):
        copies = []
        for n, ref in enumerate((t_ref, s_ref, c_ref)):
            for end in range(2):
                start = end * (ref.shape[0] - TAIL)
                copies.append(
                    pltpu.make_async_copy(
                        ref.at[pl.ds(start, TAIL), :], buffer.at[2 * n + end], sems.at[2 * n + end]
                    )
                )
        for copy in copies:
            copy.start()
        for copy in copies:
            copy.wait()
        t_first, t_last, s_first, s_last, c_first, c_last = (buffer[n].astype(F32) for n in range(6))
        row = lax.broadcasted_iota(jnp.int32, (TAIL, columns), 0)

        def four(a, b, c, d):
            rest = jnp.where(row == 2, c, jnp.where(row == 3, d, 0.0))
            return jnp.where(row == 0, a, jnp.where(row == 1, b, rest)).astype(BF)

        up[...] = four(t_first[:1], s_first[:1], s_first[1:2], c_first[:1])
        e = TAIL - 1
        down[...] = four(t_last[e:], s_last[e - 1 : e], s_last[e:], c_last[e:])

    return pl.pallas_call(
        kernel,
        out_shape=[jax.ShapeDtypeStruct((TAIL, columns), BF)] * 2,
        in_specs=[ANY] * 4,
        out_specs=[VMEM] * 2,
        scratch_shapes=[pltpu.VMEM((6, TAIL, columns), BF), pltpu.SemaphoreType.DMA((6,))],
        compiler_params=params(53),
        name="edges",
    )(mark, trunk, skip, cotangent)


def gelu_parts(pre):
    slope = math.sqrt(2.0 / math.pi)
    square = pre * pre
    bend = jnp.tanh(slope * (pre + 0.044715 * (square * pre)))
    return bend, square, slope


WIDE = 384
STRIP = 32


def forward(scalars, ours, back, tokens, skipped, out_heads, before, after, depth_weight, turned):
    rows, columns = tokens.shape
    fine = 2 * rows
    half = columns // 2
    steps = half // WIDE
    quarter = columns // 4

    def side(s_ref):
        return s_ref[1] if ours else 1 - s_ref[1]

    def kernel(s_ref, b0, b1, b2, b3, low_ref, high_ref, dw_ref, tok_ref, skip_ref, ow_ref, g_ref, *refs):
        if ours:
            up_ref, act_ref = refs[:2]
            refs = refs[2:]
        else:
            up_ref, prod_ref, act_ref = refs[:3]
            refs = refs[3:]
        att, held = refs
        j = pl.program_id(0)

        @pl.when(j == 0)
        def _():
            mixed = [b[:, :DV].astype(F32) for b in (b0, b1, b2, b3)]
            squares = sum(jnp.sum(m * m, axis=1, keepdims=True) for m in mixed)
            scale = lax.rsqrt(squares * (1.0 / (H * DV)) + 1e-05)
            for d in range(4):
                att[d] = (mixed[d] * scale).astype(BF)

        @pl.when(j < steps)
        def _():
            spot = Spot(s_ref)
            n = jnp.minimum(j, steps - 1)
            take = pl.ds(pl.multiple_of((side(s_ref) * steps + n) * WIDE, 128), WIDE)
            low, high = low_ref[...].astype(F32), high_ref[...].astype(F32)
            grown = jnp.zeros((rows + TAIL, WIDE), F32)
            for d in range(4):
                grown += jnp.dot(att[d], ow_ref[(spot.head_at + d) % 4, :, take], preferred_element_type=F32)
            hidden = (tok_ref[:, take].astype(F32) + grown[:rows]).astype(BF)
            low_hid = (low[:1] + grown[rows : rows + 1]).astype(BF).astype(F32)
            high_hid = (high[:1] + grown[rows + 1 : rows + 2]).astype(BF).astype(F32)
            twice = lax.broadcasted_iota(jnp.int32, (fine, rows), 0) // 2
            twice = jnp.where(twice == lax.broadcasted_iota(jnp.int32, (fine, rows), 1), 1.0, 0.0).astype(BF)
            doubled = jnp.dot(twice, hidden, preferred_element_type=F32)
            row = lax.broadcasted_iota(jnp.int32, (TAIL, WIDE), 0)
            edge = (low_hid + jnp.where(row == 14, low[1:2], low[2:3])).astype(BF).astype(F32)
            edge = jnp.where((row >= 14) & (spot.place > 0), edge, 0.0)
            held[:TAIL, :] = edge
            up_ref[:TAIL, :] = edge.astype(BF)
            edge = (high_hid + jnp.where(row == 0, high[1:2], high[2:3])).astype(BF).astype(F32)
            edge = jnp.where((row < 2) & (spot.place < 15), edge, 0.0)
            held[TAIL + fine :, :] = edge
            up_ref[TAIL + fine :, :] = edge.astype(BF)
            for k in range(0, fine, STRIP):
                up = (doubled[k : k + STRIP] + skip_ref[k : k + STRIP, take].astype(F32)).astype(BF)
                up_ref[TAIL + k : TAIL + k + STRIP, :] = up
                held[TAIL + k : TAIL + k + STRIP, :] = up.astype(F32)
            w = [dw_ref[t : t + 1, :] for t in range(3)]
            cut = pl.ds(0 if ours else pl.multiple_of(n * WIDE, 128), WIDE)
            for k in range(0, fine, STRIP):
                near = held[8 + k : 24 + k + STRIP, :]
                pre = w[0] * near[7 : 7 + STRIP] + w[1] * near[8 : 8 + STRIP] + w[2] * near[9 : 9 + STRIP]
                bend, _, _ = gelu_parts(pre)
                act_ref[k : k + STRIP, cut] = (pre * (0.5 + 0.5 * bend)).astype(BF)

        if not ours:

            @pl.when(j >= steps)
            def _():
                for n in range(2):
                    at = pl.multiple_of((Spot(s_ref).their_first + 2 * (j - steps) + n) % 4 * quarter, 16)
                    prod_ref[n] = jnp.dot(
                        g_ref[pl.ds(at, quarter), :], act_ref[...], preferred_element_type=F32
                    ).astype(BF)

    def cols(count, full):
        def place(j, s_ref):
            n = jnp.minimum(j, steps - 1)
            return 0, (side(s_ref) * steps + n if full else n)

        return pl.BlockSpec((count, WIDE), place)

    def flat(count, width):
        return pl.BlockSpec((count, width), lambda j, s_ref: (0, 0))

    outs = [jax.ShapeDtypeStruct((fine + 2 * TAIL, half), BF)]
    out_specs = [cols(fine + 2 * TAIL, False)]
    scratch = []
    if ours:
        outs += [jax.ShapeDtypeStruct((fine, half), BF)]
        out_specs += [cols(fine, False)]
    else:
        outs += [jax.ShapeDtypeStruct((4, quarter, half), BF)]
        out_specs += [
            pl.BlockSpec((2, quarter, half), lambda j, s_ref: (jnp.maximum(j - steps, 0), 0, 0))
        ]
        scratch += [pltpu.VMEM((fine, half), BF)]
    scratch += [
        pltpu.VMEM((4, rows + TAIL, DV), BF),
        pltpu.VMEM((fine + 2 * TAIL, WIDE), F32),
    ]
    return pl.pallas_call(
        kernel,
        out_shape=outs,
        grid_spec=pltpu.PrefetchScalarGridSpec(
            num_scalar_prefetch=1,
            grid=(steps if ours else steps + 2,),
            in_specs=[flat(rows + TAIL, 256)] * 4
            + [cols(TAIL, True), cols(TAIL, True), cols(3, True)]
            + [VMEM] * 4,
            out_specs=out_specs,
            scratch_shapes=scratch,
        ),
        compiler_params=params(24),
        cost_estimate=pl.CostEstimate(
            flops=2 * fine * columns * columns, bytes_accessed=9 << 20, transcendentals=fine * half
        ),
        name="forward",
    )(scalars, *back, before, after, depth_weight, tokens, skipped, out_heads, turned)


def load(behind, *arrays):
    count = len(arrays)

    def kernel(behind_ref, *refs):
        sems = refs[-1]
        copies = [pltpu.make_async_copy(refs[n], refs[count + n], sems.at[n]) for n in range(count)]
        for copy in copies:
            copy.start()
        for copy in copies:
            copy.wait()

    return pl.pallas_call(
        kernel,
        out_shape=[jax.ShapeDtypeStruct(a.shape, a.dtype) for a in arrays],
        in_specs=[ANY] * (1 + count),
        out_specs=[VMEM] * count,
        scratch_shapes=[pltpu.SemaphoreType.DMA((count,))],
        compiler_params=params(45),
        name="load",
    )(behind, *arrays)


def backward(scalars, theirs, ours, upstream, before, after, point_weight, depth_weight, behind):
    fine, columns = upstream.shape
    half = columns // 2
    steps = half // WIDE

    def kernel(s_ref, theirs_ref, ours_ref, g_ref, low_ref, high_ref, pw_ref, dw_ref, behind_ref, *refs):
        gs_ref, gd_theirs, gd_ours, grad, upper, ends, up_ref = refs
        j = pl.program_id(0)

        @pl.when(j < steps)
        def _():
            up_ref[...] = theirs_ref[...]

        @pl.when(j >= steps)
        def _():
            up_ref[...] = ours_ref[...]

        dims = (((1,), (1,)), ((), ()))

        @pl.when(pl.program_id(0) == 0)
        def _():
            row = lax.broadcasted_iota(jnp.int32, (TAIL, columns), 0)
            low, high = low_ref[...].astype(F32), high_ref[...].astype(F32)
            ends[...] = jnp.where(row == 7, low[3:4], jnp.where(row == 8, high[3:4], 0.0)).astype(BF)

        upper[...] = lax.dot_general(g_ref[...], pw_ref[...], dims, preferred_element_type=F32)
        outer = lax.dot_general(ends[...], pw_ref[...], dims, preferred_element_type=F32)
        w = [dw_ref[t : t + 1, :] for t in range(3)]

        def grad_of(near, start, count, coming):
            taps = [near[start - 1 + t : start - 1 + t + count] for t in range(3)]
            pre = w[0] * taps[0] + w[1] * taps[1] + w[2] * taps[2]
            bend, square, slope = gelu_parts(pre)
            rate = 0.5 + 0.5 * bend + (pre * (1.0 - bend * bend)) * (
                0.5 * slope + (1.5 * slope * 0.044715) * square
            )
            return taps, (coming * rate).astype(BF).astype(F32)

        _, grad[8:16, :] = grad_of(up_ref[:32, :].astype(F32), 8, 8, outer[:8])
        _, grad[16 + fine : 24 + fine, :] = grad_of(up_ref[fine:, :].astype(F32), 16, 8, outer[8:])
        sums = [jnp.zeros((8, WIDE), F32)] * 3
        for k in range(0, fine, STRIP):
            near = up_ref[k : k + STRIP + 2 * TAIL, :].astype(F32)
            taps, mid = grad_of(near, TAIL, STRIP, upper[k : k + STRIP, :])
            grad[16 + k : 16 + k + STRIP, :] = mid
            for t in range(3):
                term = taps[t] * mid
                for r in range(0, STRIP, 8):
                    sums[t] = sums[t] + term[r : r + 8]
        depth = [jnp.sum(total, axis=0, keepdims=True) for total in sums]
        for ref, mine in ((gd_theirs, j < steps), (gd_ours, j >= steps)):

            @pl.when(mine)
            def _():
                for t in range(3):
                    ref[t : t + 1, :] = depth[t]

        for k in range(0, fine, STRIP):
            near = grad[8 + k : 24 + k + STRIP, :]
            gs_ref[k : k + STRIP, :] = (
                w[0] * near[9 : 9 + STRIP] + w[1] * near[8 : 8 + STRIP] + w[2] * near[7 : 7 + STRIP]
            ).astype(BF)

    def block(j, s_ref):
        return jnp.where(j < steps, (1 - s_ref[1]) * steps + j, s_ref[1] * steps + j - steps)

    def cols(count):
        return pl.BlockSpec((count, WIDE), lambda j, s_ref: (0, block(j, s_ref)))

    def early(count):
        return pl.BlockSpec((count, WIDE), lambda j, s_ref: (0, jnp.minimum(j, steps - 1)))

    def late(count):
        return pl.BlockSpec((count, WIDE), lambda j, s_ref: (0, jnp.maximum(j - steps, 0)))

    def flat(count):
        return pl.BlockSpec((count, columns), lambda j, s_ref: (0, 0))

    return pl.pallas_call(
        kernel,
        out_shape=[
            jax.ShapeDtypeStruct((fine, columns), BF),
            jax.ShapeDtypeStruct((3, half), F32),
            jax.ShapeDtypeStruct((3, half), F32),
        ],
        grid_spec=pltpu.PrefetchScalarGridSpec(
            num_scalar_prefetch=1,
            grid=(2 * steps,),
            in_specs=[
                early(fine + 2 * TAIL),
                late(fine + 2 * TAIL),
                flat(fine),
                flat(TAIL),
                flat(TAIL),
                pl.BlockSpec((WIDE, columns), lambda j, s_ref: (block(j, s_ref), 0)),
                cols(3),
                ANY,
            ],
            out_specs=[cols(fine), early(3), late(3)],
            scratch_shapes=[
                pltpu.VMEM((fine + 2 * TAIL, WIDE), F32),
                pltpu.VMEM((fine, WIDE), F32),
                pltpu.VMEM((TAIL, columns), BF),
                pltpu.VMEM((fine + 2 * TAIL, WIDE), BF),
            ],
        ),
        compiler_params=params(48),
        cost_estimate=pl.CostEstimate(
            flops=2 * fine * columns * columns, bytes_accessed=11 << 20, transcendentals=fine * columns
        ),
        name="backward",
    )(scalars, theirs, ours, upstream, before, after, point_weight, depth_weight, behind)


def product(scalars, act, turned, steps, arrived):
    half, quarter = act.shape[1], turned.shape[0] // 4

    def kernel(s_ref, a_ref, g_ref, arrived_ref, *outs):
        for out, d in zip(outs, steps):
            at = pl.multiple_of((Spot(s_ref).first_at + d) % 4 * quarter, 16)
            block = jnp.dot(g_ref[pl.ds(at, quarter), :], a_ref[...], preferred_element_type=F32)
            out[...] = (block + arrived_ref[d].astype(F32)).astype(BF)

    return pl.pallas_call(
        kernel,
        out_shape=[jax.ShapeDtypeStruct((quarter, half), BF)] * len(steps),
        in_specs=[SMEM] + [VMEM] * 3,
        out_specs=[VMEM] * len(steps),
        compiler_params=params(14),
        cost_estimate=pl.CostEstimate(
            flops=2 * act.shape[0] * half * quarter * len(steps), bytes_accessed=6 << 20, transcendentals=0
        ),
        name="product",
    )(scalars, act, turned, arrived)


def split_rows(at, got):
    rows, columns = got[0].shape
    slim = rows // 4

    def kernel(at_ref, *refs):
        ins, outs = refs[:4], refs[4:]
        for d in range(4):
            take = pl.ds(pl.multiple_of((Spot(at_ref).second_at + d) % 4 * slim, 16), slim)
            outs[d][...] = total_of([r[take, :] for r in ins]).astype(BF)

    return pl.pallas_call(
        kernel,
        out_shape=[jax.ShapeDtypeStruct((slim, columns), BF)] * 4,
        in_specs=[SMEM] + [VMEM] * 4,
        out_specs=[VMEM] * 4,
        compiler_params=params(10),
        name="split_rows",
    )(at, *got)


def join_rows(at, got):
    slim, columns = got[0].shape[0] - TAIL, got[0].shape[1]
    quarter = 4 * slim

    def kernel(at_ref, *refs):
        ins, out, held = refs[:4], refs[4], refs[5]
        for d in range(4):
            put = pl.ds(pl.multiple_of((Spot(at_ref).second_at + 4 - d) % 4 * slim, 16), slim)
            held[put, :] = ins[d][:slim, :]
        out[:columns, :] = held[...].T
        last = total_of([r[slim:, :] for r in ins])[:8]
        out[columns:, :] = jnp.concatenate([last[:, :quarter], last[:, quarter:]], axis=0).astype(BF)

    return pl.pallas_call(
        kernel,
        out_shape=jax.ShapeDtypeStruct((columns + TAIL, quarter), BF),
        in_specs=[SMEM] + [VMEM] * 4,
        out_specs=VMEM,
        scratch_shapes=[pltpu.VMEM((quarter, columns), BF)],
        compiler_params=params(10),
        name="join_rows",
    )(at, *got)


def lay_out(scalars, own, other):
    half, quarter = own[0].shape[0] - TAIL, own[0].shape[1]
    parts = 4
    part = half // parts

    def kernel(s_ref, *refs):
        out, depth, sems = refs[-3:]
        spot = Spot(s_ref)
        copies = []
        for n in range(8):
            mine = n < 4
            down = (spot.core if mine else 1 - spot.core) * half
            over = ((spot.first_at if mine else spot.their_first) + 4 - n % 4) % 4 * quarter
            for k in range(parts):
                start = pl.multiple_of(down + k * part, 16)
                copies.append(
                    pltpu.make_async_copy(
                        refs[n].at[pl.ds(k * part, part), :],
                        out.at[pl.ds(start, part), pl.ds(pl.multiple_of(over, 128), quarter)],
                        sems.at[parts * n + k],
                    )
                )
        for copy in copies:
            copy.start()
        for n, side in ((0, spot.core), (4, 1 - spot.core)):
            rows = total_of([refs[n + d][half:, :] for d in range(4)])
            rows = jnp.concatenate([rows[:3], rows[8:11]], axis=1)
            depth[:, pl.ds(pl.multiple_of(side * half, 128), half)] = rows
        for copy in copies:
            copy.wait()

    return pl.pallas_call(
        kernel,
        out_shape=[
            jax.ShapeDtypeStruct((2 * half, 4 * quarter), BF),
            jax.ShapeDtypeStruct((3, 2 * half), F32),
        ],
        in_specs=[SMEM] + [VMEM] * 8,
        out_specs=[ANY, VMEM],
        scratch_shapes=[pltpu.SemaphoreType.DMA((8 * parts,))],
        compiler_params=params(12),
        name="lay_out",
    )(scalars, *own, *other)


def local(
    trunk,
    skip,
    valid_bins,
    query_weight,
    key_weight,
    value_weight,
    out_weight,
    depth_weight,
    point_weight,
    cotangent,
):
    tokens, skipped, upstream = trunk[0], skip[0], cotangent[0]
    rows, columns = tokens.shape
    fine = skipped.shape[0]
    ix, ic, iz, iy = (lax.axis_index(a) for a in AXES)
    spot = jnp.stack([v.astype(jnp.int32) for v in (ix, ic, iz, iy)])
    scalars = jnp.concatenate([spot, valid_bins.astype(jnp.int32)])
    blocks = project(spot, tokens, query_weight, key_weight, value_weight)
    down, up = edges(blocks[0], tokens, skipped, upstream)
    before = lax.ppermute(down, ("z", "y"), [(i, i + 1) for i in range(15)])
    after = lax.ppermute(up, ("z", "y"), [(i + 1, i) for i in range(15)])
    q = exchange(blocks, HEAD_RING)
    own = stack_rows(q, down)
    far = {d: lax.ppermute(own, AXES, turn(ROW_RING, d)) for d in (1, 3, 2)}
    state = attend(scalars, 0, q, [own], None)

    turned = upstream.T

    state = attend(scalars, 1, q, [far[1]], state)
    state = attend(scalars, 2, q, [far[3]], state)
    mixed = attend(scalars, 3, q, [own, far[1], far[3], far[2]], state, (before, after))
    back = exchange(mixed, HEAD_RING, -1)
    tokens_v, skipped_v, out_v = load(mixed[0], tokens, skipped, out_weight.reshape(H, DV, -1))
    swap = [(0, 1), (1, 0)]
    given = (back, tokens_v, skipped_v, out_v, before, after, depth_weight, turned)
    up_theirs, sent = forward(scalars, False, *given)
    arrived = lax.ppermute(sent, "c", swap)
    up_ours, act = forward(scalars, True, *given)
    piece_2, piece_1 = product(scalars, act, turned, (2, 1), arrived)
    piece_3, piece_0 = product(scalars, act, turned, (3, 0), arrived)
    got = exchange([piece_0, piece_1, piece_2, piece_3], SUM_RINGS[0])

    grad_skip, d_theirs, d_mine = backward(
        scalars, up_theirs, up_ours, upstream, before, after, point_weight, depth_weight, piece_0
    )
    d_sum = d_mine + lax.ppermute(d_theirs, "c", swap)
    rider = jnp.pad(d_sum.astype(BF), ((0, TAIL - 3), (0, 0)))

    got = exchange(split_rows(scalars, got), SUM_RINGS[1])
    mixed = jnp.concatenate([total_of(got).astype(BF), rider], axis=0)
    got = exchange([mixed] * 4, SUM_RINGS[2])
    norm_scale = 1.0 / math.sqrt(128 * fine)
    summed = (total_of(got) * norm_scale).astype(BF)
    joined = join_rows(scalars, exchange([summed] * 4, SUM_RINGS[1]))

    own = exchange([joined] * 4, SUM_RINGS[0])
    other = [lax.ppermute(block, "c", swap) for block in own]
    grad_pointwise, grad_depth = lay_out(scalars, own, other)
    return (grad_pointwise, grad_depth, grad_skip[None])


def solution(mesh):
    fine_mesh = Mesh(mesh.devices.reshape(SIZES), AXES)
    rows = P(("x", "c"), ("z", "y"), None)
    return jax.shard_map(
        local,
        mesh=fine_mesh,
        in_specs=(rows, rows, P(("x", "c")), P(), P(), P(), P(), P(), P(), rows),
        out_specs=(P(), P(), rows),
        check_vma=False,
    )
```

```python
import math

import jax
import jax.numpy as jnp
from jax import lax
from jax.experimental import pallas as pl
from jax.experimental.pallas import tpu as pltpu
from jax.sharding import Mesh, PartitionSpec as P

H = 4
DH = 64
DV = 192
AXES = ("x", "c", "z", "y")
SIZES = (4, 2, 4, 4)
BF = jnp.bfloat16
F32 = jnp.float32
TAIL = 16
VMEM = pl.BlockSpec(memory_space=pltpu.VMEM)
SMEM = pl.BlockSpec(memory_space=pltpu.SMEM)
ANY = pl.BlockSpec(memory_space=pl.ANY)
SUM_RINGS = (("x", "y"), ("y", "z"), ("z", "x"))
HEAD_RING = ("y", "z")
ROW_RING = ("z", "y")


class Spot:
    def __init__(self, s_ref):
        x, core, z, y = (s_ref[n] for n in range(4))
        first = core == 0
        self.core, self.y = core, y
        self.head_at = jnp.where(first, y, z)
        self.row_at = jnp.where(first, z, y)
        self.first_at = jnp.where(first, x, y)
        self.their_first = jnp.where(first, y, x)
        self.second_at = jnp.where(first, y, z)
        self.place = z * 4 + y

    def base(self, far_by, d):
        h, r = (self.head_at + 4 - d) % 4, (self.row_at + 4 - far_by) % 4
        return jnp.where(self.core == 0, r * 4 + h, h * 4 + r)

    def ring_place(self, d):
        return jnp.where(self.core == 0, (self.y + 4 - d) % 4, self.y)


def params(mib):
    return pltpu.CompilerParams(vmem_limit_bytes=mib << 20)


def turn(axes, step):
    pairs = []
    for x in range(4):
        for c in range(2):
            for z in range(4):
                for y in range(4):
                    at = {"x": x, "z": z, "y": y}
                    to = dict(at)
                    to[axes[c]] = (at[axes[c]] + step) % 4
                    flat = [((p["x"] * 2 + c) * 4 + p["z"]) * 4 + p["y"] for p in (at, to)]
                    pairs.append(tuple(flat))
    return pairs


def exchange(pieces, axes, sign=1, order=(2, 1, 3)):
    got = [pieces[0], None, None, None]
    for d in order:
        got[d] = lax.ppermute(pieces[d], AXES, turn(axes, sign * d))
    return got


def total_of(got):
    a, b, c, d = (g.astype(F32) for g in got)
    return (a + c) + (b + d)


def project(at, tokens, query_weight, key_weight, value_weight):
    rows, depth = tokens.shape
    cut = depth // 2

    def kernel(at_ref, tok_hbm, wq_hbm, wk_hbm, wv_hbm, *refs):
        outs, (tok_ref, wq_ref, wk_ref, wv_ref, held, sems) = refs[:4], refs[4:]
        wide = 2 * DV
        cuts = [pl.ds(n * cut, cut) for n in range(2)]
        copies = [pltpu.make_async_copy(tok_hbm, tok_ref, sems.at[0])]
        for w_hbm, w_ref in ((wk_hbm, wk_ref), (wq_hbm, wq_ref)):
            copies += [pltpu.make_async_copy(w_hbm.at[c, :], w_ref.at[c, :], sems.at[len(copies) + n]) for n, c in enumerate(cuts)]
        for n in range(2):
            across = pl.ds(n * wide, wide)
            copies += [
                pltpu.make_async_copy(wv_hbm.at[c, across], wv_ref.at[c, across], sems.at[len(copies) + m])
                for m, c in enumerate(cuts)
            ]
        for copy in copies:
            copy.start()
        for copy in copies[:3]:
            copy.wait()
        tok = tok_ref[...]
        k = jnp.dot(tok, wk_ref[...], preferred_element_type=F32)
        for copy in copies[3:5]:
            copy.wait()
        q = jnp.dot(tok, wq_ref[...], preferred_element_type=F32) * (1.0 / math.sqrt(DH))
        zero = jnp.zeros((rows, DH), F32)
        for n in range(2):
            for copy in copies[5 + 2 * n : 7 + 2 * n]:
                copy.wait()
            v = jnp.dot(tok, wv_ref[:, n * wide : (n + 1) * wide], preferred_element_type=F32)
            for m in range(2):
                h = 2 * n + m
                held[h] = jnp.concatenate(
                    [
                        v[:, m * DV : (m + 1) * DV],
                        k[:, h * DH : (h + 1) * DH],
                        zero,
                        q[:, h * DH : (h + 1) * DH],
                    ],
                    axis=1,
                ).astype(BF)
        for d in range(4):
            outs[d][...] = held[(Spot(at_ref).head_at + d) % 4]

    return pl.pallas_call(
        kernel,
        out_shape=[jax.ShapeDtypeStruct((rows, 384), BF)] * 4,
        in_specs=[SMEM] + [ANY] * 4,
        out_specs=[VMEM] * 4,
        scratch_shapes=[
            pltpu.VMEM((rows, depth), BF),
            pltpu.VMEM((depth, H * DH), BF),
            pltpu.VMEM((depth, H * DH), BF),
            pltpu.VMEM((depth, H * DV), BF),
            pltpu.VMEM((4, rows, 384), BF),
            pltpu.SemaphoreType.DMA((9,)),
        ],
        compiler_params=params(53),
        name="project",
    )(at, tokens, query_weight, key_weight, value_weight)


def stack_rows(parts, behind):
    rows = parts[0].shape[0]

    def kernel(*refs):
        ins, out = refs[:4], refs[5]
        row = lax.broadcasted_iota(jnp.int32, (TAIL, 128), 0)
        tail = jnp.zeros((TAIL, 128), F32)
        for d in range(4):
            out[d * rows : (d + 1) * rows, :] = ins[d][:, :256]
            first = ins[d][:TAIL, 256:].astype(F32)[:1]
            final = ins[d][rows - TAIL :, 256:].astype(F32)[TAIL - 1 :]
            tail = jnp.where(row == d, first, tail)
            tail = jnp.where(row == 4 + d, final, tail)
        out[4 * rows :, :128] = jnp.zeros((TAIL, 128), BF)
        out[4 * rows :, 128:] = tail.astype(BF)

    return pl.pallas_call(
        kernel,
        out_shape=jax.ShapeDtypeStruct((4 * rows + TAIL, 256), BF),
        in_specs=[VMEM] * 4 + [ANY],
        out_specs=VMEM,
        compiler_params=params(8),
        name="stack_rows",
    )(*parts, behind)


def attend(scalars, near, q, pairs, state, behind=()):
    rows = q[0].shape[0]
    width = 4 * rows
    first = state is None
    last = len(pairs) == 4
    strip = 32

    def kernel(s_ref, *refs):
        spot = Spot(s_ref)
        score_ref, prob_ref, peak_ref = refs[-3:]
        q_refs, refs = refs[:4], refs[4:]
        pair_refs, refs = refs[: len(pairs)], refs[len(pairs) :]
        if not first:
            old, old_peak, refs = refs[0], refs[1], refs[2:]
        refs = refs[len(behind) :]
        lane = lax.broadcasted_iota(jnp.int32, (width, 256), 1)
        place = lax.broadcasted_iota(jnp.int32, (1, rows), 1)

        def masks(n):
            far_by = (0, 2, 3, 1)[n]
            return jnp.concatenate(
                [place + spot.base(far_by, i) * rows < s_ref[4] for i in range(4)], axis=1
            )

        def values_of(ref):
            return jnp.where(lane == DV, jnp.ones((), BF), ref[:width, :])

        def raw_scores(query, ref):
            return lax.dot_general(
                query, ref[:width, 128:], (((1,), (1,)), ((), ())), preferred_element_type=F32
            )

        def shares(sums):
            return sums / sums[:, DV : DV + 1]

        if last:
            tails = [r[width:, 128:].astype(F32) for r in pair_refs]
            own, high, low = tails[0], tails[2], tails[3]
            row = lax.broadcasted_iota(jnp.int32, (TAIL, 128), 0)
            edge = jnp.zeros((TAIL, 128), F32)
            for d in range(4):
                n, m = (d + 1) % 4, (d + 3) % 4
                at = spot.ring_place(d)
                other = jnp.where(spot.core == 0, own[4 + n : 5 + n], low[4 + d : 5 + d])
                prev = jnp.where(at == 0, low[4 + n : 5 + n], other)
                other = jnp.where(spot.core == 0, own[m : m + 1], high[d : d + 1])
                nxt = jnp.where(at == 3, high[m : m + 1], other)
                edge = jnp.where(row == d, prev, edge)
                edge = jnp.where(row == 4 + d, nxt, edge)
            edge = edge.astype(BF)
            parts = [jnp.where(masks(n), raw_scores(edge, r), -1e30) for n, r in enumerate(pair_refs)]
            peak = jnp.max(parts[0], axis=1, keepdims=True)
            for s in parts[1:]:
                peak = jnp.maximum(peak, jnp.max(s, axis=1, keepdims=True))
            edge_sums = jnp.zeros((TAIL, 256), F32)
            for s, r in zip(parts, pair_refs):
                edge_sums += jnp.dot(jnp.exp(s - peak).astype(BF), values_of(r), preferred_element_type=F32)
            edge_out = shares(edge_sums)
            row = lax.broadcasted_iota(jnp.int32, (TAIL, 256), 0)

        pair_ref = pair_refs[-1]
        keep = masks(near)
        values = values_of(pair_ref)
        for i in range(4):
            score_ref[i] = raw_scores(q_refs[i][:, 256:], pair_ref)
        for i in range(4):
            for k in range(0, rows, strip):
                cut = slice(k, k + strip)
                scores = jnp.where(keep, score_ref[i, cut, :], -1e30)
                peak = jnp.broadcast_to(jnp.max(scores, axis=1, keepdims=True), (strip, 128))
                if not first:
                    peak = jnp.maximum(peak, old_peak[i * rows + k : i * rows + k + strip, :])
                across = jnp.concatenate([peak] * (width // 128), axis=1)
                prob_ref[i, cut, :] = jnp.exp(scores - across).astype(BF)
                peak_ref[i, cut, :] = peak
            update = jnp.dot(prob_ref[i], values, preferred_element_type=F32)
            if not first:
                shrink = jnp.exp(old_peak[i * rows : (i + 1) * rows, :] - peak_ref[i])
                update = update + old[i * rows : (i + 1) * rows, :] * jnp.concatenate([shrink] * 2, axis=1)
            if last:
                refs[i][:rows, :] = shares(update).astype(BF)
                ends = jnp.where(row == 0, edge_out[i : i + 1], jnp.zeros((TAIL, 256), F32))
                ends = jnp.where(row == 1, edge_out[4 + i : 5 + i], ends)
                refs[i][rows:, :] = ends.astype(BF)
            else:
                refs[0][i * rows : (i + 1) * rows, :] = update
                refs[1][i * rows : (i + 1) * rows, :] = peak_ref[i]

    ins = [*q, *pairs]
    if not first:
        ins += [*state]
    if last:
        outs = [jax.ShapeDtypeStruct((rows + TAIL, 256), BF)] * 4
    else:
        outs = [jax.ShapeDtypeStruct((4 * rows, n), F32) for n in (256, 128)]
    return pl.pallas_call(
        kernel,
        out_shape=outs,
        in_specs=[SMEM] + [VMEM] * len(ins) + [ANY] * len(behind),
        out_specs=[VMEM] * len(outs),
        scratch_shapes=[
            pltpu.VMEM((4, rows, width), F32),
            pltpu.VMEM((4, rows, width), BF),
            pltpu.VMEM((4, rows, 128), F32),
        ],
        compiler_params=params(24),
        cost_estimate=pl.CostEstimate(
            flops=4 * 2 * rows * width * 512, bytes_accessed=4 << 20, transcendentals=4 * rows * width
        ),
        name="attend",
    )(scalars, *ins, *behind)


def edges(mark, trunk, skip, cotangent):
    columns = trunk.shape[1]

    def kernel(mark_ref, t_ref, s_ref, c_ref, down, up, buffer, sems):
        copies = []
        for n, ref in enumerate((t_ref, s_ref, c_ref)):
            for end in range(2):
                start = end * (ref.shape[0] - TAIL)
                copies.append(
                    pltpu.make_async_copy(
                        ref.at[pl.ds(start, TAIL), :], buffer.at[2 * n + end], sems.at[2 * n + end]
                    )
                )
        for copy in copies:
            copy.start()
        for copy in copies:
            copy.wait()
        t_first, t_last, s_first, s_last, c_first, c_last = (buffer[n].astype(F32) for n in range(6))
        row = lax.broadcasted_iota(jnp.int32, (TAIL, columns), 0)

        def four(a, b, c, d):
            rest = jnp.where(row == 2, c, jnp.where(row == 3, d, 0.0))
            return jnp.where(row == 0, a, jnp.where(row == 1, b, rest)).astype(BF)

        up[...] = four(t_first[:1], s_first[:1], s_first[1:2], c_first[:1])
        e = TAIL - 1
        down[...] = four(t_last[e:], s_last[e - 1 : e], s_last[e:], c_last[e:])

    return pl.pallas_call(
        kernel,
        out_shape=[jax.ShapeDtypeStruct((TAIL, columns), BF)] * 2,
        in_specs=[ANY] * 4,
        out_specs=[VMEM] * 2,
        scratch_shapes=[pltpu.VMEM((6, TAIL, columns), BF), pltpu.SemaphoreType.DMA((6,))],
        compiler_params=params(53),
        name="edges",
    )(mark, trunk, skip, cotangent)


def gelu_parts(pre):
    slope = math.sqrt(2.0 / math.pi)
    square = pre * pre
    bend = jnp.tanh(slope * (pre + 0.044715 * (square * pre)))
    return bend, square, slope


WIDE = 384
STRIP = 32


def forward(scalars, ours, back, tokens, skipped, out_heads, before, after, depth_weight, turned):
    rows, columns = tokens.shape
    fine = 2 * rows
    half = columns // 2
    steps = half // WIDE
    quarter = columns // 4

    def side(s_ref):
        return s_ref[1] if ours else 1 - s_ref[1]

    def kernel(s_ref, b0, b1, b2, b3, low_ref, high_ref, dw_ref, tok_ref, skip_ref, ow_ref, g_ref, *refs):
        if ours:
            up_ref, act_ref = refs[:2]
            refs = refs[2:]
        else:
            up_ref, prod_ref, act_ref = refs[:3]
            refs = refs[3:]
        att, held = refs
        j = pl.program_id(0)

        @pl.when(j == 0)
        def _():
            mixed = [b[:, :DV].astype(F32) for b in (b0, b1, b2, b3)]
            squares = sum(jnp.sum(m * m, axis=1, keepdims=True) for m in mixed)
            scale = lax.rsqrt(squares * (1.0 / (H * DV)) + 1e-05)
            for d in range(4):
                att[d] = (mixed[d] * scale).astype(BF)

        @pl.when(j < steps)
        def _():
            spot = Spot(s_ref)
            n = jnp.minimum(j, steps - 1)
            take = pl.ds(pl.multiple_of((side(s_ref) * steps + n) * WIDE, 128), WIDE)
            low, high = low_ref[...].astype(F32), high_ref[...].astype(F32)
            grown = jnp.zeros((rows + TAIL, WIDE), F32)
            for d in range(4):
                grown += jnp.dot(att[d], ow_ref[(spot.head_at + d) % 4, :, take], preferred_element_type=F32)
            hidden = (tok_ref[:, take].astype(F32) + grown[:rows]).astype(BF)
            low_hid = (low[:1] + grown[rows : rows + 1]).astype(BF).astype(F32)
            high_hid = (high[:1] + grown[rows + 1 : rows + 2]).astype(BF).astype(F32)
            twice = lax.broadcasted_iota(jnp.int32, (fine, rows), 0) // 2
            twice = jnp.where(twice == lax.broadcasted_iota(jnp.int32, (fine, rows), 1), 1.0, 0.0).astype(BF)
            doubled = jnp.dot(twice, hidden, preferred_element_type=F32)
            row = lax.broadcasted_iota(jnp.int32, (TAIL, WIDE), 0)
            edge = (low_hid + jnp.where(row == 14, low[1:2], low[2:3])).astype(BF).astype(F32)
            edge = jnp.where((row >= 14) & (spot.place > 0), edge, 0.0)
            held[:TAIL, :] = edge
            up_ref[:TAIL, :] = edge.astype(BF)
            edge = (high_hid + jnp.where(row == 0, high[1:2], high[2:3])).astype(BF).astype(F32)
            edge = jnp.where((row < 2) & (spot.place < 15), edge, 0.0)
            held[TAIL + fine :, :] = edge
            up_ref[TAIL + fine :, :] = edge.astype(BF)
            for k in range(0, fine, STRIP):
                up = (doubled[k : k + STRIP] + skip_ref[k : k + STRIP, take].astype(F32)).astype(BF)
                up_ref[TAIL + k : TAIL + k + STRIP, :] = up
                held[TAIL + k : TAIL + k + STRIP, :] = up.astype(F32)
            w = [dw_ref[t : t + 1, :] for t in range(3)]
            cut = pl.ds(0 if ours else pl.multiple_of(n * WIDE, 128), WIDE)
            for k in range(0, fine, STRIP):
                near = held[8 + k : 24 + k + STRIP, :]
                pre = w[0] * near[7 : 7 + STRIP] + w[1] * near[8 : 8 + STRIP] + w[2] * near[9 : 9 + STRIP]
                bend, _, _ = gelu_parts(pre)
                act_ref[k : k + STRIP, cut] = (pre * (0.5 + 0.5 * bend)).astype(BF)

        if not ours:

            @pl.when(j >= steps)
            def _():
                for n in range(2):
                    at = pl.multiple_of((Spot(s_ref).their_first + 2 * (j - steps) + n) % 4 * quarter, 16)
                    prod_ref[n] = jnp.dot(
                        g_ref[pl.ds(at, quarter), :], act_ref[...], preferred_element_type=F32
                    ).astype(BF)

    def cols(count, full):
        def place(j, s_ref):
            n = jnp.minimum(j, steps - 1)
            return 0, (side(s_ref) * steps + n if full else n)

        return pl.BlockSpec((count, WIDE), place)

    def flat(count, width):
        return pl.BlockSpec((count, width), lambda j, s_ref: (0, 0))

    outs = [jax.ShapeDtypeStruct((fine + 2 * TAIL, half), BF)]
    out_specs = [cols(fine + 2 * TAIL, False)]
    scratch = []
    if ours:
        outs += [jax.ShapeDtypeStruct((fine, half), BF)]
        out_specs += [cols(fine, False)]
    else:
        outs += [jax.ShapeDtypeStruct((4, quarter, half), BF)]
        out_specs += [
            pl.BlockSpec((2, quarter, half), lambda j, s_ref: (jnp.maximum(j - steps, 0), 0, 0))
        ]
        scratch += [pltpu.VMEM((fine, half), BF)]
    scratch += [
        pltpu.VMEM((4, rows + TAIL, DV), BF),
        pltpu.VMEM((fine + 2 * TAIL, WIDE), F32),
    ]
    return pl.pallas_call(
        kernel,
        out_shape=outs,
        grid_spec=pltpu.PrefetchScalarGridSpec(
            num_scalar_prefetch=1,
            grid=(steps if ours else steps + 2,),
            in_specs=[flat(rows + TAIL, 256)] * 4
            + [cols(TAIL, True), cols(TAIL, True), cols(3, True)]
            + [VMEM] * 4,
            out_specs=out_specs,
            scratch_shapes=scratch,
        ),
        compiler_params=params(24),
        cost_estimate=pl.CostEstimate(
            flops=2 * fine * columns * columns, bytes_accessed=9 << 20, transcendentals=fine * half
        ),
        name="forward",
    )(scalars, *back, before, after, depth_weight, tokens, skipped, out_heads, turned)


def load(behind, *arrays):
    count = len(arrays)

    def kernel(behind_ref, *refs):
        sems = refs[-1]
        copies = [pltpu.make_async_copy(refs[n], refs[count + n], sems.at[n]) for n in range(count)]
        for copy in copies:
            copy.start()
        for copy in copies:
            copy.wait()

    return pl.pallas_call(
        kernel,
        out_shape=[jax.ShapeDtypeStruct(a.shape, a.dtype) for a in arrays],
        in_specs=[ANY] * (1 + count),
        out_specs=[VMEM] * count,
        scratch_shapes=[pltpu.SemaphoreType.DMA((count,))],
        compiler_params=params(47),
        name="load",
    )(behind, *arrays)


def backward(scalars, theirs, ours, upstream, before, after, point_weight, depth_weight, behind):
    fine, columns = upstream.shape
    half = columns // 2
    steps = half // WIDE

    def kernel(s_ref, theirs_ref, ours_ref, g_ref, low_ref, high_ref, pw_ref, dw_ref, behind_ref, *refs):
        gs_ref, gd_theirs, gd_ours, grad, upper, ends, up_ref = refs
        j = pl.program_id(0)

        @pl.when(j < steps)
        def _():
            up_ref[...] = theirs_ref[...]

        @pl.when(j >= steps)
        def _():
            up_ref[...] = ours_ref[...]

        dims = (((1,), (1,)), ((), ()))

        @pl.when(pl.program_id(0) == 0)
        def _():
            row = lax.broadcasted_iota(jnp.int32, (TAIL, columns), 0)
            low, high = low_ref[...].astype(F32), high_ref[...].astype(F32)
            ends[...] = jnp.where(row == 7, low[3:4], jnp.where(row == 8, high[3:4], 0.0)).astype(BF)

        upper[...] = lax.dot_general(g_ref[...], pw_ref[...], dims, preferred_element_type=F32)
        outer = lax.dot_general(ends[...], pw_ref[...], dims, preferred_element_type=F32)
        w = [dw_ref[t : t + 1, :] for t in range(3)]

        def grad_of(near, start, count, coming):
            taps = [near[start - 1 + t : start - 1 + t + count] for t in range(3)]
            pre = w[0] * taps[0] + w[1] * taps[1] + w[2] * taps[2]
            bend, square, slope = gelu_parts(pre)
            rate = 0.5 + 0.5 * bend + (pre * (1.0 - bend * bend)) * (
                0.5 * slope + (1.5 * slope * 0.044715) * square
            )
            return taps, (coming * rate).astype(BF).astype(F32)

        _, grad[8:16, :] = grad_of(up_ref[:32, :].astype(F32), 8, 8, outer[:8])
        _, grad[16 + fine : 24 + fine, :] = grad_of(up_ref[fine:, :].astype(F32), 16, 8, outer[8:])
        sums = [jnp.zeros((8, WIDE), F32)] * 3
        for k in range(0, fine, STRIP):
            near = up_ref[k : k + STRIP + 2 * TAIL, :].astype(F32)
            taps, mid = grad_of(near, TAIL, STRIP, upper[k : k + STRIP, :])
            grad[16 + k : 16 + k + STRIP, :] = mid
            for t in range(3):
                term = taps[t] * mid
                for r in range(0, STRIP, 8):
                    sums[t] = sums[t] + term[r : r + 8]
        depth = [jnp.sum(total, axis=0, keepdims=True) for total in sums]
        for ref, mine in ((gd_theirs, j < steps), (gd_ours, j >= steps)):

            @pl.when(mine)
            def _():
                for t in range(3):
                    ref[t : t + 1, :] = depth[t]

        for k in range(0, fine, STRIP):
            near = grad[8 + k : 24 + k + STRIP, :]
            gs_ref[k : k + STRIP, :] = (
                w[0] * near[9 : 9 + STRIP] + w[1] * near[8 : 8 + STRIP] + w[2] * near[7 : 7 + STRIP]
            ).astype(BF)

    def block(j, s_ref):
        return jnp.where(j < steps, (1 - s_ref[1]) * steps + j, s_ref[1] * steps + j - steps)

    def cols(count):
        return pl.BlockSpec((count, WIDE), lambda j, s_ref: (0, block(j, s_ref)))

    def early(count):
        return pl.BlockSpec((count, WIDE), lambda j, s_ref: (0, jnp.minimum(j, steps - 1)))

    def late(count):
        return pl.BlockSpec((count, WIDE), lambda j, s_ref: (0, jnp.maximum(j - steps, 0)))

    def flat(count):
        return pl.BlockSpec((count, columns), lambda j, s_ref: (0, 0))

    return pl.pallas_call(
        kernel,
        out_shape=[
            jax.ShapeDtypeStruct((fine, columns), BF),
            jax.ShapeDtypeStruct((3, half), F32),
            jax.ShapeDtypeStruct((3, half), F32),
        ],
        grid_spec=pltpu.PrefetchScalarGridSpec(
            num_scalar_prefetch=1,
            grid=(2 * steps,),
            in_specs=[
                early(fine + 2 * TAIL),
                late(fine + 2 * TAIL),
                flat(fine),
                flat(TAIL),
                flat(TAIL),
                pl.BlockSpec((WIDE, columns), lambda j, s_ref: (block(j, s_ref), 0)),
                cols(3),
                ANY,
            ],
            out_specs=[cols(fine), early(3), late(3)],
            scratch_shapes=[
                pltpu.VMEM((fine + 2 * TAIL, WIDE), F32),
                pltpu.VMEM((fine, WIDE), F32),
                pltpu.VMEM((TAIL, columns), BF),
                pltpu.VMEM((fine + 2 * TAIL, WIDE), BF),
            ],
        ),
        compiler_params=params(48),
        cost_estimate=pl.CostEstimate(
            flops=2 * fine * columns * columns, bytes_accessed=11 << 20, transcendentals=fine * columns
        ),
        name="backward",
    )(scalars, theirs, ours, upstream, before, after, point_weight, depth_weight, behind)


def product(scalars, act, turned, steps, arrived):
    half, quarter = act.shape[1], turned.shape[0] // 4

    def kernel(s_ref, a_ref, g_ref, arrived_ref, *outs):
        for out, d in zip(outs, steps):
            at = pl.multiple_of((Spot(s_ref).first_at + d) % 4 * quarter, 16)
            block = jnp.dot(g_ref[pl.ds(at, quarter), :], a_ref[...], preferred_element_type=F32)
            out[...] = (block + arrived_ref[d].astype(F32)).astype(BF)

    return pl.pallas_call(
        kernel,
        out_shape=[jax.ShapeDtypeStruct((quarter, half), BF)] * len(steps),
        in_specs=[SMEM] + [VMEM] * 3,
        out_specs=[VMEM] * len(steps),
        compiler_params=params(14),
        cost_estimate=pl.CostEstimate(
            flops=2 * act.shape[0] * half * quarter * len(steps), bytes_accessed=6 << 20, transcendentals=0
        ),
        name="product",
    )(scalars, act, turned, arrived)


def split_rows(at, got):
    rows, columns = got[0].shape
    slim = rows // 4

    def kernel(at_ref, *refs):
        ins, outs = refs[:4], refs[4:]
        for d in range(4):
            take = pl.ds(pl.multiple_of((Spot(at_ref).second_at + d) % 4 * slim, 16), slim)
            outs[d][...] = total_of([r[take, :] for r in ins]).astype(BF)

    return pl.pallas_call(
        kernel,
        out_shape=[jax.ShapeDtypeStruct((slim, columns), BF)] * 4,
        in_specs=[SMEM] + [VMEM] * 4,
        out_specs=[VMEM] * 4,
        compiler_params=params(10),
        name="split_rows",
    )(at, *got)


def join_rows(at, got):
    slim, columns = got[0].shape[0] - TAIL, got[0].shape[1]
    quarter = 4 * slim

    def kernel(at_ref, *refs):
        ins, out, held = refs[:4], refs[4], refs[5]
        for d in range(4):
            put = pl.ds(pl.multiple_of((Spot(at_ref).second_at + 4 - d) % 4 * slim, 16), slim)
            held[put, :] = ins[d][:slim, :]
        out[:columns, :] = held[...].T
        last = total_of([r[slim:, :] for r in ins])[:8]
        out[columns:, :] = jnp.concatenate([last[:, :quarter], last[:, quarter:]], axis=0).astype(BF)

    return pl.pallas_call(
        kernel,
        out_shape=jax.ShapeDtypeStruct((columns + TAIL, quarter), BF),
        in_specs=[SMEM] + [VMEM] * 4,
        out_specs=VMEM,
        scratch_shapes=[pltpu.VMEM((quarter, columns), BF)],
        compiler_params=params(10),
        name="join_rows",
    )(at, *got)


def lay_out(scalars, own, other):
    half, quarter = own[0].shape[0] - TAIL, own[0].shape[1]
    parts = 4
    part = half // parts

    def kernel(s_ref, *refs):
        out, depth, sems = refs[-3:]
        spot = Spot(s_ref)
        copies = []
        for n in range(8):
            mine = n < 4
            down = (spot.core if mine else 1 - spot.core) * half
            over = ((spot.first_at if mine else spot.their_first) + 4 - n % 4) % 4 * quarter
            for k in range(parts):
                start = pl.multiple_of(down + k * part, 16)
                copies.append(
                    pltpu.make_async_copy(
                        refs[n].at[pl.ds(k * part, part), :],
                        out.at[pl.ds(start, part), pl.ds(pl.multiple_of(over, 128), quarter)],
                        sems.at[parts * n + k],
                    )
                )
        for copy in copies:
            copy.start()
        for n, side in ((0, spot.core), (4, 1 - spot.core)):
            rows = total_of([refs[n + d][half:, :] for d in range(4)])
            rows = jnp.concatenate([rows[:3], rows[8:11]], axis=1)
            depth[:, pl.ds(pl.multiple_of(side * half, 128), half)] = rows
        for copy in copies:
            copy.wait()

    return pl.pallas_call(
        kernel,
        out_shape=[
            jax.ShapeDtypeStruct((2 * half, 4 * quarter), BF),
            jax.ShapeDtypeStruct((3, 2 * half), F32),
        ],
        in_specs=[SMEM] + [VMEM] * 8,
        out_specs=[ANY, VMEM],
        scratch_shapes=[pltpu.SemaphoreType.DMA((8 * parts,))],
        compiler_params=params(12),
        name="lay_out",
    )(scalars, *own, *other)


def local(
    trunk,
    skip,
    valid_bins,
    query_weight,
    key_weight,
    value_weight,
    out_weight,
    depth_weight,
    point_weight,
    cotangent,
):
    tokens, skipped, upstream = trunk[0], skip[0], cotangent[0]
    rows, columns = tokens.shape
    fine = skipped.shape[0]
    ix, ic, iz, iy = (lax.axis_index(a) for a in AXES)
    spot = jnp.stack([v.astype(jnp.int32) for v in (ix, ic, iz, iy)])
    scalars = jnp.concatenate([spot, valid_bins.astype(jnp.int32)])
    blocks = project(spot, tokens, query_weight, key_weight, value_weight)
    down, up = edges(blocks[0], tokens, skipped, upstream)
    before = lax.ppermute(down, ("z", "y"), [(i, i + 1) for i in range(15)])
    after = lax.ppermute(up, ("z", "y"), [(i + 1, i) for i in range(15)])
    q = exchange(blocks, HEAD_RING)
    own = stack_rows(q, down)
    far = {d: lax.ppermute(own, AXES, turn(ROW_RING, d)) for d in (2, 3, 1)}
    state = attend(scalars, 0, q, [own], None)

    turned = upstream.T

    state = attend(scalars, 1, q, [far[2]], state)
    state = attend(scalars, 2, q, [far[3]], state)
    mixed = attend(scalars, 3, q, [own, far[2], far[3], far[1]], state, (before, after))
    back = exchange(mixed, HEAD_RING, -1)
    tokens_v, skipped_v, out_v = load(mixed[0], tokens, skipped, out_weight.reshape(H, DV, -1))
    swap = [(0, 1), (1, 0)]
    given = (back, tokens_v, skipped_v, out_v, before, after, depth_weight, turned)
    up_theirs, sent = forward(scalars, False, *given)
    arrived = lax.ppermute(sent, "c", swap)
    up_ours, act = forward(scalars, True, *given)
    (piece_2,) = product(scalars, act, turned, (2,), arrived)
    (piece_1,) = product(scalars, act, turned, (1,), arrived)
    piece_3, piece_0 = product(scalars, act, turned, (3, 0), arrived)
    got = exchange([piece_0, piece_1, piece_2, piece_3], SUM_RINGS[0])

    grad_skip, d_theirs, d_mine = backward(
        scalars, up_theirs, up_ours, upstream, before, after, point_weight, depth_weight, piece_0
    )
    d_sum = d_mine + lax.ppermute(d_theirs, "c", swap)
    rider = jnp.pad(d_sum.astype(BF), ((0, TAIL - 3), (0, 0)))

    got = exchange(split_rows(scalars, got), SUM_RINGS[1])
    mixed = jnp.concatenate([total_of(got).astype(BF), rider], axis=0)
    got = exchange([mixed] * 4, SUM_RINGS[2])
    norm_scale = 1.0 / math.sqrt(128 * fine)
    summed = (total_of(got) * norm_scale).astype(BF)
    joined = join_rows(scalars, exchange([summed] * 4, SUM_RINGS[1]))

    own = exchange([joined] * 4, SUM_RINGS[0], order=(1, 3, 2))
    other = [lax.ppermute(block, "c", swap) for block in own]
    grad_pointwise, grad_depth = lay_out(scalars, own, other)
    return (grad_pointwise, grad_depth, grad_skip[None])


def solution(mesh):
    fine_mesh = Mesh(mesh.devices.reshape(SIZES), AXES)
    rows = P(("x", "c"), ("z", "y"), None)
    return jax.shard_map(
        local,
        mesh=fine_mesh,
        in_specs=(rows, rows, P(("x", "c")), P(), P(), P(), P(), P(), P(), rows),
        out_specs=(P(), P(), rows),
        check_vma=False,
    )
```

```python
import math

import jax
import jax.numpy as jnp
from jax import lax
from jax.experimental import pallas as pl
from jax.experimental.pallas import tpu as pltpu
from jax.sharding import Mesh, PartitionSpec as P

H = 4
DH = 64
DV = 192
AXES = ("x", "c", "z", "y")
SIZES = (4, 2, 4, 4)
BF = jnp.bfloat16
F32 = jnp.float32
TAIL = 16
VMEM = pl.BlockSpec(memory_space=pltpu.VMEM)
SMEM = pl.BlockSpec(memory_space=pltpu.SMEM)
ANY = pl.BlockSpec(memory_space=pl.ANY)
SUM_RINGS = (("x", "y"), ("y", "z"), ("z", "x"))
HEAD_RING = ("y", "z")
ROW_RING = ("z", "y")


class Spot:
    def __init__(self, s_ref):
        x, core, z, y = (s_ref[n] for n in range(4))
        first = core == 0
        self.core, self.y = core, y
        self.head_at = jnp.where(first, y, z)
        self.row_at = jnp.where(first, z, y)
        self.first_at = jnp.where(first, x, y)
        self.their_first = jnp.where(first, y, x)
        self.second_at = jnp.where(first, y, z)
        self.place = z * 4 + y

    def base(self, far_by, d):
        h, r = (self.head_at + 4 - d) % 4, (self.row_at + 4 - far_by) % 4
        return jnp.where(self.core == 0, r * 4 + h, h * 4 + r)

    def ring_place(self, d):
        return jnp.where(self.core == 0, (self.y + 4 - d) % 4, self.y)


def params(mib):
    return pltpu.CompilerParams(vmem_limit_bytes=mib << 20)


def turn(axes, step):
    pairs = []
    for x in range(4):
        for c in range(2):
            for z in range(4):
                for y in range(4):
                    at = {"x": x, "z": z, "y": y}
                    to = dict(at)
                    to[axes[c]] = (at[axes[c]] + step) % 4
                    flat = [((p["x"] * 2 + c) * 4 + p["z"]) * 4 + p["y"] for p in (at, to)]
                    pairs.append(tuple(flat))
    return pairs


def exchange(pieces, axes, sign=1):
    got = [pieces[0], None, None, None]
    for d in (2, 1, 3):
        got[d] = lax.ppermute(pieces[d], AXES, turn(axes, sign * d))
    return got


def total_of(got):
    a, b, c, d = (g.astype(F32) for g in got)
    return (a + c) + (b + d)


def project(tokens, query_weight, key_weight, value_weight):
    rows, depth = tokens.shape
    cut = depth // 2

    def kernel(tok_hbm, wq_hbm, wk_hbm, wv_hbm, *refs):
        head_at = jnp.where(lax.axis_index("c") == 0, lax.axis_index("y"), lax.axis_index("z"))
        outs, (tok_ref, wq_ref, wk_ref, wv_ref, held, sems) = refs[:4], refs[4:]
        low, high = pl.ds(0, cut), pl.ds(cut, depth - cut)
        copies = [
            pltpu.make_async_copy(tok_hbm, tok_ref, sems.at[0]),
            pltpu.make_async_copy(wv_hbm.at[low, :], wv_ref.at[low, :], sems.at[1]),
            pltpu.make_async_copy(wv_hbm.at[high, :], wv_ref.at[high, :], sems.at[2]),
            pltpu.make_async_copy(wk_hbm, wk_ref, sems.at[3]),
            pltpu.make_async_copy(wq_hbm, wq_ref, sems.at[4]),
        ]
        for copy in copies:
            copy.start()
        copies[0].wait()
        tok = tok_ref[...]
        copies[1].wait()
        v = jnp.dot(tok[:, :cut], wv_ref[:cut, :], preferred_element_type=F32)
        copies[2].wait()
        v += jnp.dot(tok[:, cut:], wv_ref[cut:, :], preferred_element_type=F32)
        copies[3].wait()
        k = jnp.dot(tok, wk_ref[...], preferred_element_type=F32)
        copies[4].wait()
        q = jnp.dot(tok, wq_ref[...], preferred_element_type=F32) * (1.0 / math.sqrt(DH))
        for h in range(H):
            part = slice(h * DH, (h + 1) * DH)
            held[h, :rows, :] = jnp.concatenate([v[:, h * DV : (h + 1) * DV], k[:, part]], axis=1).astype(BF)
            held[h, rows:, :] = jnp.concatenate(
                [q[n * rows // 4 : (n + 1) * rows // 4, part] for n in range(4)], axis=1
            ).astype(BF)
        for d in range(4):
            outs[d][...] = held[(head_at + d) % 4]

    return pl.pallas_call(
        kernel,
        out_shape=[jax.ShapeDtypeStruct((rows + rows // 4, 256), BF)] * 4,
        in_specs=[ANY] * 4,
        out_specs=[VMEM] * 4,
        scratch_shapes=[
            pltpu.VMEM((rows, depth), BF),
            pltpu.VMEM((depth, H * DH), BF),
            pltpu.VMEM((depth, H * DH), BF),
            pltpu.VMEM((depth, H * DV), BF),
            pltpu.VMEM((4, rows + rows // 4, 256), BF),
            pltpu.SemaphoreType.DMA((5,)),
        ],
        compiler_params=params(53),
        name="project",
    )(tokens, query_weight, key_weight, value_weight)


def stack_rows(parts, behind):
    rows = parts[0].shape[0] * 4 // 5

    def kernel(*refs):
        ins, out = refs[:4], refs[5]
        zero = jnp.zeros((1, DH), F32)
        row = lax.broadcasted_iota(jnp.int32, (TAIL, 128), 0)
        tail = jnp.zeros((TAIL, 128), F32)
        for d in range(4):
            out[d * rows : (d + 1) * rows, :] = ins[d][:rows, :]
            first = ins[d][rows : rows + TAIL, :].astype(F32)[:1, :DH]
            final = ins[d][rows + rows // 4 - TAIL :, :].astype(F32)[TAIL - 1 :, 3 * DH :]
            first, final = (jnp.concatenate([zero, r], axis=1) for r in (first, final))
            tail = jnp.where(row == d, first, tail)
            tail = jnp.where(row == 4 + d, final, tail)
        out[4 * rows :, :128] = jnp.zeros((TAIL, 128), BF)
        out[4 * rows :, 128:] = tail.astype(BF)

    return pl.pallas_call(
        kernel,
        out_shape=jax.ShapeDtypeStruct((4 * rows + TAIL, 256), BF),
        in_specs=[VMEM] * 4 + [ANY],
        out_specs=VMEM,
        compiler_params=params(8),
        name="stack_rows",
    )(*parts, behind)


def spread(parts):
    rows = parts[0].shape[0] * 4 // 5
    quarter = rows // 4

    def kernel(*refs):
        zero = jnp.zeros((quarter, DH), F32)
        for d in range(4):
            packed = refs[d][rows:, :].astype(F32)
            for n in range(4):
                refs[4 + d][n * quarter : (n + 1) * quarter, :] = jnp.concatenate(
                    [zero, packed[:, n * DH : (n + 1) * DH]], axis=1
                ).astype(BF)

    return pl.pallas_call(
        kernel,
        out_shape=[jax.ShapeDtypeStruct((rows, 128), BF)] * 4,
        in_specs=[VMEM] * 4,
        out_specs=[VMEM] * 4,
        compiler_params=params(8),
        name="spread",
    )(*parts)


def attend(scalars, near, q, pairs, state, behind=()):
    rows = q[0].shape[0]
    width = 4 * rows
    first = state is None
    last = len(pairs) == 4
    strip = 32

    def kernel(s_ref, *refs):
        spot = Spot(s_ref)
        score_ref, prob_ref, peak_ref = refs[-3:]
        q_refs, refs = refs[:4], refs[4:]
        pair_refs, refs = refs[: len(pairs)], refs[len(pairs) :]
        if not first:
            old, old_peak, refs = refs[0], refs[1], refs[2:]
        refs = refs[len(behind) :]
        lane = lax.broadcasted_iota(jnp.int32, (width, 256), 1)
        place = lax.broadcasted_iota(jnp.int32, (1, rows), 1)

        def masks(n):
            far_by = (0, 1, 3, 2)[n]
            return jnp.concatenate(
                [place + spot.base(far_by, i) * rows < s_ref[4] for i in range(4)], axis=1
            )

        def values_of(ref):
            return jnp.where(lane == DV, jnp.ones((), BF), ref[:width, :])

        def raw_scores(query, ref):
            return lax.dot_general(
                query, ref[:width, 128:], (((1,), (1,)), ((), ())), preferred_element_type=F32
            )

        def shares(sums):
            return sums / sums[:, DV : DV + 1]

        if last:
            tails = [r[width:, 128:].astype(F32) for r in pair_refs]
            own, low, high = tails[0], tails[1], tails[2]
            row = lax.broadcasted_iota(jnp.int32, (TAIL, 128), 0)
            edge = jnp.zeros((TAIL, 128), F32)
            for d in range(4):
                n, m = (d + 1) % 4, (d + 3) % 4
                at = spot.ring_place(d)
                other = jnp.where(spot.core == 0, own[4 + n : 5 + n], low[4 + d : 5 + d])
                prev = jnp.where(at == 0, low[4 + n : 5 + n], other)
                other = jnp.where(spot.core == 0, own[m : m + 1], high[d : d + 1])
                nxt = jnp.where(at == 3, high[m : m + 1], other)
                edge = jnp.where(row == d, prev, edge)
                edge = jnp.where(row == 4 + d, nxt, edge)
            edge = edge.astype(BF)
            parts = [jnp.where(masks(n), raw_scores(edge, r), -1e30) for n, r in enumerate(pair_refs)]
            peak = jnp.max(parts[0], axis=1, keepdims=True)
            for s in parts[1:]:
                peak = jnp.maximum(peak, jnp.max(s, axis=1, keepdims=True))
            edge_sums = jnp.zeros((TAIL, 256), F32)
            for s, r in zip(parts, pair_refs):
                edge_sums += jnp.dot(jnp.exp(s - peak).astype(BF), values_of(r), preferred_element_type=F32)
            edge_out = shares(edge_sums)

        pair_ref = pair_refs[-1]
        keep = masks(near)
        values = values_of(pair_ref)
        for i in range(4):
            score_ref[i] = raw_scores(q_refs[i][...], pair_ref)
        for i in range(4):
            for k in range(0, rows, strip):
                cut = slice(k, k + strip)
                scores = jnp.where(keep, score_ref[i, cut, :], -1e30)
                peak = jnp.broadcast_to(jnp.max(scores, axis=1, keepdims=True), (strip, 128))
                if not first:
                    peak = jnp.maximum(peak, old_peak[i * rows + k : i * rows + k + strip, :])
                across = jnp.concatenate([peak] * (width // 128), axis=1)
                prob_ref[i, cut, :] = jnp.exp(scores - across).astype(BF)
                peak_ref[i, cut, :] = peak
            update = jnp.dot(prob_ref[i], values, preferred_element_type=F32)
            if not first:
                shrink = jnp.exp(old_peak[i * rows : (i + 1) * rows, :] - peak_ref[i])
                update = update + old[i * rows : (i + 1) * rows, :] * jnp.concatenate([shrink] * 2, axis=1)
            if last:
                share = shares(update)
                high = share[:, 128:DV]
                refs[i][:rows, :] = share[:, :128].astype(BF)
                refs[i][rows : rows + rows // 2, :] = jnp.concatenate(
                    [high[: rows // 2], high[rows // 2 :]], axis=1
                ).astype(BF)
                ends = jnp.zeros((TAIL, 128), F32)
                for n in range(4):
                    at = i + 4 * (n % 2)
                    part = edge_out[at : at + 1, :128] if n < 2 else edge_out[at : at + 1, 128:]
                    ends = jnp.where(row == n, part, ends)
                refs[i][rows + rows // 2 :, :] = ends.astype(BF)
            else:
                refs[0][i * rows : (i + 1) * rows, :] = update
                refs[1][i * rows : (i + 1) * rows, :] = peak_ref[i]

    ins = [*q, *pairs]
    if not first:
        ins += [*state]
    if last:
        outs = [jax.ShapeDtypeStruct((rows + rows // 2 + TAIL, 128), BF)] * 4
    else:
        outs = [jax.ShapeDtypeStruct((4 * rows, n), F32) for n in (256, 128)]
    return pl.pallas_call(
        kernel,
        out_shape=outs,
        in_specs=[SMEM] + [VMEM] * len(ins) + [ANY] * len(behind),
        out_specs=[VMEM] * len(outs),
        scratch_shapes=[
            pltpu.VMEM((4, rows, width), F32),
            pltpu.VMEM((4, rows, width), BF),
            pltpu.VMEM((4, rows, 128), F32),
        ],
        compiler_params=params(24),
        cost_estimate=pl.CostEstimate(
            flops=4 * 2 * rows * width * 512, bytes_accessed=4 << 20, transcendentals=4 * rows * width
        ),
        name="attend",
    )(scalars, *ins, *behind)


def edges(mark, trunk, skip, cotangent):
    columns = trunk.shape[1]

    def kernel(mark_ref, t_ref, s_ref, c_ref, down, up, buffer, sems):
        copies = []
        for n, ref in enumerate((t_ref, s_ref, c_ref)):
            for end in range(2):
                start = end * (ref.shape[0] - TAIL)
                copies.append(
                    pltpu.make_async_copy(
                        ref.at[pl.ds(start, TAIL), :], buffer.at[2 * n + end], sems.at[2 * n + end]
                    )
                )
        for copy in copies:
            copy.start()
        for copy in copies:
            copy.wait()
        t_first, t_last, s_first, s_last, c_first, c_last = (buffer[n].astype(F32) for n in range(6))
        row = lax.broadcasted_iota(jnp.int32, (TAIL, columns), 0)

        def four(a, b, c, d):
            rest = jnp.where(row == 2, c, jnp.where(row == 3, d, 0.0))
            return jnp.where(row == 0, a, jnp.where(row == 1, b, rest)).astype(BF)

        up[...] = four(t_first[:1], s_first[:1], s_first[1:2], c_first[:1])
        e = TAIL - 1
        down[...] = four(t_last[e:], s_last[e - 1 : e], s_last[e:], c_last[e:])

    return pl.pallas_call(
        kernel,
        out_shape=[jax.ShapeDtypeStruct((TAIL, columns), BF)] * 2,
        in_specs=[ANY] * 4,
        out_specs=[VMEM] * 2,
        scratch_shapes=[pltpu.VMEM((6, TAIL, columns), BF), pltpu.SemaphoreType.DMA((6,))],
        compiler_params=params(53),
        name="edges",
    )(mark, trunk, skip, cotangent)


def gelu_parts(pre):
    slope = math.sqrt(2.0 / math.pi)
    square = pre * pre
    bend = jnp.tanh(slope * (pre + 0.044715 * (square * pre)))
    return bend, square, slope


WIDE = 384
STRIP = 32


def forward(scalars, ours, back, tokens, skipped, out_heads, before, after, depth_weight, turned):
    rows, columns = tokens.shape
    fine = 2 * rows
    half = columns // 2
    steps = half // WIDE
    quarter = columns // 4

    def side(s_ref):
        return s_ref[1] if ours else 1 - s_ref[1]

    def kernel(s_ref, b0, b1, b2, b3, low_ref, high_ref, dw_ref, tok_ref, skip_ref, ow_ref, g_ref, *refs):
        if ours:
            up_ref, act_ref = refs[:2]
            refs = refs[2:]
        else:
            up_ref, prod_ref, act_ref = refs[:3]
            refs = refs[3:]
        att, held = refs
        j = pl.program_id(0)

        @pl.when(j == 0)
        def _():
            mixed = []
            for b in (b0, b1, b2, b3):
                pair = b[rows : rows + rows // 2, :].astype(F32)
                last = b[rows + rows // 2 :, :].astype(F32)
                high = jnp.concatenate(
                    [pair[:, :64], pair[:, 64:], last[2:4, :64], jnp.zeros((TAIL - 2, 64), F32)], axis=0
                )
                left = jnp.concatenate([b[:rows, :].astype(F32), last], axis=0)
                mixed.append(jnp.concatenate([left, high], axis=1))
            squares = sum(jnp.sum(m * m, axis=1, keepdims=True) for m in mixed)
            scale = lax.rsqrt(squares * (1.0 / (H * DV)) + 1e-05)
            for d in range(4):
                att[d] = (mixed[d] * scale).astype(BF)

        @pl.when(j < steps)
        def _():
            spot = Spot(s_ref)
            n = jnp.minimum(j, steps - 1)
            take = pl.ds(pl.multiple_of((side(s_ref) * steps + n) * WIDE, 128), WIDE)
            low, high = low_ref[...].astype(F32), high_ref[...].astype(F32)
            grown = jnp.zeros((rows + TAIL, WIDE), F32)
            for d in range(4):
                grown += jnp.dot(att[d], ow_ref[(spot.head_at + d) % 4, :, take], preferred_element_type=F32)
            hidden = (tok_ref[:, take].astype(F32) + grown[:rows]).astype(BF)
            low_hid = (low[:1] + grown[rows : rows + 1]).astype(BF).astype(F32)
            high_hid = (high[:1] + grown[rows + 1 : rows + 2]).astype(BF).astype(F32)
            twice = lax.broadcasted_iota(jnp.int32, (fine, rows), 0) // 2
            twice = jnp.where(twice == lax.broadcasted_iota(jnp.int32, (fine, rows), 1), 1.0, 0.0).astype(BF)
            doubled = jnp.dot(twice, hidden, preferred_element_type=F32)
            row = lax.broadcasted_iota(jnp.int32, (TAIL, WIDE), 0)
            edge = (low_hid + jnp.where(row == 14, low[1:2], low[2:3])).astype(BF).astype(F32)
            edge = jnp.where((row >= 14) & (spot.place > 0), edge, 0.0)
            held[:TAIL, :] = edge
            up_ref[:TAIL, :] = edge.astype(BF)
            edge = (high_hid + jnp.where(row == 0, high[1:2], high[2:3])).astype(BF).astype(F32)
            edge = jnp.where((row < 2) & (spot.place < 15), edge, 0.0)
            held[TAIL + fine :, :] = edge
            up_ref[TAIL + fine :, :] = edge.astype(BF)
            for k in range(0, fine, STRIP):
                up = (doubled[k : k + STRIP] + skip_ref[k : k + STRIP, take].astype(F32)).astype(BF)
                up_ref[TAIL + k : TAIL + k + STRIP, :] = up
                held[TAIL + k : TAIL + k + STRIP, :] = up.astype(F32)
            w = [dw_ref[t : t + 1, :] for t in range(3)]
            cut = pl.ds(0 if ours else pl.multiple_of(n * WIDE, 128), WIDE)
            for k in range(0, fine, STRIP):
                near = held[8 + k : 24 + k + STRIP, :]
                pre = w[0] * near[7 : 7 + STRIP] + w[1] * near[8 : 8 + STRIP] + w[2] * near[9 : 9 + STRIP]
                bend, _, _ = gelu_parts(pre)
                act_ref[k : k + STRIP, cut] = (pre * (0.5 + 0.5 * bend)).astype(BF)

        if not ours:

            @pl.when(j >= steps)
            def _():
                for n in range(2):
                    at = pl.multiple_of((Spot(s_ref).their_first + 2 * (j - steps) + n) % 4 * quarter, 16)
                    prod_ref[n] = jnp.dot(
                        g_ref[pl.ds(at, quarter), :], act_ref[...], preferred_element_type=F32
                    ).astype(BF)

    def cols(count, full):
        def place(j, s_ref):
            n = jnp.minimum(j, steps - 1)
            return 0, (side(s_ref) * steps + n if full else n)

        return pl.BlockSpec((count, WIDE), place)

    def flat(count, width):
        return pl.BlockSpec((count, width), lambda j, s_ref: (0, 0))

    outs = [jax.ShapeDtypeStruct((fine + 2 * TAIL, half), BF)]
    out_specs = [cols(fine + 2 * TAIL, False)]
    scratch = []
    if ours:
        outs += [jax.ShapeDtypeStruct((fine, half), BF)]
        out_specs += [cols(fine, False)]
    else:
        outs += [jax.ShapeDtypeStruct((4, quarter, half), BF)]
        out_specs += [
            pl.BlockSpec((2, quarter, half), lambda j, s_ref: (jnp.maximum(j - steps, 0), 0, 0))
        ]
        scratch += [pltpu.VMEM((fine, half), BF)]
    scratch += [
        pltpu.VMEM((4, rows + TAIL, DV), BF),
        pltpu.VMEM((fine + 2 * TAIL, WIDE), F32),
    ]
    return pl.pallas_call(
        kernel,
        out_shape=outs,
        grid_spec=pltpu.PrefetchScalarGridSpec(
            num_scalar_prefetch=1,
            grid=(steps if ours else steps + 2,),
            in_specs=[flat(rows + rows // 2 + TAIL, 128)] * 4
            + [cols(TAIL, True), cols(TAIL, True), cols(3, True)]
            + [VMEM] * 4,
            out_specs=out_specs,
            scratch_shapes=scratch,
        ),
        compiler_params=params(24),
        cost_estimate=pl.CostEstimate(
            flops=2 * fine * columns * columns, bytes_accessed=9 << 20, transcendentals=fine * half
        ),
        name="forward",
    )(scalars, *back, before, after, depth_weight, tokens, skipped, out_heads, turned)


def load(behind, *arrays):
    count = len(arrays)

    def kernel(behind_ref, *refs):
        sems = refs[-1]
        copies = [pltpu.make_async_copy(refs[n], refs[count + n], sems.at[n]) for n in range(count)]
        for copy in copies:
            copy.start()
        for copy in copies:
            copy.wait()

    return pl.pallas_call(
        kernel,
        out_shape=[jax.ShapeDtypeStruct(a.shape, a.dtype) for a in arrays],
        in_specs=[ANY] * (1 + count),
        out_specs=[VMEM] * count,
        scratch_shapes=[pltpu.SemaphoreType.DMA((count,))],
        compiler_params=params(45),
        name="load",
    )(behind, *arrays)


def backward(scalars, theirs, ours, upstream, before, after, point_weight, depth_weight, behind):
    fine, columns = upstream.shape
    half = columns // 2
    steps = half // WIDE

    def kernel(s_ref, theirs_ref, ours_ref, g_ref, low_ref, high_ref, pw_ref, dw_ref, behind_ref, *refs):
        gs_ref, gd_theirs, gd_ours, grad, upper, ends, up_ref = refs
        j = pl.program_id(0)

        @pl.when(j < steps)
        def _():
            up_ref[...] = theirs_ref[...]

        @pl.when(j >= steps)
        def _():
            up_ref[...] = ours_ref[...]

        dims = (((1,), (1,)), ((), ()))

        @pl.when(pl.program_id(0) == 0)
        def _():
            row = lax.broadcasted_iota(jnp.int32, (TAIL, columns), 0)
            low, high = low_ref[...].astype(F32), high_ref[...].astype(F32)
            ends[...] = jnp.where(row == 7, low[3:4], jnp.where(row == 8, high[3:4], 0.0)).astype(BF)

        upper[...] = lax.dot_general(g_ref[...], pw_ref[...], dims, preferred_element_type=F32)
        outer = lax.dot_general(ends[...], pw_ref[...], dims, preferred_element_type=F32)
        w = [dw_ref[t : t + 1, :] for t in range(3)]

        def grad_of(near, start, count, coming):
            taps = [near[start - 1 + t : start - 1 + t + count] for t in range(3)]
            pre = w[0] * taps[0] + w[1] * taps[1] + w[2] * taps[2]
            bend, square, slope = gelu_parts(pre)
            rate = 0.5 + 0.5 * bend + (pre * (1.0 - bend * bend)) * (
                0.5 * slope + (1.5 * slope * 0.044715) * square
            )
            return taps, (coming * rate).astype(BF).astype(F32)

        _, grad[8:16, :] = grad_of(up_ref[:32, :].astype(F32), 8, 8, outer[:8])
        _, grad[16 + fine : 24 + fine, :] = grad_of(up_ref[fine:, :].astype(F32), 16, 8, outer[8:])
        sums = [jnp.zeros((8, WIDE), F32)] * 3
        for k in range(0, fine, STRIP):
            near = up_ref[k : k + STRIP + 2 * TAIL, :].astype(F32)
            taps, mid = grad_of(near, TAIL, STRIP, upper[k : k + STRIP, :])
            grad[16 + k : 16 + k + STRIP, :] = mid
            for t in range(3):
                term = taps[t] * mid
                for r in range(0, STRIP, 8):
                    sums[t] = sums[t] + term[r : r + 8]
        depth = [jnp.sum(total, axis=0, keepdims=True) for total in sums]
        for ref, mine in ((gd_theirs, j < steps), (gd_ours, j >= steps)):

            @pl.when(mine)
            def _():
                for t in range(3):
                    ref[t : t + 1, :] = depth[t]

        for k in range(0, fine, STRIP):
            near = grad[8 + k : 24 + k + STRIP, :]
            gs_ref[k : k + STRIP, :] = (
                w[0] * near[9 : 9 + STRIP] + w[1] * near[8 : 8 + STRIP] + w[2] * near[7 : 7 + STRIP]
            ).astype(BF)

    def block(j, s_ref):
        return jnp.where(j < steps, (1 - s_ref[1]) * steps + j, s_ref[1] * steps + j - steps)

    def cols(count):
        return pl.BlockSpec((count, WIDE), lambda j, s_ref: (0, block(j, s_ref)))

    def early(count):
        return pl.BlockSpec((count, WIDE), lambda j, s_ref: (0, jnp.minimum(j, steps - 1)))

    def late(count):
        return pl.BlockSpec((count, WIDE), lambda j, s_ref: (0, jnp.maximum(j - steps, 0)))

    def flat(count):
        return pl.BlockSpec((count, columns), lambda j, s_ref: (0, 0))

    return pl.pallas_call(
        kernel,
        out_shape=[
            jax.ShapeDtypeStruct((fine, columns), BF),
            jax.ShapeDtypeStruct((3, half), F32),
            jax.ShapeDtypeStruct((3, half), F32),
        ],
        grid_spec=pltpu.PrefetchScalarGridSpec(
            num_scalar_prefetch=1,
            grid=(2 * steps,),
            in_specs=[
                early(fine + 2 * TAIL),
                late(fine + 2 * TAIL),
                flat(fine),
                flat(TAIL),
                flat(TAIL),
                pl.BlockSpec((WIDE, columns), lambda j, s_ref: (block(j, s_ref), 0)),
                cols(3),
                ANY,
            ],
            out_specs=[cols(fine), early(3), late(3)],
            scratch_shapes=[
                pltpu.VMEM((fine + 2 * TAIL, WIDE), F32),
                pltpu.VMEM((fine, WIDE), F32),
                pltpu.VMEM((TAIL, columns), BF),
                pltpu.VMEM((fine + 2 * TAIL, WIDE), BF),
            ],
        ),
        compiler_params=params(48),
        cost_estimate=pl.CostEstimate(
            flops=2 * fine * columns * columns, bytes_accessed=11 << 20, transcendentals=fine * columns
        ),
        name="backward",
    )(scalars, theirs, ours, upstream, before, after, point_weight, depth_weight, behind)


def product(scalars, act, turned, steps, arrived):
    half, quarter = act.shape[1], turned.shape[0] // 4

    def kernel(s_ref, a_ref, g_ref, arrived_ref, *outs):
        for out, d in zip(outs, steps):
            at = pl.multiple_of((Spot(s_ref).first_at + d) % 4 * quarter, 16)
            block = jnp.dot(g_ref[pl.ds(at, quarter), :], a_ref[...], preferred_element_type=F32)
            out[...] = (block + arrived_ref[d].astype(F32)).astype(BF)

    return pl.pallas_call(
        kernel,
        out_shape=[jax.ShapeDtypeStruct((quarter, half), BF)] * len(steps),
        in_specs=[SMEM] + [VMEM] * 3,
        out_specs=[VMEM] * len(steps),
        compiler_params=params(14),
        cost_estimate=pl.CostEstimate(
            flops=2 * act.shape[0] * half * quarter * len(steps), bytes_accessed=6 << 20, transcendentals=0
        ),
        name="product",
    )(scalars, act, turned, arrived)


def split_rows(at, got):
    rows, columns = got[0].shape
    slim = rows // 4

    def kernel(at_ref, *refs):
        ins, outs = refs[:4], refs[4:]
        for d in range(4):
            take = pl.ds(pl.multiple_of((Spot(at_ref).second_at + d) % 4 * slim, 16), slim)
            outs[d][...] = total_of([r[take, :] for r in ins]).astype(BF)

    return pl.pallas_call(
        kernel,
        out_shape=[jax.ShapeDtypeStruct((slim, columns), BF)] * 4,
        in_specs=[SMEM] + [VMEM] * 4,
        out_specs=[VMEM] * 4,
        compiler_params=params(10),
        name="split_rows",
    )(at, *got)


def join_rows(at, got):
    slim, columns = got[0].shape[0] - TAIL, got[0].shape[1]
    quarter = 4 * slim

    def kernel(at_ref, *refs):
        ins, out, held = refs[:4], refs[4], refs[5]
        for d in range(4):
            put = pl.ds(pl.multiple_of((Spot(at_ref).second_at + 4 - d) % 4 * slim, 16), slim)
            held[put, :] = ins[d][:slim, :]
        out[:columns, :] = held[...].T
        last = total_of([r[slim:, :] for r in ins])[:8]
        out[columns:, :] = jnp.concatenate([last[:, :quarter], last[:, quarter:]], axis=0).astype(BF)

    return pl.pallas_call(
        kernel,
        out_shape=jax.ShapeDtypeStruct((columns + TAIL, quarter), BF),
        in_specs=[SMEM] + [VMEM] * 4,
        out_specs=VMEM,
        scratch_shapes=[pltpu.VMEM((quarter, columns), BF)],
        compiler_params=params(10),
        name="join_rows",
    )(at, *got)


def lay_out(scalars, own, other):
    half, quarter = own[0].shape[0] - TAIL, own[0].shape[1]
    parts = 4
    part = half // parts

    def kernel(s_ref, *refs):
        out, depth, sems = refs[-3:]
        spot = Spot(s_ref)
        copies = []
        for n in range(8):
            mine = n < 4
            down = (spot.core if mine else 1 - spot.core) * half
            over = ((spot.first_at if mine else spot.their_first) + 4 - n % 4) % 4 * quarter
            for k in range(parts):
                start = pl.multiple_of(down + k * part, 16)
                copies.append(
                    pltpu.make_async_copy(
                        refs[n].at[pl.ds(k * part, part), :],
                        out.at[pl.ds(start, part), pl.ds(pl.multiple_of(over, 128), quarter)],
                        sems.at[parts * n + k],
                    )
                )
        for copy in copies:
            copy.start()
        for n, side in ((0, spot.core), (4, 1 - spot.core)):
            rows = total_of([refs[n + d][half:, :] for d in range(4)])
            rows = jnp.concatenate([rows[:3], rows[8:11]], axis=1)
            depth[:, pl.ds(pl.multiple_of(side * half, 128), half)] = rows
        for copy in copies:
            copy.wait()

    return pl.pallas_call(
        kernel,
        out_shape=[
            jax.ShapeDtypeStruct((2 * half, 4 * quarter), BF),
            jax.ShapeDtypeStruct((3, 2 * half), F32),
        ],
        in_specs=[SMEM] + [VMEM] * 8,
        out_specs=[ANY, VMEM],
        scratch_shapes=[pltpu.SemaphoreType.DMA((8 * parts,))],
        compiler_params=params(12),
        name="lay_out",
    )(scalars, *own, *other)


def local(
    trunk,
    skip,
    valid_bins,
    query_weight,
    key_weight,
    value_weight,
    out_weight,
    depth_weight,
    point_weight,
    cotangent,
):
    tokens, skipped, upstream = trunk[0], skip[0], cotangent[0]
    rows, columns = tokens.shape
    fine = skipped.shape[0]
    ix, ic, iz, iy = (lax.axis_index(a) for a in AXES)
    spot = jnp.stack([v.astype(jnp.int32) for v in (ix, ic, iz, iy)])
    scalars = jnp.concatenate([spot, valid_bins.astype(jnp.int32)])
    blocks = project(tokens, query_weight, key_weight, value_weight)
    down, up = edges(blocks[0], tokens, skipped, upstream)
    before = lax.ppermute(down, ("z", "y"), [(i, i + 1) for i in range(15)])
    after = lax.ppermute(up, ("z", "y"), [(i + 1, i) for i in range(15)])
    blocks = exchange(blocks, HEAD_RING)
    own = stack_rows(blocks, down)
    q = spread(blocks)
    far = {d: lax.ppermute(own, AXES, turn(ROW_RING, d)) for d in (1, 3, 2)}
    state = attend(scalars, 0, q, [own], None)

    turned = upstream.T

    state = attend(scalars, 1, q, [far[1]], state)
    state = attend(scalars, 2, q, [far[3]], state)
    mixed = attend(scalars, 3, q, [own, far[1], far[3], far[2]], state, (before, after))
    back = exchange(mixed, HEAD_RING, -1)
    tokens_v, skipped_v, out_v = load(mixed[0], tokens, skipped, out_weight.reshape(H, DV, -1))
    swap = [(0, 1), (1, 0)]
    given = (back, tokens_v, skipped_v, out_v, before, after, depth_weight, turned)
    up_theirs, sent = forward(scalars, False, *given)
    arrived = lax.ppermute(sent, "c", swap)
    up_ours, act = forward(scalars, True, *given)
    piece_2, piece_1 = product(scalars, act, turned, (2, 1), arrived)
    piece_3, piece_0 = product(scalars, act, turned, (3, 0), arrived)
    got = exchange([piece_0, piece_1, piece_2, piece_3], SUM_RINGS[0])

    grad_skip, d_theirs, d_mine = backward(
        scalars, up_theirs, up_ours, upstream, before, after, point_weight, depth_weight, piece_0
    )
    d_sum = d_mine + lax.ppermute(d_theirs, "c", swap)
    rider = jnp.pad(d_sum.astype(BF), ((0, TAIL - 3), (0, 0)))

    got = exchange(split_rows(scalars, got), SUM_RINGS[1])
    mixed = jnp.concatenate([total_of(got).astype(BF), rider], axis=0)
    got = exchange([mixed] * 4, SUM_RINGS[2])
    norm_scale = 1.0 / math.sqrt(128 * fine)
    summed = (total_of(got) * norm_scale).astype(BF)
    joined = join_rows(scalars, exchange([summed] * 4, SUM_RINGS[1]))

    own = exchange([joined] * 4, SUM_RINGS[0])
    other = [lax.ppermute(block, "c", swap) for block in own]
    grad_pointwise, grad_depth = lay_out(scalars, own, other)
    return (grad_pointwise, grad_depth, grad_skip[None])


def solution(mesh):
    fine_mesh = Mesh(mesh.devices.reshape(SIZES), AXES)
    rows = P(("x", "c"), ("z", "y"), None)
    return jax.shard_map(
        local,
        mesh=fine_mesh,
        in_specs=(rows, rows, P(("x", "c")), P(), P(), P(), P(), P(), P(), rows),
        out_specs=(P(), P(), rows),
        check_vma=False,
    )
```

```python
import math

import jax
import jax.numpy as jnp
from jax import lax
from jax.experimental import pallas as pl
from jax.experimental.pallas import tpu as pltpu
from jax.sharding import Mesh, PartitionSpec as P

H = 4
DH = 64
DV = 192
AXES = ("x", "c", "z", "y")
SIZES = (4, 2, 4, 4)
BF = jnp.bfloat16
F32 = jnp.float32
TAIL = 16
VMEM = pl.BlockSpec(memory_space=pltpu.VMEM)
SMEM = pl.BlockSpec(memory_space=pltpu.SMEM)
ANY = pl.BlockSpec(memory_space=pl.ANY)
SUM_RINGS = (("x", "y"), ("y", "z"), ("z", "x"))
HEAD_RING = ("y", "z")
ROW_RING = ("z", "y")


class Spot:
    def __init__(self, s_ref):
        x, core, z, y = (s_ref[n] for n in range(4))
        first = core == 0
        self.core, self.y = core, y
        self.head_at = jnp.where(first, y, z)
        self.row_at = jnp.where(first, z, y)
        self.first_at = jnp.where(first, x, y)
        self.their_first = jnp.where(first, y, x)
        self.second_at = jnp.where(first, y, z)
        self.place = z * 4 + y

    def base(self, far_by, d):
        h, r = (self.head_at + 4 - d) % 4, (self.row_at + 4 - far_by) % 4
        return jnp.where(self.core == 0, r * 4 + h, h * 4 + r)

    def ring_place(self, d):
        return jnp.where(self.core == 0, (self.y + 4 - d) % 4, self.y)


def params(mib):
    return pltpu.CompilerParams(vmem_limit_bytes=mib << 20)


def turn(axes, step):
    pairs = []
    for x in range(4):
        for c in range(2):
            for z in range(4):
                for y in range(4):
                    at = {"x": x, "z": z, "y": y}
                    to = dict(at)
                    to[axes[c]] = (at[axes[c]] + step) % 4
                    flat = [((p["x"] * 2 + c) * 4 + p["z"]) * 4 + p["y"] for p in (at, to)]
                    pairs.append(tuple(flat))
    return pairs


def exchange(pieces, axes, sign=1):
    got = [pieces[0], None, None, None]
    for d in (2, 1, 3):
        got[d] = lax.ppermute(pieces[d], AXES, turn(axes, sign * d))
    return got


def total_of(got):
    a, b, c, d = (g.astype(F32) for g in got)
    return (a + c) + (b + d)


def project(tokens, query_weight, key_weight, value_weight):
    rows, depth = tokens.shape
    cut = depth // 2

    def kernel(tok_hbm, wq_hbm, wk_hbm, wv_hbm, *refs):
        head_at = jnp.where(lax.axis_index("c") == 0, lax.axis_index("y"), lax.axis_index("z"))
        outs, (tok_ref, wq_ref, wk_ref, wv_ref, held, sems) = refs[:4], refs[4:]
        low, high = pl.ds(0, cut), pl.ds(cut, depth - cut)
        copies = [
            pltpu.make_async_copy(tok_hbm, tok_ref, sems.at[0]),
            pltpu.make_async_copy(wv_hbm.at[low, :], wv_ref.at[low, :], sems.at[1]),
            pltpu.make_async_copy(wv_hbm.at[high, :], wv_ref.at[high, :], sems.at[2]),
            pltpu.make_async_copy(wk_hbm, wk_ref, sems.at[3]),
            pltpu.make_async_copy(wq_hbm, wq_ref, sems.at[4]),
        ]
        for copy in copies:
            copy.start()
        copies[0].wait()
        tok = tok_ref[...]
        copies[1].wait()
        v = jnp.dot(tok[:, :cut], wv_ref[:cut, :], preferred_element_type=F32)
        copies[2].wait()
        v += jnp.dot(tok[:, cut:], wv_ref[cut:, :], preferred_element_type=F32)
        copies[3].wait()
        k = jnp.dot(tok, wk_ref[...], preferred_element_type=F32)
        copies[4].wait()
        q = jnp.dot(tok, wq_ref[...], preferred_element_type=F32) * (1.0 / math.sqrt(DH))
        for h in range(H):
            part = slice(h * DH, (h + 1) * DH)
            held[h, :rows, :] = jnp.concatenate([v[:, h * DV : (h + 1) * DV], k[:, part]], axis=1).astype(BF)
            held[h, rows:, :] = jnp.concatenate(
                [q[n * rows // 4 : (n + 1) * rows // 4, part] for n in range(4)], axis=1
            ).astype(BF)
        for d in range(4):
            outs[d][...] = held[(head_at + d) % 4]

    return pl.pallas_call(
        kernel,
        out_shape=[jax.ShapeDtypeStruct((rows + rows // 4, 256), BF)] * 4,
        in_specs=[ANY] * 4,
        out_specs=[VMEM] * 4,
        scratch_shapes=[
            pltpu.VMEM((rows, depth), BF),
            pltpu.VMEM((depth, H * DH), BF),
            pltpu.VMEM((depth, H * DH), BF),
            pltpu.VMEM((depth, H * DV), BF),
            pltpu.VMEM((4, rows + rows // 4, 256), BF),
            pltpu.SemaphoreType.DMA((5,)),
        ],
        compiler_params=params(53),
        name="project",
    )(tokens, query_weight, key_weight, value_weight)


def stack_rows(parts, behind):
    rows = parts[0].shape[0] * 4 // 5

    def kernel(*refs):
        ins, out = refs[:4], refs[5]
        zero = jnp.zeros((1, DH), F32)
        row = lax.broadcasted_iota(jnp.int32, (TAIL, 128), 0)
        tail = jnp.zeros((TAIL, 128), F32)
        for d in range(4):
            out[d * rows : (d + 1) * rows, :] = ins[d][:rows, :]
            first = ins[d][rows : rows + TAIL, :].astype(F32)[:1, :DH]
            final = ins[d][rows + rows // 4 - TAIL :, :].astype(F32)[TAIL - 1 :, 3 * DH :]
            first, final = (jnp.concatenate([zero, r], axis=1) for r in (first, final))
            tail = jnp.where(row == d, first, tail)
            tail = jnp.where(row == 4 + d, final, tail)
        out[4 * rows :, :128] = jnp.zeros((TAIL, 128), BF)
        out[4 * rows :, 128:] = tail.astype(BF)

    return pl.pallas_call(
        kernel,
        out_shape=jax.ShapeDtypeStruct((4 * rows + TAIL, 256), BF),
        in_specs=[VMEM] * 4 + [ANY],
        out_specs=VMEM,
        compiler_params=params(8),
        name="stack_rows",
    )(*parts, behind)


def spread(parts):
    rows = parts[0].shape[0] * 4 // 5
    quarter = rows // 4

    def kernel(*refs):
        zero = jnp.zeros((quarter, DH), F32)
        for d in range(4):
            packed = refs[d][rows:, :].astype(F32)
            for n in range(4):
                refs[4 + d][n * quarter : (n + 1) * quarter, :] = jnp.concatenate(
                    [zero, packed[:, n * DH : (n + 1) * DH]], axis=1
                ).astype(BF)

    return pl.pallas_call(
        kernel,
        out_shape=[jax.ShapeDtypeStruct((rows, 128), BF)] * 4,
        in_specs=[VMEM] * 4,
        out_specs=[VMEM] * 4,
        compiler_params=params(8),
        name="spread",
    )(*parts)


def attend(scalars, near, q, pairs, state, behind=()):
    rows = q[0].shape[0]
    width = 4 * rows
    first = state is None
    last = len(pairs) == 4
    strip = 32

    def kernel(s_ref, *refs):
        spot = Spot(s_ref)
        score_ref, prob_ref, peak_ref = refs[-3:]
        q_refs, refs = refs[:4], refs[4:]
        pair_refs, refs = refs[: len(pairs)], refs[len(pairs) :]
        if not first:
            old, old_peak, refs = refs[0], refs[1], refs[2:]
        refs = refs[len(behind) :]
        lane = lax.broadcasted_iota(jnp.int32, (width, 256), 1)
        place = lax.broadcasted_iota(jnp.int32, (1, rows), 1)

        def masks(n):
            far_by = (0, 1, 3, 2)[n]
            return jnp.concatenate(
                [place + spot.base(far_by, i) * rows < s_ref[4] for i in range(4)], axis=1
            )

        def values_of(ref):
            return jnp.where(lane == DV, jnp.ones((), BF), ref[:width, :])

        def raw_scores(query, ref):
            return lax.dot_general(
                query, ref[:width, 128:], (((1,), (1,)), ((), ())), preferred_element_type=F32
            )

        def shares(sums):
            return sums / sums[:, DV : DV + 1]

        if last:
            tails = [r[width:, 128:].astype(F32) for r in pair_refs]
            own, low, high = tails[0], tails[1], tails[2]
            row = lax.broadcasted_iota(jnp.int32, (TAIL, 128), 0)
            edge = jnp.zeros((TAIL, 128), F32)
            for d in range(4):
                n, m = (d + 1) % 4, (d + 3) % 4
                at = spot.ring_place(d)
                other = jnp.where(spot.core == 0, own[4 + n : 5 + n], low[4 + d : 5 + d])
                prev = jnp.where(at == 0, low[4 + n : 5 + n], other)
                other = jnp.where(spot.core == 0, own[m : m + 1], high[d : d + 1])
                nxt = jnp.where(at == 3, high[m : m + 1], other)
                edge = jnp.where(row == d, prev, edge)
                edge = jnp.where(row == 4 + d, nxt, edge)
            edge = edge.astype(BF)
            parts = [jnp.where(masks(n), raw_scores(edge, r), -1e30) for n, r in enumerate(pair_refs)]
            peak = jnp.max(parts[0], axis=1, keepdims=True)
            for s in parts[1:]:
                peak = jnp.maximum(peak, jnp.max(s, axis=1, keepdims=True))
            edge_sums = jnp.zeros((TAIL, 256), F32)
            for s, r in zip(parts, pair_refs):
                edge_sums += jnp.dot(jnp.exp(s - peak).astype(BF), values_of(r), preferred_element_type=F32)
            edge_out = shares(edge_sums)

        pair_ref = pair_refs[-1]
        keep = masks(near)
        values = values_of(pair_ref)
        for i in range(4):
            score_ref[i] = raw_scores(q_refs[i][...], pair_ref)
        for i in range(4):
            for k in range(0, rows, strip):
                cut = slice(k, k + strip)
                scores = jnp.where(keep, score_ref[i, cut, :], -1e30)
                peak = jnp.broadcast_to(jnp.max(scores, axis=1, keepdims=True), (strip, 128))
                if not first:
                    peak = jnp.maximum(peak, old_peak[i * rows + k : i * rows + k + strip, :])
                across = jnp.concatenate([peak] * (width // 128), axis=1)
                prob_ref[i, cut, :] = jnp.exp(scores - across).astype(BF)
                peak_ref[i, cut, :] = peak
            update = jnp.dot(prob_ref[i], values, preferred_element_type=F32)
            if not first:
                shrink = jnp.exp(old_peak[i * rows : (i + 1) * rows, :] - peak_ref[i])
                update = update + old[i * rows : (i + 1) * rows, :] * jnp.concatenate([shrink] * 2, axis=1)
            if last:
                share = shares(update)
                high = share[:, 128:DV]
                refs[i][:rows, :] = share[:, :128].astype(BF)
                refs[i][rows : rows + rows // 2, :] = jnp.concatenate(
                    [high[: rows // 2], high[rows // 2 :]], axis=1
                ).astype(BF)
                ends = jnp.zeros((TAIL, 128), F32)
                for n in range(4):
                    at = i + 4 * (n % 2)
                    part = edge_out[at : at + 1, :128] if n < 2 else edge_out[at : at + 1, 128:]
                    ends = jnp.where(row == n, part, ends)
                refs[i][rows + rows // 2 :, :] = ends.astype(BF)
            else:
                refs[0][i * rows : (i + 1) * rows, :] = update
                refs[1][i * rows : (i + 1) * rows, :] = peak_ref[i]

    ins = [*q, *pairs]
    if not first:
        ins += [*state]
    if last:
        outs = [jax.ShapeDtypeStruct((rows + rows // 2 + TAIL, 128), BF)] * 4
    else:
        outs = [jax.ShapeDtypeStruct((4 * rows, n), F32) for n in (256, 128)]
    return pl.pallas_call(
        kernel,
        out_shape=outs,
        in_specs=[SMEM] + [VMEM] * len(ins) + [ANY] * len(behind),
        out_specs=[VMEM] * len(outs),
        scratch_shapes=[
            pltpu.VMEM((4, rows, width), F32),
            pltpu.VMEM((4, rows, width), BF),
            pltpu.VMEM((4, rows, 128), F32),
        ],
        compiler_params=params(24),
        cost_estimate=pl.CostEstimate(
            flops=4 * 2 * rows * width * 512, bytes_accessed=4 << 20, transcendentals=4 * rows * width
        ),
        name="attend",
    )(scalars, *ins, *behind)


def edges(mark, trunk, skip, cotangent):
    columns = trunk.shape[1]

    def kernel(mark_ref, t_ref, s_ref, c_ref, down, up, buffer, sems):
        copies = []
        for n, ref in enumerate((t_ref, s_ref, c_ref)):
            for end in range(2):
                start = end * (ref.shape[0] - TAIL)
                copies.append(
                    pltpu.make_async_copy(
                        ref.at[pl.ds(start, TAIL), :], buffer.at[2 * n + end], sems.at[2 * n + end]
                    )
                )
        for copy in copies:
            copy.start()
        for copy in copies:
            copy.wait()
        t_first, t_last, s_first, s_last, c_first, c_last = (buffer[n].astype(F32) for n in range(6))
        row = lax.broadcasted_iota(jnp.int32, (TAIL, columns), 0)

        def four(a, b, c, d):
            rest = jnp.where(row == 2, c, jnp.where(row == 3, d, 0.0))
            return jnp.where(row == 0, a, jnp.where(row == 1, b, rest)).astype(BF)

        up[...] = four(t_first[:1], s_first[:1], s_first[1:2], c_first[:1])
        e = TAIL - 1
        down[...] = four(t_last[e:], s_last[e - 1 : e], s_last[e:], c_last[e:])

    return pl.pallas_call(
        kernel,
        out_shape=[jax.ShapeDtypeStruct((TAIL, columns), BF)] * 2,
        in_specs=[ANY] * 4,
        out_specs=[VMEM] * 2,
        scratch_shapes=[pltpu.VMEM((6, TAIL, columns), BF), pltpu.SemaphoreType.DMA((6,))],
        compiler_params=params(53),
        name="edges",
    )(mark, trunk, skip, cotangent)


def gelu_parts(pre):
    slope = math.sqrt(2.0 / math.pi)
    square = pre * pre
    bend = jnp.tanh(slope * (pre + 0.044715 * (square * pre)))
    return bend, square, slope


WIDE = 384
STRIP = 32


def forward(scalars, ours, back, tokens, skipped, out_heads, before, after, depth_weight, turned):
    rows, columns = tokens.shape
    fine = 2 * rows
    half = columns // 2
    steps = half // WIDE
    quarter = columns // 4

    def side(s_ref):
        return s_ref[1] if ours else 1 - s_ref[1]

    def kernel(s_ref, b0, b1, b2, b3, low_ref, high_ref, dw_ref, tok_ref, skip_ref, ow_ref, g_ref, *refs):
        if ours:
            up_ref, act_ref = refs[:2]
            refs = refs[2:]
        else:
            up_ref, prod_ref, act_ref = refs[:3]
            refs = refs[3:]
        att, held = refs
        j = pl.program_id(0)

        @pl.when(j == 0)
        def _():
            mixed = []
            for b in (b0, b1, b2, b3):
                pair = b[rows : rows + rows // 2, :].astype(F32)
                last = b[rows + rows // 2 :, :].astype(F32)
                high = jnp.concatenate(
                    [pair[:, :64], pair[:, 64:], last[2:4, :64], jnp.zeros((TAIL - 2, 64), F32)], axis=0
                )
                left = jnp.concatenate([b[:rows, :].astype(F32), last], axis=0)
                mixed.append(jnp.concatenate([left, high], axis=1))
            squares = sum(jnp.sum(m * m, axis=1, keepdims=True) for m in mixed)
            scale = lax.rsqrt(squares * (1.0 / (H * DV)) + 1e-05)
            for d in range(4):
                att[d] = (mixed[d] * scale).astype(BF)

        @pl.when(j < steps)
        def _():
            spot = Spot(s_ref)
            n = jnp.minimum(j, steps - 1)
            take = pl.ds(pl.multiple_of((side(s_ref) * steps + n) * WIDE, 128), WIDE)
            low, high = low_ref[...].astype(F32), high_ref[...].astype(F32)
            grown = jnp.zeros((rows + TAIL, WIDE), F32)
            for d in range(4):
                grown += jnp.dot(att[d], ow_ref[(spot.head_at + d) % 4, :, take], preferred_element_type=F32)
            hidden = (tok_ref[:, take].astype(F32) + grown[:rows]).astype(BF)
            low_hid = (low[:1] + grown[rows : rows + 1]).astype(BF).astype(F32)
            high_hid = (high[:1] + grown[rows + 1 : rows + 2]).astype(BF).astype(F32)
            twice = lax.broadcasted_iota(jnp.int32, (fine, rows), 0) // 2
            twice = jnp.where(twice == lax.broadcasted_iota(jnp.int32, (fine, rows), 1), 1.0, 0.0).astype(BF)
            doubled = jnp.dot(twice, hidden, preferred_element_type=F32)
            row = lax.broadcasted_iota(jnp.int32, (TAIL, WIDE), 0)
            edge = (low_hid + jnp.where(row == 14, low[1:2], low[2:3])).astype(BF).astype(F32)
            edge = jnp.where((row >= 14) & (spot.place > 0), edge, 0.0)
            held[:TAIL, :] = edge
            up_ref[:TAIL, :] = edge.astype(BF)
            edge = (high_hid + jnp.where(row == 0, high[1:2], high[2:3])).astype(BF).astype(F32)
            edge = jnp.where((row < 2) & (spot.place < 15), edge, 0.0)
            held[TAIL + fine :, :] = edge
            up_ref[TAIL + fine :, :] = edge.astype(BF)
            for k in range(0, fine, STRIP):
                up = (doubled[k : k + STRIP] + skip_ref[k : k + STRIP, take].astype(F32)).astype(BF)
                up_ref[TAIL + k : TAIL + k + STRIP, :] = up
                held[TAIL + k : TAIL + k + STRIP, :] = up.astype(F32)
            w = [dw_ref[t : t + 1, :] for t in range(3)]
            cut = pl.ds(0 if ours else pl.multiple_of(n * WIDE, 128), WIDE)
            for k in range(0, fine, STRIP):
                near = held[8 + k : 24 + k + STRIP, :]
                pre = w[0] * near[7 : 7 + STRIP] + w[1] * near[8 : 8 + STRIP] + w[2] * near[9 : 9 + STRIP]
                bend, _, _ = gelu_parts(pre)
                act_ref[k : k + STRIP, cut] = (pre * (0.5 + 0.5 * bend)).astype(BF)

        if not ours:

            @pl.when(j >= steps)
            def _():
                for n in range(2):
                    at = pl.multiple_of((Spot(s_ref).their_first + 2 * (j - steps) + n) % 4 * quarter, 16)
                    prod_ref[n] = jnp.dot(
                        g_ref[pl.ds(at, quarter), :], act_ref[...], preferred_element_type=F32
                    ).astype(BF)

    def cols(count, full):
        def place(j, s_ref):
            n = jnp.minimum(j, steps - 1)
            return 0, (side(s_ref) * steps + n if full else n)

        return pl.BlockSpec((count, WIDE), place)

    def flat(count, width):
        return pl.BlockSpec((count, width), lambda j, s_ref: (0, 0))

    outs = [jax.ShapeDtypeStruct((fine + 2 * TAIL, half), BF)]
    out_specs = [cols(fine + 2 * TAIL, False)]
    scratch = []
    if ours:
        outs += [jax.ShapeDtypeStruct((fine, half), BF)]
        out_specs += [cols(fine, False)]
    else:
        outs += [jax.ShapeDtypeStruct((4, quarter, half), BF)]
        out_specs += [
            pl.BlockSpec((2, quarter, half), lambda j, s_ref: (jnp.maximum(j - steps, 0), 0, 0))
        ]
        scratch += [pltpu.VMEM((fine, half), BF)]
    scratch += [
        pltpu.VMEM((4, rows + TAIL, DV), BF),
        pltpu.VMEM((fine + 2 * TAIL, WIDE), F32),
    ]
    return pl.pallas_call(
        kernel,
        out_shape=outs,
        grid_spec=pltpu.PrefetchScalarGridSpec(
            num_scalar_prefetch=1,
            grid=(steps if ours else steps + 2,),
            in_specs=[flat(rows + rows // 2 + TAIL, 128)] * 4
            + [cols(TAIL, True), cols(TAIL, True), cols(3, True)]
            + [VMEM] * 4,
            out_specs=out_specs,
            scratch_shapes=scratch,
        ),
        compiler_params=params(24),
        cost_estimate=pl.CostEstimate(
            flops=2 * fine * columns * columns, bytes_accessed=9 << 20, transcendentals=fine * half
        ),
        name="forward",
    )(scalars, *back, before, after, depth_weight, tokens, skipped, out_heads, turned)


def load(behind, *arrays):
    count = len(arrays)

    def kernel(behind_ref, *refs):
        sems = refs[-1]
        copies = [pltpu.make_async_copy(refs[n], refs[count + n], sems.at[n]) for n in range(count)]
        for copy in copies:
            copy.start()
        for copy in copies:
            copy.wait()

    return pl.pallas_call(
        kernel,
        out_shape=[jax.ShapeDtypeStruct(a.shape, a.dtype) for a in arrays],
        in_specs=[ANY] * (1 + count),
        out_specs=[VMEM] * count,
        scratch_shapes=[pltpu.SemaphoreType.DMA((count,))],
        compiler_params=params(45),
        name="load",
    )(behind, *arrays)


def backward(scalars, theirs, ours, upstream, before, after, point_weight, depth_weight, behind):
    fine, columns = upstream.shape
    half = columns // 2
    steps = half // WIDE

    def kernel(s_ref, theirs_ref, ours_ref, g_ref, low_ref, high_ref, pw_ref, dw_ref, behind_ref, *refs):
        grad_ref, gd_theirs, gd_ours, upper, ends, up_ref = refs
        j = pl.program_id(0)

        @pl.when(j < steps)
        def _():
            up_ref[...] = theirs_ref[...]

        @pl.when(j >= steps)
        def _():
            up_ref[...] = ours_ref[...]

        dims = (((1,), (1,)), ((), ()))

        @pl.when(pl.program_id(0) == 0)
        def _():
            row = lax.broadcasted_iota(jnp.int32, (TAIL, columns), 0)
            low, high = low_ref[...].astype(F32), high_ref[...].astype(F32)
            ends[...] = jnp.where(row == 7, low[3:4], jnp.where(row == 8, high[3:4], 0.0)).astype(BF)

        upper[...] = lax.dot_general(g_ref[...], pw_ref[...], dims, preferred_element_type=F32)
        outer = lax.dot_general(ends[...], pw_ref[...], dims, preferred_element_type=F32)
        w = [dw_ref[t : t + 1, :] for t in range(3)]

        def grad_of(near, start, count, coming):
            taps = [near[start - 1 + t : start - 1 + t + count] for t in range(3)]
            pre = w[0] * taps[0] + w[1] * taps[1] + w[2] * taps[2]
            bend, square, slope = gelu_parts(pre)
            rate = 0.5 + 0.5 * bend + (pre * (1.0 - bend * bend)) * (
                0.5 * slope + (1.5 * slope * 0.044715) * square
            )
            return taps, (coming * rate).astype(BF).astype(F32)

        blank = jnp.zeros((8, WIDE), F32)
        _, edge = grad_of(up_ref[:32, :].astype(F32), 8, 8, outer[:8])
        grad_ref[:TAIL, :] = jnp.concatenate([blank, edge], axis=0).astype(BF)
        _, edge = grad_of(up_ref[fine:, :].astype(F32), 16, 8, outer[8:])
        grad_ref[TAIL + fine :, :] = jnp.concatenate([edge, blank], axis=0).astype(BF)
        sums = [jnp.zeros((8, WIDE), F32)] * 3
        for k in range(0, fine, STRIP):
            near = up_ref[k : k + STRIP + 2 * TAIL, :].astype(F32)
            taps, mid = grad_of(near, TAIL, STRIP, upper[k : k + STRIP, :])
            grad_ref[TAIL + k : TAIL + k + STRIP, :] = mid.astype(BF)
            for t in range(3):
                term = taps[t] * mid
                for r in range(0, STRIP, 8):
                    sums[t] = sums[t] + term[r : r + 8]
        depth = [jnp.sum(total, axis=0, keepdims=True) for total in sums]
        for ref, mine in ((gd_theirs, j < steps), (gd_ours, j >= steps)):

            @pl.when(mine)
            def _():
                for t in range(3):
                    ref[t : t + 1, :] = depth[t]

    def block(j, s_ref):
        return jnp.where(j < steps, (1 - s_ref[1]) * steps + j, s_ref[1] * steps + j - steps)

    def cols(count):
        return pl.BlockSpec((count, WIDE), lambda j, s_ref: (0, block(j, s_ref)))

    def early(count):
        return pl.BlockSpec((count, WIDE), lambda j, s_ref: (0, jnp.minimum(j, steps - 1)))

    def late(count):
        return pl.BlockSpec((count, WIDE), lambda j, s_ref: (0, jnp.maximum(j - steps, 0)))

    def flat(count):
        return pl.BlockSpec((count, columns), lambda j, s_ref: (0, 0))

    return pl.pallas_call(
        kernel,
        out_shape=[
            jax.ShapeDtypeStruct((fine + 2 * TAIL, columns), BF),
            jax.ShapeDtypeStruct((3, half), F32),
            jax.ShapeDtypeStruct((3, half), F32),
        ],
        grid_spec=pltpu.PrefetchScalarGridSpec(
            num_scalar_prefetch=1,
            grid=(2 * steps,),
            in_specs=[
                early(fine + 2 * TAIL),
                late(fine + 2 * TAIL),
                flat(fine),
                flat(TAIL),
                flat(TAIL),
                pl.BlockSpec((WIDE, columns), lambda j, s_ref: (block(j, s_ref), 0)),
                cols(3),
                ANY,
            ],
            out_specs=[cols(fine + 2 * TAIL), early(3), late(3)],
            scratch_shapes=[
                pltpu.VMEM((fine, WIDE), F32),
                pltpu.VMEM((TAIL, columns), BF),
                pltpu.VMEM((fine + 2 * TAIL, WIDE), BF),
            ],
        ),
        compiler_params=params(48),
        cost_estimate=pl.CostEstimate(
            flops=2 * fine * columns * columns, bytes_accessed=11 << 20, transcendentals=fine * columns
        ),
        name="backward",
    )(scalars, theirs, ours, upstream, before, after, point_weight, depth_weight, behind)


def spread_back(grad_pre, depth_weight):
    fine, columns = grad_pre.shape[0] - 2 * TAIL, grad_pre.shape[1]

    def kernel(grad_ref, dw_ref, gs_ref, mark_ref):
        mark_ref[...] = jnp.zeros((8, 128), F32)
        w = [dw_ref[t : t + 1, :] for t in range(3)]
        for k in range(0, fine, STRIP):
            near = grad_ref[k : k + STRIP + 2 * TAIL, :].astype(F32)
            gs_ref[k : k + STRIP, :] = (
                w[0] * near[TAIL + 1 : TAIL + 1 + STRIP]
                + w[1] * near[TAIL : TAIL + STRIP]
                + w[2] * near[TAIL - 1 : TAIL - 1 + STRIP]
            ).astype(BF)

    def cols(count):
        return pl.BlockSpec((count, WIDE), lambda j: (0, j))

    return pl.pallas_call(
        kernel,
        grid=(columns // WIDE,),
        out_shape=[jax.ShapeDtypeStruct((fine, columns), BF), jax.ShapeDtypeStruct((8, 128), F32)],
        in_specs=[cols(fine + 2 * TAIL), cols(3)],
        out_specs=[cols(fine), pl.BlockSpec((8, 128), lambda j: (0, 0))],
        compiler_params=params(16),
        name="spread_back",
    )(grad_pre, depth_weight)


def product(scalars, act, turned, steps, arrived):
    half, quarter = act.shape[1], turned.shape[0] // 4

    def kernel(s_ref, a_ref, g_ref, arrived_ref, *outs):
        for out, d in zip(outs, steps):
            at = pl.multiple_of((Spot(s_ref).first_at + d) % 4 * quarter, 16)
            block = jnp.dot(g_ref[pl.ds(at, quarter), :], a_ref[...], preferred_element_type=F32)
            out[...] = (block + arrived_ref[d].astype(F32)).astype(BF)

    return pl.pallas_call(
        kernel,
        out_shape=[jax.ShapeDtypeStruct((quarter, half), BF)] * len(steps),
        in_specs=[SMEM] + [VMEM] * 3,
        out_specs=[VMEM] * len(steps),
        compiler_params=params(14),
        cost_estimate=pl.CostEstimate(
            flops=2 * act.shape[0] * half * quarter * len(steps), bytes_accessed=6 << 20, transcendentals=0
        ),
        name="product",
    )(scalars, act, turned, arrived)


def split_rows(at, got):
    rows, columns = got[0].shape
    slim = rows // 4

    def kernel(at_ref, *refs):
        ins, outs = refs[:4], refs[4:]
        for d in range(4):
            take = pl.ds(pl.multiple_of((Spot(at_ref).second_at + d) % 4 * slim, 16), slim)
            outs[d][...] = total_of([r[take, :] for r in ins]).astype(BF)

    return pl.pallas_call(
        kernel,
        out_shape=[jax.ShapeDtypeStruct((slim, columns), BF)] * 4,
        in_specs=[SMEM] + [VMEM] * 4,
        out_specs=[VMEM] * 4,
        compiler_params=params(10),
        name="split_rows",
    )(at, *got)


def join_rows(at, got, behind):
    slim, columns = got[0].shape[0] - TAIL, got[0].shape[1]
    quarter = 4 * slim

    def kernel(at_ref, *refs):
        ins, out, held = refs[:4], refs[5], refs[6]
        for d in range(4):
            put = pl.ds(pl.multiple_of((Spot(at_ref).second_at + 4 - d) % 4 * slim, 16), slim)
            held[put, :] = ins[d][:slim, :]
        out[:columns, :] = held[...].T
        last = total_of([r[slim:, :] for r in ins])[:8]
        out[columns:, :] = jnp.concatenate([last[:, :quarter], last[:, quarter:]], axis=0).astype(BF)

    return pl.pallas_call(
        kernel,
        out_shape=jax.ShapeDtypeStruct((columns + TAIL, quarter), BF),
        in_specs=[SMEM] + [VMEM] * 4 + [ANY],
        out_specs=VMEM,
        scratch_shapes=[pltpu.VMEM((quarter, columns), BF)],
        compiler_params=params(10),
        name="join_rows",
    )(at, *got, behind)


def lay_out(scalars, own, other):
    half, quarter = own[0].shape[0] - TAIL, own[0].shape[1]
    parts = 4
    part = half // parts

    def kernel(s_ref, *refs):
        out, depth, sems = refs[-3:]
        spot = Spot(s_ref)
        copies = []
        for n in range(8):
            mine = n < 4
            down = (spot.core if mine else 1 - spot.core) * half
            over = ((spot.first_at if mine else spot.their_first) + 4 - n % 4) % 4 * quarter
            for k in range(parts):
                start = pl.multiple_of(down + k * part, 16)
                copies.append(
                    pltpu.make_async_copy(
                        refs[n].at[pl.ds(k * part, part), :],
                        out.at[pl.ds(start, part), pl.ds(pl.multiple_of(over, 128), quarter)],
                        sems.at[parts * n + k],
                    )
                )
        for copy in copies:
            copy.start()
        for n, side in ((0, spot.core), (4, 1 - spot.core)):
            rows = total_of([refs[n + d][half:, :] for d in range(4)])
            rows = jnp.concatenate([rows[:3], rows[8:11]], axis=1)
            depth[:, pl.ds(pl.multiple_of(side * half, 128), half)] = rows
        for copy in copies:
            copy.wait()

    return pl.pallas_call(
        kernel,
        out_shape=[
            jax.ShapeDtypeStruct((2 * half, 4 * quarter), BF),
            jax.ShapeDtypeStruct((3, 2 * half), F32),
        ],
        in_specs=[SMEM] + [VMEM] * 8,
        out_specs=[ANY, VMEM],
        scratch_shapes=[pltpu.SemaphoreType.DMA((8 * parts,))],
        compiler_params=params(12),
        name="lay_out",
    )(scalars, *own, *other)


def local(
    trunk,
    skip,
    valid_bins,
    query_weight,
    key_weight,
    value_weight,
    out_weight,
    depth_weight,
    point_weight,
    cotangent,
):
    tokens, skipped, upstream = trunk[0], skip[0], cotangent[0]
    rows, columns = tokens.shape
    fine = skipped.shape[0]
    ix, ic, iz, iy = (lax.axis_index(a) for a in AXES)
    spot = jnp.stack([v.astype(jnp.int32) for v in (ix, ic, iz, iy)])
    scalars = jnp.concatenate([spot, valid_bins.astype(jnp.int32)])
    blocks = project(tokens, query_weight, key_weight, value_weight)
    down, up = edges(blocks[0], tokens, skipped, upstream)
    before = lax.ppermute(down, ("z", "y"), [(i, i + 1) for i in range(15)])
    after = lax.ppermute(up, ("z", "y"), [(i + 1, i) for i in range(15)])
    blocks = exchange(blocks, HEAD_RING)
    own = stack_rows(blocks, down)
    q = spread(blocks)
    far = {d: lax.ppermute(own, AXES, turn(ROW_RING, d)) for d in (1, 3, 2)}
    state = attend(scalars, 0, q, [own], None)

    turned = upstream.T

    state = attend(scalars, 1, q, [far[1]], state)
    state = attend(scalars, 2, q, [far[3]], state)
    mixed = attend(scalars, 3, q, [own, far[1], far[3], far[2]], state, (before, after))
    back = exchange(mixed, HEAD_RING, -1)
    tokens_v, skipped_v, out_v = load(mixed[0], tokens, skipped, out_weight.reshape(H, DV, -1))
    swap = [(0, 1), (1, 0)]
    given = (back, tokens_v, skipped_v, out_v, before, after, depth_weight, turned)
    up_theirs, sent = forward(scalars, False, *given)
    arrived = lax.ppermute(sent, "c", swap)
    up_ours, act = forward(scalars, True, *given)
    piece_2, piece_1 = product(scalars, act, turned, (2, 1), arrived)
    piece_3, piece_0 = product(scalars, act, turned, (3, 0), arrived)
    got = exchange([piece_0, piece_1, piece_2, piece_3], SUM_RINGS[0])

    grad_pre, d_theirs, d_mine = backward(
        scalars, up_theirs, up_ours, upstream, before, after, point_weight, depth_weight, piece_0
    )
    d_sum = d_mine + lax.ppermute(d_theirs, "c", swap)
    rider = jnp.pad(d_sum.astype(BF), ((0, TAIL - 3), (0, 0)))

    got = exchange(split_rows(scalars, got), SUM_RINGS[1])
    mixed = jnp.concatenate([total_of(got).astype(BF), rider], axis=0)
    got = exchange([mixed] * 4, SUM_RINGS[2])
    norm_scale = 1.0 / math.sqrt(128 * fine)
    summed = (total_of(got) * norm_scale).astype(BF)
    grad_skip, mark = spread_back(grad_pre, depth_weight)
    joined = join_rows(scalars, exchange([summed] * 4, SUM_RINGS[1]), mark)

    own = exchange([joined] * 4, SUM_RINGS[0])
    other = [lax.ppermute(block, "c", swap) for block in own]
    grad_pointwise, grad_depth = lay_out(scalars, own, other)
    return (grad_pointwise, grad_depth, grad_skip[None])


def solution(mesh):
    fine_mesh = Mesh(mesh.devices.reshape(SIZES), AXES)
    rows = P(("x", "c"), ("z", "y"), None)
    return jax.shard_map(
        local,
        mesh=fine_mesh,
        in_specs=(rows, rows, P(("x", "c")), P(), P(), P(), P(), P(), P(), rows),
        out_specs=(P(), P(), rows),
        check_vma=False,
    )
```

```python
import math

import jax
import jax.numpy as jnp
from jax import lax
from jax.experimental import pallas as pl
from jax.experimental.pallas import tpu as pltpu
from jax.sharding import Mesh, PartitionSpec as P

H = 4
DH = 64
DV = 192
AXES = ("x", "c", "z", "y")
SIZES = (4, 2, 4, 4)
BF = jnp.bfloat16
F32 = jnp.float32
TAIL = 16
VMEM = pl.BlockSpec(memory_space=pltpu.VMEM)
SMEM = pl.BlockSpec(memory_space=pltpu.SMEM)
ANY = pl.BlockSpec(memory_space=pl.ANY)
SUM_RINGS = (("x", "y"), ("y", "z"), ("z", "x"))
HEAD_RING = ("y", "z")
ROW_RING = ("z", "y")


class Spot:
    def __init__(self, s_ref):
        x, core, z, y = (s_ref[n] for n in range(4))
        first = core == 0
        self.core, self.y = core, y
        self.head_at = jnp.where(first, y, z)
        self.row_at = jnp.where(first, z, y)
        self.first_at = jnp.where(first, x, y)
        self.their_first = jnp.where(first, y, x)
        self.second_at = jnp.where(first, y, z)
        self.place = z * 4 + y

    def base(self, far_by, d):
        h, r = (self.head_at + 4 - d) % 4, (self.row_at + 4 - far_by) % 4
        return jnp.where(self.core == 0, r * 4 + h, h * 4 + r)

    def ring_place(self, d):
        return jnp.where(self.core == 0, (self.y + 4 - d) % 4, self.y)


def params(mib):
    return pltpu.CompilerParams(vmem_limit_bytes=mib << 20)


def turn(axes, step):
    pairs = []
    for x in range(4):
        for c in range(2):
            for z in range(4):
                for y in range(4):
                    at = {"x": x, "z": z, "y": y}
                    to = dict(at)
                    to[axes[c]] = (at[axes[c]] + step) % 4
                    flat = [((p["x"] * 2 + c) * 4 + p["z"]) * 4 + p["y"] for p in (at, to)]
                    pairs.append(tuple(flat))
    return pairs


def exchange(pieces, axes, sign=1):
    got = [pieces[0], None, None, None]
    for d in (2, 1, 3):
        got[d] = lax.ppermute(pieces[d], AXES, turn(axes, sign * d))
    return got


def total_of(got):
    a, b, c, d = (g.astype(F32) for g in got)
    return (a + c) + (b + d)


def project(tokens, query_weight, key_weight, value_weight):
    rows, depth = tokens.shape
    cut = depth // 2

    def kernel(tok_hbm, wq_hbm, wk_hbm, wv_hbm, *refs):
        head_at = jnp.where(lax.axis_index("c") == 0, lax.axis_index("y"), lax.axis_index("z"))
        outs, (tok_ref, wq_ref, wk_ref, wv_ref, held, sems) = refs[:4], refs[4:]
        low, high = pl.ds(0, cut), pl.ds(cut, depth - cut)
        copies = [
            pltpu.make_async_copy(tok_hbm, tok_ref, sems.at[0]),
            pltpu.make_async_copy(wv_hbm.at[low, :], wv_ref.at[low, :], sems.at[1]),
            pltpu.make_async_copy(wv_hbm.at[high, :], wv_ref.at[high, :], sems.at[2]),
            pltpu.make_async_copy(wk_hbm, wk_ref, sems.at[3]),
            pltpu.make_async_copy(wq_hbm, wq_ref, sems.at[4]),
        ]
        for copy in copies:
            copy.start()
        copies[0].wait()
        tok = tok_ref[...]
        copies[1].wait()
        v = jnp.dot(tok[:, :cut], wv_ref[:cut, :], preferred_element_type=F32)
        copies[2].wait()
        v += jnp.dot(tok[:, cut:], wv_ref[cut:, :], preferred_element_type=F32)
        copies[3].wait()
        k = jnp.dot(tok, wk_ref[...], preferred_element_type=F32)
        copies[4].wait()
        q = jnp.dot(tok, wq_ref[...], preferred_element_type=F32) * (1.0 / math.sqrt(DH))
        for h in range(H):
            part = slice(h * DH, (h + 1) * DH)
            held[h, :rows, :] = jnp.concatenate([v[:, h * DV : (h + 1) * DV], k[:, part]], axis=1).astype(BF)
            held[h, rows:, :] = jnp.concatenate(
                [q[n * rows // 4 : (n + 1) * rows // 4, part] for n in range(4)], axis=1
            ).astype(BF)
        for d in range(4):
            outs[d][...] = held[(head_at + d) % 4]

    return pl.pallas_call(
        kernel,
        out_shape=[jax.ShapeDtypeStruct((rows + rows // 4, 256), BF)] * 4,
        in_specs=[ANY] * 4,
        out_specs=[VMEM] * 4,
        scratch_shapes=[
            pltpu.VMEM((rows, depth), BF),
            pltpu.VMEM((depth, H * DH), BF),
            pltpu.VMEM((depth, H * DH), BF),
            pltpu.VMEM((depth, H * DV), BF),
            pltpu.VMEM((4, rows + rows // 4, 256), BF),
            pltpu.SemaphoreType.DMA((5,)),
        ],
        compiler_params=params(53),
        name="project",
    )(tokens, query_weight, key_weight, value_weight)


def stack_rows(parts, behind):
    rows = parts[0].shape[0] * 4 // 5

    def kernel(*refs):
        ins, out = refs[:4], refs[5]
        zero = jnp.zeros((1, DH), F32)
        row = lax.broadcasted_iota(jnp.int32, (TAIL, 128), 0)
        tail = jnp.zeros((TAIL, 128), F32)
        for d in range(4):
            out[d * rows : (d + 1) * rows, :] = ins[d][:rows, :]
            first = ins[d][rows : rows + TAIL, :].astype(F32)[:1, :DH]
            final = ins[d][rows + rows // 4 - TAIL :, :].astype(F32)[TAIL - 1 :, 3 * DH :]
            first, final = (jnp.concatenate([zero, r], axis=1) for r in (first, final))
            tail = jnp.where(row == d, first, tail)
            tail = jnp.where(row == 4 + d, final, tail)
        out[4 * rows :, :128] = jnp.zeros((TAIL, 128), BF)
        out[4 * rows :, 128:] = tail.astype(BF)

    return pl.pallas_call(
        kernel,
        out_shape=jax.ShapeDtypeStruct((4 * rows + TAIL, 256), BF),
        in_specs=[VMEM] * 4 + [ANY],
        out_specs=VMEM,
        compiler_params=params(8),
        name="stack_rows",
    )(*parts, behind)


def spread(parts):
    rows = parts[0].shape[0] * 4 // 5
    quarter = rows // 4

    def kernel(*refs):
        zero = jnp.zeros((quarter, DH), F32)
        for d in range(4):
            packed = refs[d][rows:, :].astype(F32)
            for n in range(4):
                refs[4 + d][n * quarter : (n + 1) * quarter, :] = jnp.concatenate(
                    [zero, packed[:, n * DH : (n + 1) * DH]], axis=1
                ).astype(BF)

    return pl.pallas_call(
        kernel,
        out_shape=[jax.ShapeDtypeStruct((rows, 128), BF)] * 4,
        in_specs=[VMEM] * 4,
        out_specs=[VMEM] * 4,
        compiler_params=params(8),
        name="spread",
    )(*parts)


def attend(scalars, near, q, pairs, state, behind=()):
    rows = q[0].shape[0]
    width = 4 * rows
    first = state is None
    last = len(pairs) == 4
    strip = 32

    def kernel(s_ref, *refs):
        spot = Spot(s_ref)
        score_ref, prob_ref, peak_ref = refs[-3:]
        q_refs, refs = refs[:4], refs[4:]
        pair_refs, refs = refs[: len(pairs)], refs[len(pairs) :]
        if not first:
            old, old_peak, refs = refs[0], refs[1], refs[2:]
        refs = refs[len(behind) :]
        lane = lax.broadcasted_iota(jnp.int32, (width, 256), 1)
        place = lax.broadcasted_iota(jnp.int32, (1, rows), 1)

        def masks(n):
            far_by = (0, 1, 3, 2)[n]
            return jnp.concatenate(
                [place + spot.base(far_by, i) * rows < s_ref[4] for i in range(4)], axis=1
            )

        def values_of(ref):
            return jnp.where(lane == DV, jnp.ones((), BF), ref[:width, :])

        def raw_scores(query, ref):
            return lax.dot_general(
                query, ref[:width, 128:], (((1,), (1,)), ((), ())), preferred_element_type=F32
            )

        def shares(sums):
            return sums / sums[:, DV : DV + 1]

        if last:
            tails = [r[width:, 128:].astype(F32) for r in pair_refs]
            own, low, high = tails[0], tails[1], tails[2]
            row = lax.broadcasted_iota(jnp.int32, (TAIL, 128), 0)
            edge = jnp.zeros((TAIL, 128), F32)
            for d in range(4):
                n, m = (d + 1) % 4, (d + 3) % 4
                at = spot.ring_place(d)
                other = jnp.where(spot.core == 0, own[4 + n : 5 + n], low[4 + d : 5 + d])
                prev = jnp.where(at == 0, low[4 + n : 5 + n], other)
                other = jnp.where(spot.core == 0, own[m : m + 1], high[d : d + 1])
                nxt = jnp.where(at == 3, high[m : m + 1], other)
                edge = jnp.where(row == d, prev, edge)
                edge = jnp.where(row == 4 + d, nxt, edge)
            edge = edge.astype(BF)
            parts = [jnp.where(masks(n), raw_scores(edge, r), -1e30) for n, r in enumerate(pair_refs)]
            peak = jnp.max(parts[0], axis=1, keepdims=True)
            for s in parts[1:]:
                peak = jnp.maximum(peak, jnp.max(s, axis=1, keepdims=True))
            edge_sums = jnp.zeros((TAIL, 256), F32)
            for s, r in zip(parts, pair_refs):
                edge_sums += jnp.dot(jnp.exp(s - peak).astype(BF), values_of(r), preferred_element_type=F32)
            edge_out = shares(edge_sums)

        pair_ref = pair_refs[-1]
        keep = masks(near)
        values = values_of(pair_ref)
        for i in range(4):
            score_ref[i] = raw_scores(q_refs[i][...], pair_ref)
        for i in range(4):
            for k in range(0, rows, strip):
                cut = slice(k, k + strip)
                scores = jnp.where(keep, score_ref[i, cut, :], -1e30)
                peak = jnp.broadcast_to(jnp.max(scores, axis=1, keepdims=True), (strip, 128))
                if not first:
                    peak = jnp.maximum(peak, old_peak[i * rows + k : i * rows + k + strip, :])
                across = jnp.concatenate([peak] * (width // 128), axis=1)
                prob_ref[i, cut, :] = jnp.exp(scores - across).astype(BF)
                peak_ref[i, cut, :] = peak
            update = jnp.dot(prob_ref[i], values, preferred_element_type=F32)
            if not first:
                shrink = jnp.exp(old_peak[i * rows : (i + 1) * rows, :] - peak_ref[i])
                update = update + old[i * rows : (i + 1) * rows, :] * jnp.concatenate([shrink] * 2, axis=1)
            if last:
                share = shares(update)
                high = share[:, 128:DV]
                refs[i][:rows, :] = share[:, :128].astype(BF)
                refs[i][rows : rows + rows // 2, :] = jnp.concatenate(
                    [high[: rows // 2], high[rows // 2 :]], axis=1
                ).astype(BF)
                ends = jnp.zeros((TAIL, 128), F32)
                for n in range(4):
                    at = i + 4 * (n % 2)
                    part = edge_out[at : at + 1, :128] if n < 2 else edge_out[at : at + 1, 128:]
                    ends = jnp.where(row == n, part, ends)
                refs[i][rows + rows // 2 :, :] = ends.astype(BF)
            else:
                refs[0][i * rows : (i + 1) * rows, :] = update
                refs[1][i * rows : (i + 1) * rows, :] = peak_ref[i]

    ins = [*q, *pairs]
    if not first:
        ins += [*state]
    if last:
        outs = [jax.ShapeDtypeStruct((rows + rows // 2 + TAIL, 128), BF)] * 4
    else:
        outs = [jax.ShapeDtypeStruct((4 * rows, n), F32) for n in (256, 128)]
    return pl.pallas_call(
        kernel,
        out_shape=outs,
        in_specs=[SMEM] + [VMEM] * len(ins) + [ANY] * len(behind),
        out_specs=[VMEM] * len(outs),
        scratch_shapes=[
            pltpu.VMEM((4, rows, width), F32),
            pltpu.VMEM((4, rows, width), BF),
            pltpu.VMEM((4, rows, 128), F32),
        ],
        compiler_params=params(24),
        cost_estimate=pl.CostEstimate(
            flops=4 * 2 * rows * width * 512, bytes_accessed=4 << 20, transcendentals=4 * rows * width
        ),
        name="attend",
    )(scalars, *ins, *behind)


def edges(mark, trunk, skip, cotangent):
    columns = trunk.shape[1]

    def kernel(mark_ref, t_ref, s_ref, c_ref, down, up, buffer, sems):
        copies = []
        for n, ref in enumerate((t_ref, s_ref, c_ref)):
            for end in range(2):
                start = end * (ref.shape[0] - TAIL)
                copies.append(
                    pltpu.make_async_copy(
                        ref.at[pl.ds(start, TAIL), :], buffer.at[2 * n + end], sems.at[2 * n + end]
                    )
                )
        for copy in copies:
            copy.start()
        for copy in copies:
            copy.wait()
        t_first, t_last, s_first, s_last, c_first, c_last = (buffer[n].astype(F32) for n in range(6))
        row = lax.broadcasted_iota(jnp.int32, (TAIL, columns), 0)

        def four(a, b, c, d):
            rest = jnp.where(row == 2, c, jnp.where(row == 3, d, 0.0))
            return jnp.where(row == 0, a, jnp.where(row == 1, b, rest)).astype(BF)

        up[...] = four(t_first[:1], s_first[:1], s_first[1:2], c_first[:1])
        e = TAIL - 1
        down[...] = four(t_last[e:], s_last[e - 1 : e], s_last[e:], c_last[e:])

    return pl.pallas_call(
        kernel,
        out_shape=[jax.ShapeDtypeStruct((TAIL, columns), BF)] * 2,
        in_specs=[ANY] * 4,
        out_specs=[VMEM] * 2,
        scratch_shapes=[pltpu.VMEM((6, TAIL, columns), BF), pltpu.SemaphoreType.DMA((6,))],
        compiler_params=params(53),
        name="edges",
    )(mark, trunk, skip, cotangent)


def gelu_parts(pre):
    slope = math.sqrt(2.0 / math.pi)
    square = pre * pre
    bend = jnp.tanh(slope * (pre + 0.044715 * (square * pre)))
    return bend, square, slope


WIDE = 384
STRIP = 32


def forward(scalars, ours, back, tokens, skipped, out_heads, before, after, depth_weight, turned):
    rows, columns = tokens.shape
    fine = 2 * rows
    half = columns // 2
    steps = half // WIDE
    quarter = columns // 4

    def side(s_ref):
        return s_ref[1] if ours else 1 - s_ref[1]

    def kernel(s_ref, b0, b1, b2, b3, low_ref, high_ref, dw_ref, tok_ref, skip_ref, ow_ref, g_ref, *refs):
        if ours:
            up_ref, act_ref = refs[:2]
            refs = refs[2:]
        else:
            up_ref, prod_ref, act_ref = refs[:3]
            refs = refs[3:]
        att, held = refs
        j = pl.program_id(0)

        @pl.when(j == 0)
        def _():
            mixed = []
            for b in (b0, b1, b2, b3):
                pair = b[rows : rows + rows // 2, :].astype(F32)
                last = b[rows + rows // 2 :, :].astype(F32)
                high = jnp.concatenate(
                    [pair[:, :64], pair[:, 64:], last[2:4, :64], jnp.zeros((TAIL - 2, 64), F32)], axis=0
                )
                left = jnp.concatenate([b[:rows, :].astype(F32), last], axis=0)
                mixed.append(jnp.concatenate([left, high], axis=1))
            squares = sum(jnp.sum(m * m, axis=1, keepdims=True) for m in mixed)
            scale = lax.rsqrt(squares * (1.0 / (H * DV)) + 1e-05)
            for d in range(4):
                att[d] = (mixed[d] * scale).astype(BF)

        @pl.when(j < steps)
        def _():
            spot = Spot(s_ref)
            n = jnp.minimum(j, steps - 1)
            take = pl.ds(pl.multiple_of((side(s_ref) * steps + n) * WIDE, 128), WIDE)
            low, high = low_ref[...].astype(F32), high_ref[...].astype(F32)
            grown = jnp.zeros((rows + TAIL, WIDE), F32)
            for d in range(4):
                grown += jnp.dot(att[d], ow_ref[(spot.head_at + d) % 4, :, take], preferred_element_type=F32)
            hidden = (tok_ref[:, take].astype(F32) + grown[:rows]).astype(BF)
            low_hid = (low[:1] + grown[rows : rows + 1]).astype(BF).astype(F32)
            high_hid = (high[:1] + grown[rows + 1 : rows + 2]).astype(BF).astype(F32)
            twice = lax.broadcasted_iota(jnp.int32, (fine, rows), 0) // 2
            twice = jnp.where(twice == lax.broadcasted_iota(jnp.int32, (fine, rows), 1), 1.0, 0.0).astype(BF)
            doubled = jnp.dot(twice, hidden, preferred_element_type=F32)
            row = lax.broadcasted_iota(jnp.int32, (TAIL, WIDE), 0)
            edge = (low_hid + jnp.where(row == 14, low[1:2], low[2:3])).astype(BF).astype(F32)
            edge = jnp.where((row >= 14) & (spot.place > 0), edge, 0.0)
            held[:TAIL, :] = edge
            up_ref[:TAIL, :] = edge.astype(BF)
            edge = (high_hid + jnp.where(row == 0, high[1:2], high[2:3])).astype(BF).astype(F32)
            edge = jnp.where((row < 2) & (spot.place < 15), edge, 0.0)
            held[TAIL + fine :, :] = edge
            up_ref[TAIL + fine :, :] = edge.astype(BF)
            for k in range(0, fine, STRIP):
                up = (doubled[k : k + STRIP] + skip_ref[k : k + STRIP, take].astype(F32)).astype(BF)
                up_ref[TAIL + k : TAIL + k + STRIP, :] = up
                held[TAIL + k : TAIL + k + STRIP, :] = up.astype(F32)
            w = [dw_ref[t : t + 1, :] for t in range(3)]
            cut = pl.ds(0 if ours else pl.multiple_of(n * WIDE, 128), WIDE)
            for k in range(0, fine, STRIP):
                near = held[8 + k : 24 + k + STRIP, :]
                pre = w[0] * near[7 : 7 + STRIP] + w[1] * near[8 : 8 + STRIP] + w[2] * near[9 : 9 + STRIP]
                bend, _, _ = gelu_parts(pre)
                act_ref[k : k + STRIP, cut] = (pre * (0.5 + 0.5 * bend)).astype(BF)

        if not ours:

            @pl.when(j >= steps)
            def _():
                for n in range(2):
                    at = pl.multiple_of((Spot(s_ref).their_first + 2 * (j - steps) + n) % 4 * quarter, 16)
                    prod_ref[n] = jnp.dot(
                        g_ref[pl.ds(at, quarter), :], act_ref[...], preferred_element_type=F32
                    ).astype(BF)

    def cols(count, full):
        def place(j, s_ref):
            n = jnp.minimum(j, steps - 1)
            return 0, (side(s_ref) * steps + n if full else n)

        return pl.BlockSpec((count, WIDE), place)

    def flat(count, width):
        return pl.BlockSpec((count, width), lambda j, s_ref: (0, 0))

    outs = [jax.ShapeDtypeStruct((fine + 2 * TAIL, half), BF)]
    out_specs = [cols(fine + 2 * TAIL, False)]
    scratch = []
    if ours:
        outs += [jax.ShapeDtypeStruct((fine, half), BF)]
        out_specs += [cols(fine, False)]
    else:
        outs += [jax.ShapeDtypeStruct((4, quarter, half), BF)]
        out_specs += [
            pl.BlockSpec((2, quarter, half), lambda j, s_ref: (jnp.maximum(j - steps, 0), 0, 0))
        ]
        scratch += [pltpu.VMEM((fine, half), BF)]
    scratch += [
        pltpu.VMEM((4, rows + TAIL, DV), BF),
        pltpu.VMEM((fine + 2 * TAIL, WIDE), F32),
    ]
    return pl.pallas_call(
        kernel,
        out_shape=outs,
        grid_spec=pltpu.PrefetchScalarGridSpec(
            num_scalar_prefetch=1,
            grid=(steps if ours else steps + 2,),
            in_specs=[flat(rows + rows // 2 + TAIL, 128)] * 4
            + [cols(TAIL, True), cols(TAIL, True), cols(3, True)]
            + [VMEM] * 4,
            out_specs=out_specs,
            scratch_shapes=scratch,
        ),
        compiler_params=params(24),
        cost_estimate=pl.CostEstimate(
            flops=2 * fine * columns * columns, bytes_accessed=9 << 20, transcendentals=fine * half
        ),
        name="forward",
    )(scalars, *back, before, after, depth_weight, tokens, skipped, out_heads, turned)


def load(behind, *arrays):
    count = len(arrays)

    def kernel(behind_ref, *refs):
        sems = refs[-1]
        copies = [pltpu.make_async_copy(refs[n], refs[count + n], sems.at[n]) for n in range(count)]
        for copy in copies:
            copy.start()
        for copy in copies:
            copy.wait()

    return pl.pallas_call(
        kernel,
        out_shape=[jax.ShapeDtypeStruct(a.shape, a.dtype) for a in arrays],
        in_specs=[ANY] * (1 + count),
        out_specs=[VMEM] * count,
        scratch_shapes=[pltpu.SemaphoreType.DMA((count,))],
        compiler_params=params(45),
        name="load",
    )(behind, *arrays)


def backward(scalars, theirs, ours, upstream, before, after, point_weight, depth_weight, behind):
    fine, columns = upstream.shape
    half = columns // 2
    steps = half // WIDE

    def kernel(s_ref, theirs_ref, ours_ref, g_ref, low_ref, high_ref, pw_ref, dw_ref, behind_ref, *refs):
        grad_ref, gd_theirs, gd_ours, upper, ends, up_ref = refs
        j = pl.program_id(0)

        @pl.when(j < steps)
        def _():
            up_ref[...] = theirs_ref[...]

        @pl.when(j >= steps)
        def _():
            up_ref[...] = ours_ref[...]

        dims = (((1,), (1,)), ((), ()))

        @pl.when(pl.program_id(0) == 0)
        def _():
            row = lax.broadcasted_iota(jnp.int32, (TAIL, columns), 0)
            low, high = low_ref[...].astype(F32), high_ref[...].astype(F32)
            ends[...] = jnp.where(row == 7, low[3:4], jnp.where(row == 8, high[3:4], 0.0)).astype(BF)

        upper[...] = lax.dot_general(g_ref[...], pw_ref[...], dims, preferred_element_type=F32)
        outer = lax.dot_general(ends[...], pw_ref[...], dims, preferred_element_type=F32)
        w = [dw_ref[t : t + 1, :] for t in range(3)]

        def grad_of(near, start, count, coming):
            taps = [near[start - 1 + t : start - 1 + t + count] for t in range(3)]
            pre = w[0] * taps[0] + w[1] * taps[1] + w[2] * taps[2]
            bend, square, slope = gelu_parts(pre)
            rate = 0.5 + 0.5 * bend + (pre * (1.0 - bend * bend)) * (
                0.5 * slope + (1.5 * slope * 0.044715) * square
            )
            return taps, (coming * rate).astype(BF).astype(F32)

        blank = jnp.zeros((8, WIDE), F32)
        _, edge = grad_of(up_ref[:32, :].astype(F32), 8, 8, outer[:8])
        grad_ref[:TAIL, :] = jnp.concatenate([blank, edge], axis=0).astype(BF)
        _, edge = grad_of(up_ref[fine:, :].astype(F32), 16, 8, outer[8:])
        grad_ref[TAIL + fine :, :] = jnp.concatenate([edge, blank], axis=0).astype(BF)
        sums = [jnp.zeros((8, WIDE), F32)] * 3
        for k in range(0, fine, STRIP):
            near = up_ref[k : k + STRIP + 2 * TAIL, :].astype(F32)
            taps, mid = grad_of(near, TAIL, STRIP, upper[k : k + STRIP, :])
            grad_ref[TAIL + k : TAIL + k + STRIP, :] = mid.astype(BF)
            for t in range(3):
                term = taps[t] * mid
                for r in range(0, STRIP, 8):
                    sums[t] = sums[t] + term[r : r + 8]
        depth = [jnp.sum(total, axis=0, keepdims=True) for total in sums]
        for ref, mine in ((gd_theirs, j < steps), (gd_ours, j >= steps)):

            @pl.when(mine)
            def _():
                for t in range(3):
                    ref[t : t + 1, :] = depth[t]

    def block(j, s_ref):
        return jnp.where(j < steps, (1 - s_ref[1]) * steps + j, s_ref[1] * steps + j - steps)

    def cols(count):
        return pl.BlockSpec((count, WIDE), lambda j, s_ref: (0, block(j, s_ref)))

    def early(count):
        return pl.BlockSpec((count, WIDE), lambda j, s_ref: (0, jnp.minimum(j, steps - 1)))

    def late(count):
        return pl.BlockSpec((count, WIDE), lambda j, s_ref: (0, jnp.maximum(j - steps, 0)))

    def flat(count):
        return pl.BlockSpec((count, columns), lambda j, s_ref: (0, 0))

    return pl.pallas_call(
        kernel,
        out_shape=[
            jax.ShapeDtypeStruct((fine + 2 * TAIL, columns), BF),
            jax.ShapeDtypeStruct((3, half), F32),
            jax.ShapeDtypeStruct((3, half), F32),
        ],
        grid_spec=pltpu.PrefetchScalarGridSpec(
            num_scalar_prefetch=1,
            grid=(2 * steps,),
            in_specs=[
                early(fine + 2 * TAIL),
                late(fine + 2 * TAIL),
                flat(fine),
                flat(TAIL),
                flat(TAIL),
                pl.BlockSpec((WIDE, columns), lambda j, s_ref: (block(j, s_ref), 0)),
                cols(3),
                ANY,
            ],
            out_specs=[cols(fine + 2 * TAIL), early(3), late(3)],
            scratch_shapes=[
                pltpu.VMEM((fine, WIDE), F32),
                pltpu.VMEM((TAIL, columns), BF),
                pltpu.VMEM((fine + 2 * TAIL, WIDE), BF),
            ],
        ),
        compiler_params=params(48),
        cost_estimate=pl.CostEstimate(
            flops=2 * fine * columns * columns, bytes_accessed=11 << 20, transcendentals=fine * columns
        ),
        name="backward",
    )(scalars, theirs, ours, upstream, before, after, point_weight, depth_weight, behind)


def spread_back(grad_pre, depth_weight):
    fine, columns = grad_pre.shape[0] - 2 * TAIL, grad_pre.shape[1]

    def kernel(grad_ref, dw_ref, gs_ref, mark_ref):
        mark_ref[...] = jnp.zeros((8, 128), F32)
        w = [dw_ref[t : t + 1, :] for t in range(3)]
        for k in range(0, fine, STRIP):
            near = grad_ref[k : k + STRIP + 2 * TAIL, :].astype(F32)
            gs_ref[k : k + STRIP, :] = (
                w[0] * near[TAIL + 1 : TAIL + 1 + STRIP]
                + w[1] * near[TAIL : TAIL + STRIP]
                + w[2] * near[TAIL - 1 : TAIL - 1 + STRIP]
            ).astype(BF)

    def cols(count):
        return pl.BlockSpec((count, WIDE), lambda j: (0, j))

    return pl.pallas_call(
        kernel,
        grid=(columns // WIDE,),
        out_shape=[jax.ShapeDtypeStruct((fine, columns), BF), jax.ShapeDtypeStruct((8, 128), F32)],
        in_specs=[cols(fine + 2 * TAIL), cols(3)],
        out_specs=[cols(fine), pl.BlockSpec((8, 128), lambda j: (0, 0))],
        compiler_params=params(16),
        name="spread_back",
    )(grad_pre, depth_weight)


def product(scalars, act, turned, steps, arrived):
    half, quarter = act.shape[1], turned.shape[0] // 4

    def kernel(s_ref, a_ref, g_ref, arrived_ref, *outs):
        for out, d in zip(outs, steps):
            at = pl.multiple_of((Spot(s_ref).first_at + d) % 4 * quarter, 16)
            block = jnp.dot(g_ref[pl.ds(at, quarter), :], a_ref[...], preferred_element_type=F32)
            out[...] = (block + arrived_ref[d].astype(F32)).astype(BF)

    return pl.pallas_call(
        kernel,
        out_shape=[jax.ShapeDtypeStruct((quarter, half), BF)] * len(steps),
        in_specs=[SMEM] + [VMEM] * 3,
        out_specs=[VMEM] * len(steps),
        compiler_params=params(14),
        cost_estimate=pl.CostEstimate(
            flops=2 * act.shape[0] * half * quarter * len(steps), bytes_accessed=6 << 20, transcendentals=0
        ),
        name="product",
    )(scalars, act, turned, arrived)


def split_rows(at, got):
    rows, columns = got[0].shape
    slim = rows // 4

    def kernel(at_ref, *refs):
        ins, outs = refs[:4], refs[4:]
        for d in range(4):
            take = pl.ds(pl.multiple_of((Spot(at_ref).second_at + d) % 4 * slim, 16), slim)
            outs[d][...] = total_of([r[take, :] for r in ins]).astype(BF)

    return pl.pallas_call(
        kernel,
        out_shape=[jax.ShapeDtypeStruct((slim, columns), BF)] * 4,
        in_specs=[SMEM] + [VMEM] * 4,
        out_specs=[VMEM] * 4,
        compiler_params=params(10),
        name="split_rows",
    )(at, *got)


def join_rows(at, got, behind):
    slim, columns = got[0].shape[0] - TAIL, got[0].shape[1]
    quarter = 4 * slim

    def kernel(at_ref, *refs):
        ins, out, held = refs[:4], refs[5], refs[6]
        for d in range(4):
            put = pl.ds(pl.multiple_of((Spot(at_ref).second_at + 4 - d) % 4 * slim, 16), slim)
            held[put, :] = ins[d][:slim, :]
        out[:columns, :] = held[...].T
        last = total_of([r[slim:, :] for r in ins])[:8]
        out[columns:, :] = jnp.concatenate([last[:, :quarter], last[:, quarter:]], axis=0).astype(BF)

    return pl.pallas_call(
        kernel,
        out_shape=jax.ShapeDtypeStruct((columns + TAIL, quarter), BF),
        in_specs=[SMEM] + [VMEM] * 4 + [ANY],
        out_specs=VMEM,
        scratch_shapes=[pltpu.VMEM((quarter, columns), BF)],
        compiler_params=params(10),
        name="join_rows",
    )(at, *got, behind)


def lay_out(scalars, own, other):
    half, quarter = own[0].shape[0] - TAIL, own[0].shape[1]
    parts = 2
    part = half // parts

    def kernel(s_ref, *refs):
        out, depth, sems = refs[-3:]
        spot = Spot(s_ref)
        copies = []
        for n in range(8):
            mine = n < 4
            down = (spot.core if mine else 1 - spot.core) * half
            over = ((spot.first_at if mine else spot.their_first) + 4 - n % 4) % 4 * quarter
            for k in range(parts):
                start = pl.multiple_of(down + k * part, 16)
                copies.append(
                    pltpu.make_async_copy(
                        refs[n].at[pl.ds(k * part, part), :],
                        out.at[pl.ds(start, part), pl.ds(pl.multiple_of(over, 128), quarter)],
                        sems.at[parts * n + k],
                    )
                )
        for copy in copies:
            copy.start()
        for n, side in ((0, spot.core), (4, 1 - spot.core)):
            rows = total_of([refs[n + d][half:, :] for d in range(4)])
            rows = jnp.concatenate([rows[:3], rows[8:11]], axis=1)
            depth[:, pl.ds(pl.multiple_of(side * half, 128), half)] = rows
        for copy in copies:
            copy.wait()

    return pl.pallas_call(
        kernel,
        out_shape=[
            jax.ShapeDtypeStruct((2 * half, 4 * quarter), BF),
            jax.ShapeDtypeStruct((3, 2 * half), F32),
        ],
        in_specs=[SMEM] + [VMEM] * 8,
        out_specs=[ANY, VMEM],
        scratch_shapes=[pltpu.SemaphoreType.DMA((8 * parts,))],
        compiler_params=params(12),
        name="lay_out",
    )(scalars, *own, *other)


def local(
    trunk,
    skip,
    valid_bins,
    query_weight,
    key_weight,
    value_weight,
    out_weight,
    depth_weight,
    point_weight,
    cotangent,
):
    tokens, skipped, upstream = trunk[0], skip[0], cotangent[0]
    rows, columns = tokens.shape
    fine = skipped.shape[0]
    ix, ic, iz, iy = (lax.axis_index(a) for a in AXES)
    spot = jnp.stack([v.astype(jnp.int32) for v in (ix, ic, iz, iy)])
    scalars = jnp.concatenate([spot, valid_bins.astype(jnp.int32)])
    blocks = project(tokens, query_weight, key_weight, value_weight)
    down, up = edges(blocks[0], tokens, skipped, upstream)
    before = lax.ppermute(down, ("z", "y"), [(i, i + 1) for i in range(15)])
    after = lax.ppermute(up, ("z", "y"), [(i + 1, i) for i in range(15)])
    blocks = exchange(blocks, HEAD_RING)
    own = stack_rows(blocks, down)
    q = spread(blocks)
    far = {d: lax.ppermute(own, AXES, turn(ROW_RING, d)) for d in (1, 3, 2)}
    state = attend(scalars, 0, q, [own], None)

    turned = upstream.T

    state = attend(scalars, 1, q, [far[1]], state)
    state = attend(scalars, 2, q, [far[3]], state)
    mixed = attend(scalars, 3, q, [own, far[1], far[3], far[2]], state, (before, after))
    back = exchange(mixed, HEAD_RING, -1)
    tokens_v, skipped_v, out_v = load(mixed[0], tokens, skipped, out_weight.reshape(H, DV, -1))
    swap = [(0, 1), (1, 0)]
    given = (back, tokens_v, skipped_v, out_v, before, after, depth_weight, turned)
    up_theirs, sent = forward(scalars, False, *given)
    arrived = lax.ppermute(sent, "c", swap)
    up_ours, act = forward(scalars, True, *given)
    piece_2, piece_1 = product(scalars, act, turned, (2, 1), arrived)
    piece_3, piece_0 = product(scalars, act, turned, (3, 0), arrived)
    got = exchange([piece_0, piece_1, piece_2, piece_3], SUM_RINGS[0])

    grad_pre, d_theirs, d_mine = backward(
        scalars, up_theirs, up_ours, upstream, before, after, point_weight, depth_weight, piece_0
    )
    d_sum = d_mine + lax.ppermute(d_theirs, "c", swap)
    rider = jnp.pad(d_sum.astype(BF), ((0, TAIL - 3), (0, 0)))

    got = exchange(split_rows(scalars, got), SUM_RINGS[1])
    mixed = jnp.concatenate([total_of(got).astype(BF), rider], axis=0)
    got = exchange([mixed] * 4, SUM_RINGS[2])
    norm_scale = 1.0 / math.sqrt(128 * fine)
    summed = (total_of(got) * norm_scale).astype(BF)
    grad_skip, mark = spread_back(grad_pre, depth_weight)
    joined = join_rows(scalars, exchange([summed] * 4, SUM_RINGS[1]), mark)

    own = exchange([joined] * 4, SUM_RINGS[0])
    other = [lax.ppermute(block, "c", swap) for block in own]
    grad_pointwise, grad_depth = lay_out(scalars, own, other)
    return (grad_pointwise, grad_depth, grad_skip[None])


def solution(mesh):
    fine_mesh = Mesh(mesh.devices.reshape(SIZES), AXES)
    rows = P(("x", "c"), ("z", "y"), None)
    return jax.shard_map(
        local,
        mesh=fine_mesh,
        in_specs=(rows, rows, P(("x", "c")), P(), P(), P(), P(), P(), P(), rows),
        out_specs=(P(), P(), rows),
        check_vma=False,
    )
```
